32 devices in a mesh: dp: 2 (over x), ctx: 4 (over y, core), tp: 4 (over z).
Axes of the slice: x: 2, y: 2, z: 4, core: 2. Of those that a mesh axis runs over, the one named last changes fastest.
Arguments:
- tokens: bfloat16 [4, 2048, 1280], P('dp', ('ctx', 'tp')), may hold values from -6 to 6
- prefix: int32 [4], P('dp'), may hold values from 204 to 1024
- w_query: bfloat16 [2, 1280, 1280], P(None, ('dp', 'ctx'), 'tp'), may hold values from -0.15625 to 0.15625
- key_weight: bfloat16 [2, 1280, 320], P(None, ('dp', 'ctx')), may hold values from -0.15625 to 0.15625
- value_weight: bfloat16 [2, 1280, 320], P(None, ('dp', 'ctx')), may hold values from -0.15625 to 0.15625
- w_out: bfloat16 [2, 1280, 1280], P(None, ('dp', 'ctx'), 'tp'), may hold values from -3 to 3
- w_gate: bfloat16 [2, 1280, 3584], P(None, ('dp', 'ctx'), 'tp'), may hold values from -0.15625 to 0.15625
- w_up: bfloat16 [2, 1280, 3584], P(None, ('dp', 'ctx'), 'tp'), may hold values from -0.15625 to 0.15625
- w_down: bfloat16 [2, 1280, 3584], P(None, ('dp', 'ctx'), 'tp'), may hold values from -0.09375 to 0.09375
- gain_attn: bfloat16 [2, 1280], P(None, ('dp', 'ctx')), may hold values from 0.099609375 to 1.8984375
- gain_ffn: bfloat16 [2, 1280], P(None, ('dp', 'ctx')), may hold values from 0.099609375 to 1.8984375
- cotangent: bfloat16 [4, 2048, 1280], P('dp', ('ctx', 'tp')), may hold values from -6 to 6
Outputs:
- output: bfloat16 [4, 2048, 1280], P('dp', ('ctx', 'tp'))
- grad_tokens: float32 [4, 2048, 1280], P('dp', ('ctx', 'tp'))
- grad_w_query: float32 [2, 1280, 1280], P(None, ('dp', 'ctx'), 'tp')
- grad_w_key: float32 [2, 1280, 320], P(None, ('dp', 'ctx'))
- grad_w_value: float32 [2, 1280, 320], P(None, ('dp', 'ctx'))
- grad_w_out: float32 [2, 1280, 1280], P(None, ('dp', 'ctx'), 'tp')
- grad_w_gate: float32 [2, 1280, 3584], P(None, ('dp', 'ctx'), 'tp')
- grad_w_up: float32 [2, 1280, 3584], P(None, ('dp', 'ctx'), 'tp')
- grad_w_down: float32 [2, 1280, 3584], P(None, ('dp', 'ctx'), 'tp')
- grad_gain_attn: float32 [2, 1280], P(None, ('dp', 'ctx'))
- grad_gain_ffn: float32 [2, 1280], P(None, ('dp', 'ctx'))
The draws below stay inside these ranges and needn't reach their ends.
All inputs are finite; a program needn't handle non-finite values.
Results may differ from the reference program's by a relative error of at most 0.035.
Values may be sent and summed in bfloat16 or wider, within the bound.
A program may use at most 384 MiB of HBM per device.

```python
import math
import jax
import jax.numpy as jnp
from jax import lax

MODEL_DIMENSION = 1280
QUERY_HEADS = 20
KEY_VALUE_HEADS = 5
HEAD_SIZE = 64
FF = 3584
LEN = 2048
LAYER_COUNT = 2
SEQS = 4
N_TP = 4


def place_ends(values, key, smallest, top_value):
    shape = values.shape
    place = [jax.random.randint(jax.random.fold_in(key, axis), (), 0, shape[axis]) for axis in range(len(shape))]
    values = values.at[tuple(place)].set(smallest)
    longest = shape.index(max(shape))
    place[longest] = (place[longest] + 1) % shape[longest]
    return values.at[tuple(place)].set(top_value)


def level_of(key, extent, cuts, least, top_value):
    def one(axis_at, parts):
        draws = jax.random.uniform(jax.random.fold_in(jax.random.fold_in(key, 6), axis_at), (parts,), jnp.float32, least / len(cuts), top_value / len(cuts))
        return jnp.repeat(jnp.exp(draws), extent[axis_at] // parts).reshape((-1,) + (1,) * (len(extent) - axis_at - 1))

    level = one(*cuts[0])
    for cut in cuts[1:]:
        level = level * one(*cut)
    return level


def normal_values(stream_key, dims, spread, limit, pieces=(), dtype=jnp.bfloat16):
    factor_of = level_of(stream_key, dims, pieces, -0.22, 0.18) if pieces else 1.0
    values = jax.random.normal(stream_key, dims, jnp.float32) * spread * factor_of
    return jnp.minimum(jnp.maximum(values, -limit), limit).astype(dtype)


def setup_inputs(seed: int = 0) -> dict:
    key_list = jax.random.split(jax.random.key(seed), 13)
    tokens = normal_values(key_list[0], (SEQS, LEN, MODEL_DIMENSION), 1.0, 6.0, ((0, 2), (1, 16)))
    prefix = place_ends(jax.random.randint(key_list[1], (SEQS,), LEN // 10, LEN // 2 + 1), jax.random.fold_in(key_list[1], 1), LEN // 10, (LEN // 2 + 1) - 1).astype(jnp.int32)
    w_query = normal_values(key_list[2], (LAYER_COUNT, MODEL_DIMENSION, QUERY_HEADS * HEAD_SIZE), MODEL_DIMENSION ** -0.5, 0.15625, ((1, 8), (2, 4)))
    key_weight = normal_values(key_list[3], (LAYER_COUNT, MODEL_DIMENSION, KEY_VALUE_HEADS * HEAD_SIZE), MODEL_DIMENSION ** -0.5, 0.15625, ((1, 8),))
    value_weight = normal_values(key_list[4], (LAYER_COUNT, MODEL_DIMENSION, KEY_VALUE_HEADS * HEAD_SIZE), MODEL_DIMENSION ** -0.5, 0.15625, ((1, 8),))
    w_out = normal_values(key_list[5], (LAYER_COUNT, MODEL_DIMENSION, QUERY_HEADS * HEAD_SIZE), 4 ** -0.5, 3.0, ((1, 8), (2, 4)))
    w_gate = normal_values(key_list[6], (LAYER_COUNT, MODEL_DIMENSION, FF), MODEL_DIMENSION ** -0.5, 0.15625, ((1, 8), (2, 4)))
    w_up = normal_values(key_list[7], (LAYER_COUNT, MODEL_DIMENSION, FF), MODEL_DIMENSION ** -0.5, 0.15625, ((1, 8), (2, 4)))
    w_down = normal_values(key_list[8], (LAYER_COUNT, MODEL_DIMENSION, FF), FF ** -0.5, 0.09375, ((1, 8), (2, 4)))
    gain_attn = jnp.clip(1.0 + 0.18 * jax.random.normal(key_list[9], (LAYER_COUNT, MODEL_DIMENSION), jnp.float32), 0.099609375, 1.8984375).astype(jnp.bfloat16)
    gain_ffn = jnp.clip(1.0 + 0.18 * jax.random.normal(key_list[10], (LAYER_COUNT, MODEL_DIMENSION), jnp.float32), 0.099609375, 1.8984375).astype(jnp.bfloat16)
    cotangent = normal_values(key_list[11], (SEQS, LEN, MODEL_DIMENSION), 1.0, 6.0, ((0, 2), (1, 16)))
    return dict(tokens=tokens, prefix=prefix, w_query=w_query, key_weight=key_weight, value_weight=value_weight, w_out=w_out, w_gate=w_gate, w_up=w_up, w_down=w_down, gain_attn=gain_attn, gain_ffn=gain_ffn, cotangent=cotangent)


epsilon = 1e-05
masked_score = -1e+30
highest = lax.Precision.HIGHEST

@jax.custom_vjp
def low(v):
    return lax.optimization_barrier(v.astype(jnp.bfloat16)).astype(jnp.float32)

@jax.custom_vjp
def low_back(v):
    return v

def low_keep(v):
    return (low(v), None)

def low_pass(kept, grad):
    return (grad,)

def back_keep(v):
    return (v, None)

def back_low(kept, grad):
    return (low(grad),)
low.defvjp(low_keep, low_pass)
low_back.defvjp(back_keep, back_low)

def mult(left_side, right_side):
    return jnp.dot(left_side, right_side, precision=highest)

def normalize(values):
    return values * lax.rsqrt(lax.optimization_barrier(jnp.mean(values * values, axis=-1, keepdims=True)) + epsilon)

def rope_tables(positions):
    half_size = HEAD_SIZE // 2
    frequency = jnp.exp(-math.log(10000.0) * jnp.arange(half_size).astype(jnp.float32) / half_size)
    angles = positions.astype(jnp.float32)[:, None] * frequency[None, :]
    return (jnp.cos(angles)[:, None, :], jnp.sin(angles)[:, None, :])

def rotate(values, cosine, sine):
    half_size = values.shape[-1] // 2
    first_half = values[..., :half_size]
    second_half = values[..., half_size:]
    return jnp.concatenate([first_half * cosine - second_half * sine, second_half * cosine + first_half * sine], axis=-1)

def attend(queries, key_heads, value_heads, prefix_len):
    block_size = min(512, LEN)
    key_pos = jnp.arange(LEN).astype(jnp.int32)

    def one_block(block_index):
        query_block = lax.dynamic_slice_in_dim(queries, block_index * block_size, block_size, 0)
        scores = jnp.einsum('qhd,khd->hqk', query_block, key_heads, precision=highest) * (1.0 / math.sqrt(HEAD_SIZE))
        scores = low_back(scores)
        query_pos = block_index * block_size + jnp.arange(block_size).astype(jnp.int32)
        visible = (key_pos[None, :] <= query_pos[:, None]) | (key_pos[None, :] < prefix_len)
        scores = jnp.where(visible[None], scores, masked_score)
        top_score = lax.optimization_barrier(jnp.max(scores, axis=-1, keepdims=True))
        exponent = jnp.exp(scores - top_score)
        weights = exponent / lax.optimization_barrier(jnp.sum(exponent, axis=-1, keepdims=True))
        return jnp.einsum('hqk,khd->qhd', low(weights), value_heads, precision=highest)
    blocks = lax.map(jax.checkpoint(one_block), jnp.arange(LEN // block_size).astype(jnp.int32))
    return blocks.reshape(LEN, queries.shape[1], HEAD_SIZE)

def layer_forward(stream, layer_weights, prefix_len, cosine, sine):
    w_query, key_weight, value_weight, w_out, w_gate, w_up, w_down, gain_attn, gain_ffn = layer_weights
    heads_here = QUERY_HEADS // N_TP
    group_width = QUERY_HEADS // KEY_VALUE_HEADS
    normed = low(normalize(stream) * gain_attn)
    queries = low(rotate(low_back(mult(normed, w_query)).reshape(LEN, QUERY_HEADS, HEAD_SIZE), cosine, sine))
    outputs = []
    for tp_rank in range(N_TP):
        low_head = tp_rank * heads_here // group_width
        key_rows = low(rotate(low_back(mult(normed, key_weight[:, low_head * HEAD_SIZE:(low_head + 2) * HEAD_SIZE])).reshape(LEN, 2, HEAD_SIZE), cosine, sine))
        value_rows = low(low_back(mult(normed, value_weight[:, low_head * HEAD_SIZE:(low_head + 2) * HEAD_SIZE])).reshape(LEN, 2, HEAD_SIZE))
        pick_index = [(tp_rank * heads_here + head_index) // group_width - low_head for head_index in range(heads_here)]
        outputs.append(attend(queries[:, tp_rank * heads_here:(tp_rank + 1) * heads_here], key_rows[:, pick_index], value_rows[:, pick_index], prefix_len))
    attended = low(low_back(jnp.concatenate(outputs, axis=1).reshape(LEN, QUERY_HEADS * HEAD_SIZE)))
    middle = stream + low_back(mult(attended, w_out.T))
    normed_ffn = low(normalize(middle) * gain_ffn)
    gate_lin = low_back(mult(normed_ffn, w_gate))
    up_lin = low_back(mult(normed_ffn, w_up))
    hidden = low(gate_lin / (1.0 + jnp.exp(-gate_lin)) * up_lin)
    return middle + low_back(mult(hidden, w_down.T))

def reference(tokens, prefix, w_query, key_weight, value_weight, w_out, w_gate, w_up, w_down, gain_attn, gain_ffn, cotangent):
    weights = tuple((member.astype(jnp.float32) for member in (w_query, key_weight, value_weight, w_out, w_gate, w_up, w_down, gain_attn, gain_ffn)))
    cosine, sine = rope_tables(jnp.arange(LEN).astype(jnp.int32))

    def forward(stream, weight_sets, prefix_len):
        for layer_index in range(LAYER_COUNT):
            stream = layer_forward(stream, tuple((weight_set[layer_index] for weight_set in weight_sets)), prefix_len, cosine, sine)
        return stream

    def one_sequence(carried, member):
        sequence, cotan_rows, prefix_len = member
        result, pullback = jax.vjp(lambda start_rows, weight_sets: forward(start_rows, weight_sets, prefix_len), sequence.astype(jnp.float32), weights)
        grad_rows, grad_sets = pullback(cotan_rows.astype(jnp.float32))
        carried = tuple((so_far + fresh_grad for so_far, fresh_grad in zip(carried, grad_sets)))
        return (carried, (result.astype(jnp.bfloat16), grad_rows))
    zero_grads = tuple((jnp.zeros_like(weight_set) for weight_set in weights))
    totals, (outputs, grad_tokens) = lax.scan(one_sequence, zero_grads, (tokens, cotangent, prefix))
    return (outputs, grad_tokens, totals[0], totals[1], totals[2], totals[3], totals[4], totals[5], totals[6], totals[7], totals[8])
```

```python
import functools
import math

import jax
import jax.numpy as jnp
from jax import lax
from jax.experimental import pallas as pl
from jax.experimental.pallas import tpu as pltpu
from jax.sharding import PartitionSpec as P

QUERY_HEADS = 20
KEY_VALUE_HEADS = 5
D = 64
GROUP = QUERY_HEADS // KEY_VALUE_HEADS
EPS = 1e-05
MASKED = -1e30
BF = jnp.bfloat16
F32 = jnp.float32
SLOTS = 4
LANES = 128


def nt(a, b):
    return lax.dot_general(a, b, (((1,), (1,)), ((), ())), preferred_element_type=F32)


def nn(a, b):
    return lax.dot_general(a, b, (((1,), (0,)), ((), ())), preferred_element_type=F32)


def tn(a, b):
    return lax.dot_general(a, b, (((0,), (0,)), ((), ())), preferred_element_type=F32)


def half_turn(x):
    lane = lax.broadcasted_iota(jnp.int32, x.shape, 1)
    return jnp.where((lane & 32) == 0, pltpu.roll(x, LANES - 32, 1), pltpu.roll(x, 32, 1))


def call(kernel, ins, outs, smem=0, scratch=(), flops=0, exps=0, vmem=56):
    total = sum(math.prod(a.shape) * a.dtype.itemsize for a in ins) + sum(
        math.prod(s) * jnp.dtype(d).itemsize for s, d in outs
    )
    return pl.pallas_call(
        kernel,
        out_shape=[jax.ShapeDtypeStruct(s, d) for s, d in outs],
        in_specs=[pl.BlockSpec(memory_space=pltpu.SMEM)] * smem
        + [pl.BlockSpec(memory_space=pltpu.VMEM)] * (len(ins) - smem),
        out_specs=[pl.BlockSpec(memory_space=pltpu.VMEM)] * len(outs),
        scratch_shapes=list(scratch),
        compiler_params=pltpu.CompilerParams(vmem_limit_bytes=vmem * 2**20),
        cost_estimate=pl.CostEstimate(
            flops=int(flops), bytes_accessed=int(total), transcendentals=int(exps)
        ),
    )(*ins)


def flip(x, axis, m):
    return lax.ppermute(x, axis, [(i, i ^ m) for i in range(4)])


def ctx_gather(x):
    far = flip(x, "ctx", 2)
    return [x, flip(x, "ctx", 1), far, flip(far, "ctx", 1)]


def ctx_reduce(parts):
    far = (parts[2].astype(F32) + flip(parts[3], "ctx", 1).astype(F32)).astype(BF)
    near = flip(parts[1], "ctx", 1)
    return parts[0].astype(F32) + near.astype(F32) + flip(far, "ctx", 2).astype(F32)


def inner(t):
    return (t == 1) | (t == 2)


def tp_gather(x):
    t = lax.axis_index("tp")
    two = flip(x, "tp", 2)
    mid = lax.ppermute(x, "tp", [(1, 2), (2, 1)])
    end = lax.ppermute(two, "tp", [(1, 0), (2, 3)])
    return [x, flip(x, "tp", 1), two, jnp.where(inner(t), mid, end)]


def tp_reduce(parts):
    one = flip(parts[1], "tp", 1)
    handed = lax.ppermute(parts[3], "tp", [(0, 1), (3, 2)])
    mid = lax.ppermute(parts[3], "tp", [(1, 2), (2, 1)])
    two = flip((parts[2].astype(F32) + handed.astype(F32)).astype(BF), "tp", 2)
    return (
        parts[0].astype(F32) + one.astype(F32) + two.astype(F32) + mid.astype(F32)
    )


def ctx_exchange(stacked, own_first):
    c = lax.axis_index("ctx")
    got = []
    for m in range(4):
        piece = lax.dynamic_index_in_dim(stacked, c ^ m, 0, keepdims=False)
        got.append(piece if m == 0 else flip(piece, "ctx", m))
    return by_ctx(jnp.stack(got))


def by_ctx(stacked):
    c = lax.axis_index("ctx")
    return jnp.stack(
        [lax.dynamic_index_in_dim(stacked, c ^ i, 0, keepdims=False) for i in range(4)]
    )


def head_side(c, heads, h):
    return (c * heads + h) // GROUP - (c * heads) // GROUP


def qkv_kernel(heads, s_ref, x0, x1, x2, x3, w_ref, cos_ref, sin_ref, rows_o, q_o, kv_o):
    del s_ref
    block = x0.shape[0]
    for m, x in enumerate((x0, x1, x2, x3)):
        rows_o[m] = x[...]
    rows = rows_o[...].reshape(4 * block, x0.shape[1])
    cos, sin = cos_ref[...], sin_ref[...]
    at = 0
    total = (heads + 2) * LANES
    while at < total:
        width = min(3 * LANES, total - at)
        lin = nt(rows, w_ref[at : at + width])
        for j in range(width // LANES):
            slot = at // LANES + j
            v = lin[:, j * LANES : (j + 1) * LANES]
            if slot <= heads:
                v = v * cos + half_turn(v) * sin
            if slot < heads:
                v = (v * 0.125).astype(BF)
                for m in range(4):
                    q_o[m, slot] = v[m * block : (m + 1) * block]
            else:
                v = v.astype(BF)
                lo = (slot - heads) * LANES
                for m in range(4):
                    kv_o[m, :, lo : lo + LANES] = v[m * block : (m + 1) * block]
        at += width


def side_mask(c, heads, block):
    head = lax.broadcasted_iota(jnp.int32, (heads * block, LANES), 0) // block
    lane = lax.broadcasted_iota(jnp.int32, (heads * block, LANES), 1)
    return (lane // D) == ((c * heads + head) // GROUP - (c * heads) // GROUP)


def key_positions(t, block, first, count):
    row = lax.broadcasted_iota(jnp.int32, (count, 1), 0)
    return first + ((row // block) ^ t) * block + row % block


def attn_kernel(
    heads, s_ref, q_ref, k0, k1, k2, k3, w_ref, att_o, lse_o, p0, p1, p2, p3, k_s, vt_s, m_s, l_s, a_s
):
    c, t, prefix = s_ref[0], s_ref[1], s_ref[2]
    block = q_ref.shape[2]
    keys = 4 * block
    wide = heads * block
    for ck in range(4):
        m = c ^ ck
        v = jnp.concatenate([r[m, :, LANES:] for r in (k0, k1, k2, k3)], axis=0)
        vt_s[ck] = jnp.transpose(v.astype(F32)).astype(BF)
        for i, r in enumerate((k0, k1, k2, k3)):
            k_s[ck, i * block : (i + 1) * block] = r[m, :, :LANES]
    mask = side_mask(c, heads, block)
    q_at = lax.broadcasted_iota(jnp.int32, (1, wide), 1) % block + t * block

    for cq in range(4):
        m = c ^ cq
        q = q_ref[m].reshape(wide, LANES)
        m_s[...] = jnp.full_like(m_s, MASKED)
        l_s[...] = jnp.zeros_like(l_s)
        a_s[...] = jnp.zeros_like(a_s)

        def step(ck, q=q, cq=cq):
            s = nt(k_s[ck], q)
            if ck >= cq:
                at = key_positions(t, block, ck * keys, keys)
                seen = (at <= q_at + cq * keys) | (at < prefix)
                s = jnp.where(seen, s, MASKED)
            old = m_s[...]
            top = jnp.maximum(old, jnp.max(s, axis=0, keepdims=True))
            p = jnp.exp(s - top)
            decay = jnp.exp(old - top)
            l_s[...] = l_s[...] * decay + jnp.sum(p, axis=0, keepdims=True)
            a_s[...] = a_s[...] * decay + nn(vt_s[ck], p.astype(BF))
            m_s[...] = top

        for ck in range(4):
            if ck <= cq:
                step(ck)
            else:
                pl.when(ck * keys < prefix)(functools.partial(step, ck))
        o = jnp.transpose(a_s[...] / l_s[...])
        o = jnp.where(mask, o, 0.0).astype(BF)
        for h in range(heads):
            att_o[m, :, h * LANES : (h + 1) * LANES] = o[h * block : (h + 1) * block]
        lse_o[cq] = m_s[...] + jnp.log(l_s[...])
    full = att_o[...].reshape(4 * block, heads * LANES)
    w_at = (heads + 2) * LANES
    part = nn(full, w_ref[w_at : w_at + heads * LANES]).astype(BF)
    for m, r in enumerate((p0, p1, p2, p3)):
        r[...] = part[m * block : (m + 1) * block]


def attn_back_kernel(
    heads, s_ref, y0, y1, y2, y3, w_ref, q_ref, k0, k1, k2, k3, att_ref, lse_ref, cos_ref, sin_ref,
    rows_o, dq_o, g0, g1, g2, g3, do_s, de_s, dqt_s, dk_s, dv_s
):
    c, t, prefix = s_ref[0], s_ref[1], s_ref[2]
    block = q_ref.shape[2]
    keys = 4 * block
    wide = heads * block
    for m, y in enumerate((y0, y1, y2, y3)):
        rows_o[m] = y[...]
    w_at = (heads + 2) * LANES
    do = nt(rows_o[...].reshape(keys, y0.shape[1]), w_ref[w_at : w_at + heads * LANES]).astype(BF)
    for m in range(4):
        for h in range(heads):
            do_s[m, h * block : (h + 1) * block] = do[m * block : (m + 1) * block, h * LANES : (h + 1) * LANES]
    mask = side_mask(c, heads, block)
    for cq in range(4):
        m = c ^ cq
        a = att_ref[m]
        a = jnp.concatenate([a[:, h * LANES : (h + 1) * LANES] for h in range(heads)], axis=0)
        prod = a.astype(F32) * do_s[m].astype(F32)
        de_s[cq] = jnp.sum(jnp.transpose(prod), axis=0, keepdims=True)
    dqt_s[...] = jnp.zeros_like(dqt_s)
    q_at = lax.broadcasted_iota(jnp.int32, (1, wide), 1) % block + t * block
    for ck in range(4):
        mk = c ^ ck
        k = jnp.concatenate([r[mk, :, :LANES] for r in (k0, k1, k2, k3)], axis=0)
        v = jnp.concatenate([r[mk, :, LANES:] for r in (k0, k1, k2, k3)], axis=0)
        kt = jnp.transpose(k.astype(F32)).astype(BF)
        dk_s[...] = jnp.zeros_like(dk_s)
        dv_s[...] = jnp.zeros_like(dv_s)

        def step(cq, k=k, v=v, kt=kt, ck=ck):
            m = c ^ cq
            q = q_ref[m].reshape(wide, LANES)
            d_out = do_s[m]
            p = jnp.exp(nt(k, q) - lse_ref[cq])
            if ck >= cq:
                at = key_positions(t, block, ck * keys, keys)
                seen = (at <= q_at + cq * keys) | (at < prefix)
                p = jnp.where(seen, p, 0.0)
            ds = (p * (nt(v, d_out) - de_s[cq])).astype(BF)
            dk_s[...] += nn(ds, q)
            dv_s[...] += nn(p.astype(BF), d_out)
            dqt_s[cq] += nn(kt, ds)

        for cq in range(4):
            if cq >= ck:
                step(cq)
            else:
                pl.when(ck * keys < prefix)(functools.partial(step, cq))
        for i, r in enumerate((g0, g1, g2, g3)):
            r[mk, :, :LANES] = dk_s[i * block : (i + 1) * block].astype(BF)
            r[mk, :, LANES:] = dv_s[i * block : (i + 1) * block].astype(BF)
    for cq in range(4):
        m = c ^ cq
        dq = jnp.transpose(dqt_s[cq]) * 0.125
        turned = half_turn(dq)
        cos, sin = cos_ref[m], sin_ref[m]
        for h in range(heads):
            own = slice(h * block, (h + 1) * block)
            back = dq[own] * cos - turned[own] * sin
            dq_o[m, :, h * LANES : (h + 1) * LANES] = jnp.where(mask[own], back, 0.0).astype(BF)


def proj_back_kernel(heads, g0, g1, g2, g3, dq_ref, w_ref, cos_ref, sin_ref, d_o, p0, p1, p2, p3):
    block = dq_ref.shape[1]
    low = heads * LANES
    for m in range(4):
        d_o[m, :, :low] = dq_ref[m]
        total = (
            g0[m].astype(F32) + g1[m].astype(F32) + g2[m].astype(F32) + g3[m].astype(F32)
        )
        dk = total[:, :LANES]
        dk = dk * cos_ref[m] - half_turn(dk) * sin_ref[m]
        d_o[m, :, low : low + LANES] = dk.astype(BF)
        d_o[m, :, low + LANES :] = total[:, LANES:].astype(BF)
    full = d_o[...].reshape(4 * block, low + 2 * LANES)
    part = nn(full, w_ref[: low + 2 * LANES]).astype(BF)
    for m, r in enumerate((p0, p1, p2, p3)):
        r[...] = part[m * block : (m + 1) * block]


def chunks(width, step=256):
    return [(at, min(step, width - at)) for at in range(0, width, step)]


def ffn_kernel(x0, x1, x2, x3, w_ref, rows_o, gate_o, up_o, p0, p1, p2, p3, acc):
    block = x0.shape[0]
    for m, x in enumerate((x0, x1, x2, x3)):
        rows_o[m] = x[...]
    rows = rows_o[...].reshape(4 * block, x0.shape[1])
    for at, width in chunks(w_ref.shape[1]):
        g = nt(rows, w_ref[0, at : at + width])
        u = nt(rows, w_ref[1, at : at + width])
        gate_o[:, at : at + width] = g.astype(BF)
        up_o[:, at : at + width] = u.astype(BF)
        hidden = (g / (1.0 + jnp.exp(-g)) * u).astype(BF)
        term = nn(hidden, w_ref[2, at : at + width])
        if at == 0:
            acc[...] = term
        else:
            acc[...] += term
    for m, r in enumerate((p0, p1, p2, p3)):
        r[...] = acc[m * block : (m + 1) * block].astype(BF)


def ffn_back_kernel(
    y0, y1, y2, y3, w_ref, gate_ref, up_ref, rows_o, dg_o, du_o, h_o, p0, p1, p2, p3, acc
):
    block = y0.shape[0]
    for m, y in enumerate((y0, y1, y2, y3)):
        rows_o[m] = y[...]
    rows = rows_o[...].reshape(4 * block, y0.shape[1])
    for at, width in chunks(w_ref.shape[1]):
        own = slice(at, at + width)
        dh = nt(rows, w_ref[2, own])
        g = gate_ref[:, own].astype(F32)
        u = up_ref[:, own].astype(F32)
        s = 1.0 / (1.0 + jnp.exp(-g))
        dg = (dh * u * s * (1.0 + g * (1.0 - s))).astype(BF)
        du = (dh * g * s).astype(BF)
        dg_o[:, own] = dg
        du_o[:, own] = du
        h_o[:, own] = (g * s * u).astype(BF)
        term = nn(dg, w_ref[0, own]) + nn(du, w_ref[1, own])
        if at == 0:
            acc[...] = term
        else:
            acc[...] += term
    for m, r in enumerate((p0, p1, p2, p3)):
        r[...] = acc[m * block : (m + 1) * block].astype(BF)


def weight_grad_kernel(parts, count, *refs):
    lefts, rights, outs = refs[:count], refs[count : 2 * count], refs[2 * count :]
    cols = rights[0].shape[-1] // parts
    rows = lefts[0].shape[0]
    for x in range(parts):
        for at, width in chunks(lefts[0].shape[1]):
            total = None
            for left, right in zip(lefts, rights):
                r = right[:, :, x * cols : (x + 1) * cols].reshape(rows, cols)
                term = tn(left[:, at : at + width], r)
                total = term if total is None else total + term
            outs[x][at : at + width] = total.astype(BF)


def pad_kernel(heads, s_ref, w_ref, o_ref):
    c = s_ref[0]
    o_ref[...] = jnp.zeros_like(o_ref)
    for h in range(heads):
        side = head_side(c, heads, h) * D
        o_ref[pl.ds(pl.multiple_of(h * LANES + side, D), D)] = w_ref[h * D : (h + 1) * D]
        o_ref[pl.ds(pl.multiple_of((heads + 2 + h) * LANES + side, D), D)] = w_ref[
            heads * D + 2 * LANES + h * D : heads * D + 2 * LANES + (h + 1) * D
        ]
    o_ref[heads * LANES : (heads + 2) * LANES] = w_ref[heads * D : heads * D + 2 * LANES]


def unpad_kernel(heads, s_ref, a_ref, b_ref, o_ref):
    c = s_ref[0]
    for h in range(heads):
        at = pl.multiple_of(h * LANES + head_side(c, heads, h) * D, D)
        o_ref[h * D : (h + 1) * D] = a_ref[pl.ds(at, D)]
        lo = heads * D + 2 * LANES + h * D
        o_ref[lo : lo + D] = b_ref[pl.ds(at, D)]
    o_ref[heads * D : heads * D + 2 * LANES] = a_ref[heads * LANES : (heads + 2) * LANES]


def rms(v):
    r = lax.rsqrt(jnp.mean(v * v, axis=-1, keepdims=True) + EPS)
    return v * r, r


def per_device(
    tokens, prefix, w_query, key_weight, value_weight, w_out, w_gate, w_up, w_down, gain_attn, gain_ffn,
    cotangent,
):
    layers = w_query.shape[0]
    seqs, block, width = tokens.shape
    dps = lax.axis_size("dp")
    x, c, t = (lax.axis_index(a) for a in ("dp", "ctx", "tp"))
    heads = w_query.shape[2] // D
    share = w_query.shape[1]
    part = 4 * share
    units = w_gate.shape[2]
    quarter = units // 4
    low = (c * heads) // GROUP
    keys = 4 * block
    long = 4 * keys

    half = D // 2
    freq = jnp.exp(-math.log(10000.0) * jnp.arange(half).astype(F32) / half)
    at = ((c ^ jnp.arange(4)) * keys + t * block)[:, None] + jnp.arange(block)[None, :]
    angle = at.astype(F32).reshape(keys, 1) * freq[None, :]
    cos = jnp.tile(jnp.cos(angle), (1, 4))
    sin = jnp.sin(angle)
    sin = jnp.concatenate([-sin, sin, -sin, sin], axis=1)
    cos4, sin4 = cos.reshape(4, block, LANES), sin.reshape(4, block, LANES)
    scalars = [
        jnp.stack([c, t, prefix[s]]).astype(jnp.int32) for s in range(seqs)
    ]

    gains = jnp.stack([gain_attn, gain_ffn])
    gains = lax.all_gather(gains, ("dp", "ctx"), axis=2, tiled=True).astype(F32)

    def spread_dp(own):
        if dps == 2:
            other = lax.ppermute(own, "dp", [(0, 1), (1, 0)])
            return jnp.concatenate(
                [jnp.where(x == 0, own, other), jnp.where(x == 0, other, own)], axis=-1
            )
        return lax.all_gather(own, "dp", axis=own.ndim - 1, tiled=True)

    def attn_weights(l):
        qo = jnp.concatenate([w_query[l], w_out[l]], axis=1)
        slots = jnp.stack(tp_gather(qo))
        to_ctx = jnp.stack(
            [lax.dynamic_index_in_dim(slots, t ^ i, 0, keepdims=False) for i in range(4)]
        )
        got = ctx_exchange(to_ctx, True).reshape(part, 2 * heads * D).T
        kv = jnp.concatenate([key_weight[l], value_weight[l]], axis=1)
        kv = by_ctx(jnp.stack([kv] + [flip(kv, "ctx", m) for m in (1, 2, 3)]))
        kv = kv.reshape(part, 2 * KEY_VALUE_HEADS * D).T
        k = lax.dynamic_slice_in_dim(kv, low * D, 2 * D, 0)
        v = lax.dynamic_slice_in_dim(kv, (KEY_VALUE_HEADS + low) * D, 2 * D, 0)
        own = jnp.concatenate([got[: heads * D], k, v, got[heads * D :]], axis=0)
        full = spread_dp(own)
        return call(
            functools.partial(pad_kernel, heads),
            [scalars[0], full],
            [((2 * (heads + 1) * LANES, width), BF)],
            smem=1,
        )[0]

    def ffn_weights(l):
        raw = jnp.concatenate([w_gate[l], w_up[l], w_down[l]], axis=0).T
        got = ctx_exchange(raw.reshape(4, quarter, 3 * share), True)
        own = jnp.transpose(got.reshape(4, quarter, 3, share), (2, 1, 0, 3)).reshape(
            3, quarter, part
        )
        slots = [spread_dp(s) for s in tp_gather(own)]
        return jnp.concatenate(slots, axis=1)

    watt = [None] * layers
    wffn = [None] * layers
    for l in range(layers):
        watt[l] = attn_weights(l)
        wffn[l] = ffn_weights(l)

    stream = [tokens[s].astype(F32) for s in range(seqs)]
    kept = {}
    for l in range(layers):
        for s in range(seqs):
            u, _ = rms(stream[s])
            pieces = ctx_gather((u * gains[0, l]).astype(BF))
            rows, q, kv = call(
                functools.partial(qkv_kernel, heads),
                [scalars[s], *pieces, watt[l], cos, sin],
                [((4, block, width), BF), ((4, heads, block, LANES), BF), ((4, block, 2 * LANES), BF)],
                smem=1,
                flops=2 * keys * width * (heads + 2) * LANES,
            )
            kvs = tp_gather(kv)
            att, lse, *parts = call(
                functools.partial(attn_kernel, heads),
                [scalars[s], q, *kvs, watt[l]],
                [((4, block, heads * LANES), BF), ((4, 1, heads * block), F32)] + [((block, width), BF)] * 4,
                smem=1,
                scratch=[
                    pltpu.VMEM((4, keys, LANES), BF),
                    pltpu.VMEM((4, LANES, keys), BF),
                    pltpu.VMEM((1, heads * block), F32),
                    pltpu.VMEM((1, heads * block), F32),
                    pltpu.VMEM((LANES, heads * block), F32),
                ],
                flops=2 * 2 * keys * long * heads * 256 * 0.7 + 2 * keys * heads * LANES * width,
                exps=keys * long * heads,
            )
            middle = stream[s] + ctx_reduce(parts)
            u, _ = rms(middle)
            pieces = ctx_gather((u * gains[1, l]).astype(BF))
            frows, gate, up, *parts = call(
                ffn_kernel,
                [*pieces, wffn[l]],
                [((4, block, width), BF)] + [((keys, units), BF)] * 2 + [((block, width), BF)] * 4,
                scratch=[pltpu.VMEM((keys, width), F32)],
                flops=2 * keys * width * units * 3,
            )
            kept[l, s] = (stream[s], rows, q, kvs, att, lse, middle, frows, gate, up)
            stream[s] = middle + ctx_reduce(parts)

    def norm_back(grad, local, v, gain):
        u, r = rms(v)
        e = local * gain
        grad = grad + r * (e - u * jnp.mean(e * u, axis=-1, keepdims=True))
        return grad, jnp.sum(local * u, axis=0)

    def weight_grad(lefts, rights):
        n = len(lefts)
        u_count = lefts[0].shape[-1]
        return call(
            functools.partial(weight_grad_kernel, dps if dps == 2 else 1, n),
            [a.reshape(keys, u_count) for a in lefts] + list(rights),
            [((u_count, width // dps), BF)] * 2 if dps == 2 else [((u_count, width), BF)],
            flops=2 * n * keys * u_count * width,
        )

    def collect_dp(halves):
        if dps == 2:
            mine = jnp.where(x == 0, halves[0], halves[1])
            other = jnp.where(x == 0, halves[1], halves[0])
            got = lax.ppermute(other, "dp", [(0, 1), (1, 0)])
            return mine.astype(F32) + got.astype(F32)
        return lax.psum_scatter(
            halves[0], "dp", scatter_dimension=halves[0].ndim - 1, tiled=True
        ).astype(F32)

    grads = {}

    def ffn_grads(l, lefts_rights):
        sums = [collect_dp(weight_grad(a, b)).reshape(4, quarter, part) for a, b in lefts_rights]
        slots = [jnp.stack([s[i] for s in sums]).astype(BF) for i in range(4)]
        own = tp_reduce(slots).reshape(3 * quarter, part).astype(BF)
        got = ctx_exchange(own.T.reshape(4, share, 3 * quarter), False).astype(F32)
        got = jnp.transpose(got.reshape(4, share, 3, quarter), (2, 1, 0, 3)).reshape(3, share, units)
        grads[l, "g"], grads[l, "u"], grads[l, "d"] = got[0], got[1], got[2]

    def attn_grads(l, dqkv, rows, att, drows):
        a = weight_grad(dqkv, rows)
        b = weight_grad(att, drows)
        halves = [
            call(
                functools.partial(unpad_kernel, heads),
                [scalars[0], i, j],
                [((2 * heads * D + 2 * LANES, i.shape[1]), BF)],
                smem=1,
            )[0]
            for i, j in zip(a, b)
        ]
        own = collect_dp(halves).astype(BF).T.reshape(4, share, 2 * heads * D + 2 * LANES)
        got = ctx_exchange(own, False)
        lo, hi = heads * D, heads * D + 2 * LANES
        qo = jnp.concatenate([got[:, :, :lo], got[:, :, hi:]], axis=-1)
        qo = [lax.dynamic_index_in_dim(qo, t ^ i, 0, keepdims=False) for i in range(4)]
        qo = tp_reduce(qo)
        grads[l, "q"], grads[l, "o"] = qo[:, :lo], qo[:, lo:]
        kv = got[:, :, lo:hi].astype(F32)
        both = []
        for first in (0, LANES):
            total = jnp.zeros((share, KEY_VALUE_HEADS * D), F32)
            for i in range(4):
                h = i * heads // GROUP
                term = kv[i, :, first : first + LANES]
                total = total + jnp.pad(term, ((0, 0), (h * D, (KEY_VALUE_HEADS - 2 - h) * D)))
            both.append(total)
        both = jnp.concatenate(both, axis=1)
        sent = both.astype(BF)
        for m in (1, 2, 3):
            both = both + flip(sent, "tp", m).astype(F32)
        grads[l, "k"], grads[l, "v"] = (
            both[:, : KEY_VALUE_HEADS * D],
            both[:, KEY_VALUE_HEADS * D :],
        )

    grad = [cotangent[s].astype(F32) for s in range(seqs)]
    gain_sums = {}
    for l in reversed(range(layers)):
        hidden, dgate, dup, dy = [], [], [], []
        gain_sums[1, l] = 0.0
        gain_sums[0, l] = 0.0
        for s in range(seqs):
            _, _, _, _, _, _, middle, frows, gate, up = kept[l, s]
            drows, dg, du, hid, *parts = call(
                ffn_back_kernel,
                [*ctx_gather(grad[s].astype(BF)), wffn[l], gate, up],
                [((4, block, width), BF)] + [((keys, units), BF)] * 3 + [((block, width), BF)] * 4,
                scratch=[pltpu.VMEM((keys, width), F32)],
                flops=2 * keys * width * units * 3,
            )
            hidden.append(hid), dgate.append(dg), dup.append(du), dy.append(drows)
            grad[s], extra = norm_back(grad[s], ctx_reduce(parts), middle, gains[1, l])
            gain_sums[1, l] += extra
        ffn_grads(
            l,
            [
                (dgate, [kept[l, s][7] for s in range(seqs)]),
                (dup, [kept[l, s][7] for s in range(seqs)]),
                (hidden, dy),
            ],
        )
        dqkvs, dys = [], []
        for s in range(seqs):
            start, rows, q, kvs, att, lse, *_ = kept[l, s]
            drows, dq, *dkv = call(
                functools.partial(attn_back_kernel, heads),
                [scalars[s], *ctx_gather(grad[s].astype(BF)), watt[l], q, *kvs, att, lse, cos4, sin4],
                [((4, block, width), BF), ((4, block, heads * LANES), BF)] + [((4, block, 2 * LANES), BF)] * 4,
                smem=1,
                scratch=[
                    pltpu.VMEM((4, heads * block, LANES), BF),
                    pltpu.VMEM((4, 1, heads * block), F32),
                    pltpu.VMEM((4, LANES, heads * block), F32),
                    pltpu.VMEM((keys, LANES), F32),
                    pltpu.VMEM((keys, LANES), F32),
                ],
                flops=2 * 5 * keys * long * heads * 256 * 0.7 + 2 * keys * heads * LANES * width,
                exps=keys * long * heads,
            )
            one = flip(dkv[1], "tp", 1)
            handed = lax.ppermute(dkv[3], "tp", [(0, 1), (3, 2)])
            mid = lax.ppermute(dkv[3], "tp", [(1, 2), (2, 1)])
            two = flip((dkv[2].astype(F32) + handed.astype(F32)).astype(BF), "tp", 2)
            dqkv, *parts = call(
                functools.partial(proj_back_kernel, heads),
                [dkv[0], one, two, mid, dq, watt[l], cos4, sin4],
                [((4, block, (heads + 2) * LANES), BF)] + [((block, width), BF)] * 4,
                flops=2 * keys * (heads + 2) * LANES * width,
            )
            dqkvs.append(dqkv), dys.append(drows)
            grad[s], extra = norm_back(grad[s], ctx_reduce(parts), start, gains[0, l])
            gain_sums[0, l] += extra
        attn_grads(
            l,
            dqkvs,
            [kept[l, s][1] for s in range(seqs)],
            [kept[l, s][4] for s in range(seqs)],
            dys,
        )

    sums = jnp.stack([gain_sums[k, l] for k in range(2) for l in range(layers)])
    sums = lax.psum(sums, ("dp", "ctx", "tp"))
    sums = lax.dynamic_slice_in_dim(sums, (x * 4 + c) * share, share, 1).reshape(2, layers, share)

    def stacked(name):
        return jnp.stack([grads[l, name] for l in range(layers)])

    return (
        jnp.stack(stream).astype(BF),
        jnp.stack(grad),
        stacked("q"),
        stacked("k"),
        stacked("v"),
        stacked("o"),
        stacked("g"),
        stacked("u"),
        stacked("d"),
        sums[0],
        sums[1],
    )


def solution(mesh):
    rows = P("dp", ("ctx", "tp"), None)
    sharded = P(None, ("dp", "ctx"), "tp")
    heads = P(None, ("dp", "ctx"), None)
    gains = P(None, ("dp", "ctx"))
    in_specs = (rows, P("dp"), sharded, heads, heads, sharded, sharded, sharded, sharded, gains, gains, rows)
    out_specs = (rows, rows, sharded, heads, heads, sharded, sharded, sharded, sharded, gains, gains)
    return jax.shard_map(
        per_device, mesh=mesh, in_specs=in_specs, out_specs=out_specs, check_vma=False
    )
```

```python
import functools
import math
import types

import jax
import jax.numpy as jnp
from jax import lax
from jax.experimental import pallas as pl
from jax.experimental.pallas import tpu as pltpu
from jax.sharding import PartitionSpec as P

QUERY_HEADS = 20
KEY_VALUE_HEADS = 5
D = 64
GROUP = QUERY_HEADS // KEY_VALUE_HEADS
EPS = 1e-05
MASKED = -1e30
BF = jnp.bfloat16
F32 = jnp.float32
SLOTS = 4
LANES = 128
DP, CTX, TP = "dp", "ctx", "tp"
PREFIX_MAX = 1024


def nt(a, b):
    return lax.dot_general(a, b, (((1,), (1,)), ((), ())), preferred_element_type=F32)


def nn(a, b):
    return lax.dot_general(a, b, (((1,), (0,)), ((), ())), preferred_element_type=F32)


def tn(a, b):
    return lax.dot_general(a, b, (((0,), (0,)), ((), ())), preferred_element_type=F32)


def half_turn(x):
    lane = lax.broadcasted_iota(jnp.int32, x.shape, 1)
    return jnp.where((lane & 32) == 0, pltpu.roll(x, LANES - 32, 1), pltpu.roll(x, 32, 1))


def call(kernel, ins, outs, smem=0, scratch=(), flops=0, exps=0, vmem=56):
    total = sum(math.prod(a.shape) * a.dtype.itemsize for a in ins) + sum(
        math.prod(s) * jnp.dtype(d).itemsize for s, d in outs
    )
    return pl.pallas_call(
        kernel,
        out_shape=[jax.ShapeDtypeStruct(s, d) for s, d in outs],
        in_specs=[pl.BlockSpec(memory_space=pltpu.SMEM)] * smem
        + [pl.BlockSpec(memory_space=pltpu.VMEM)] * (len(ins) - smem),
        out_specs=[pl.BlockSpec(memory_space=pltpu.VMEM)] * len(outs),
        scratch_shapes=list(scratch),
        compiler_params=pltpu.CompilerParams(vmem_limit_bytes=vmem * 2**20),
        cost_estimate=pl.CostEstimate(
            flops=int(flops), bytes_accessed=int(total), transcendentals=int(exps)
        ),
    )(*ins)


def flip(x, axis, m):
    return lax.ppermute(x, axis, [(i, i ^ m) for i in range(4)])


def ctx_gather(x):
    far = flip(x, CTX, 2)
    return [x, flip(x, CTX, 1), far, flip(far, CTX, 1)]


def ctx_reduce(parts):
    far = (parts[2].astype(F32) + flip(parts[3], CTX, 1).astype(F32)).astype(BF)
    near = flip(parts[1], CTX, 1)
    return parts[0].astype(F32) + near.astype(F32) + flip(far, CTX, 2).astype(F32)


def inner(t):
    return (t == 1) | (t == 2)


def tp_gather(x):
    t = lax.axis_index(TP)
    two = flip(x, TP, 2)
    mid = lax.ppermute(x, TP, [(1, 2), (2, 1)])
    end = lax.ppermute(two, TP, [(1, 0), (2, 3)])
    return [x, flip(x, TP, 1), two, jnp.where(inner(t), mid, end)]


def tp_reduce(parts):
    one = flip(parts[1], TP, 1)
    handed = lax.ppermute(parts[3], TP, [(0, 1), (3, 2)])
    mid = lax.ppermute(parts[3], TP, [(1, 2), (2, 1)])
    two = flip((parts[2].astype(F32) + handed.astype(F32)).astype(BF), TP, 2)
    return (
        parts[0].astype(F32) + one.astype(F32) + two.astype(F32) + mid.astype(F32)
    )


def ctx_exchange(stacked, own_first):
    c = lax.axis_index(CTX)
    got = []
    for m in range(4):
        piece = lax.dynamic_index_in_dim(stacked, c ^ m, 0, keepdims=False)
        got.append(piece if m == 0 else flip(piece, CTX, m))
    return by_ctx(jnp.stack(got))


def by_ctx(stacked):
    c = lax.axis_index(CTX)
    return jnp.stack(
        [lax.dynamic_index_in_dim(stacked, c ^ i, 0, keepdims=False) for i in range(4)]
    )


def head_side(c, heads, h):
    return (c * heads + h) // GROUP - (c * heads) // GROUP


def qkv_kernel(heads, s_ref, x0, x1, x2, x3, w_ref, cos_ref, sin_ref, rows_o, q_o, kv_o):
    del s_ref
    block = x0.shape[0]
    for m, x in enumerate((x0, x1, x2, x3)):
        rows_o[m] = x[...]
    rows = rows_o[...].reshape(4 * block, x0.shape[1])
    cos, sin = cos_ref[...], sin_ref[...]
    at = 0
    total = (heads + 2) * LANES
    while at < total:
        width = min(3 * LANES, total - at)
        lin = nt(rows, w_ref[at : at + width])
        for j in range(width // LANES):
            slot = at // LANES + j
            v = lin[:, j * LANES : (j + 1) * LANES]
            if slot <= heads:
                v = v * cos + half_turn(v) * sin
            if slot < heads:
                v = (v * 0.125).astype(BF)
                for m in range(4):
                    q_o[m, slot] = v[m * block : (m + 1) * block]
            else:
                v = v.astype(BF)
                lo = (slot - heads) * LANES
                for m in range(4):
                    kv_o[m, :, lo : lo + LANES] = v[m * block : (m + 1) * block]
        at += width


def side_mask(c, heads, block):
    head = lax.broadcasted_iota(jnp.int32, (heads * block, LANES), 0) // block
    lane = lax.broadcasted_iota(jnp.int32, (heads * block, LANES), 1)
    return (lane // D) == ((c * heads + head) // GROUP - (c * heads) // GROUP)


def key_positions(t, block, first, count):
    row = lax.broadcasted_iota(jnp.int32, (count, 1), 0)
    return first + ((row // block) ^ t) * block + row % block


def attn_kernel(
    heads, s_ref, q_ref, k0, k1, k2, k3, w_ref, att_o, lse_o, p0, p1, p2, p3, k_s, vt_s, m_s, l_s, a_s
):
    c, t, prefix = s_ref[0], s_ref[1], s_ref[2]
    block = q_ref.shape[2]
    keys = 4 * block
    wide = heads * block
    for ck in range(4):
        m = c ^ ck
        v = jnp.concatenate([r[m, :, LANES:] for r in (k0, k1, k2, k3)], axis=0)
        vt_s[ck] = jnp.transpose(v.astype(F32)).astype(BF)
        for i, r in enumerate((k0, k1, k2, k3)):
            k_s[ck, i * block : (i + 1) * block] = r[m, :, :LANES]
    mask = side_mask(c, heads, block)
    q_at = lax.broadcasted_iota(jnp.int32, (1, wide), 1) % block + t * block

    for cq in range(4):
        m = c ^ cq
        q = q_ref[m].reshape(wide, LANES)
        m_s[...] = jnp.full_like(m_s, MASKED)
        l_s[...] = jnp.zeros_like(l_s)
        a_s[...] = jnp.zeros_like(a_s)

        def step(ck, q=q, cq=cq):
            s = nt(k_s[ck], q)
            if ck >= cq:
                at = key_positions(t, block, ck * keys, keys)
                seen = (at <= q_at + cq * keys) | (at < prefix)
                s = jnp.where(seen, s, MASKED)
            old = m_s[...]
            top = jnp.maximum(old, jnp.max(s, axis=0, keepdims=True))
            p = jnp.exp(s - top)
            decay = jnp.exp(old - top)
            l_s[...] = l_s[...] * decay + jnp.sum(p, axis=0, keepdims=True)
            a_s[...] = a_s[...] * decay + nn(vt_s[ck], p.astype(BF))
            m_s[...] = top

        for ck in range(4):
            if ck <= cq:
                step(ck)
            else:
                pl.when(ck * keys < prefix)(functools.partial(step, ck))
        o = jnp.transpose(a_s[...] / l_s[...])
        o = jnp.where(mask, o, 0.0).astype(BF)
        for h in range(heads):
            att_o[m, :, h * LANES : (h + 1) * LANES] = o[h * block : (h + 1) * block]
        lse_o[cq] = m_s[...] + jnp.log(l_s[...])
    full = att_o[...].reshape(4 * block, heads * LANES)
    w_at = (heads + 2) * LANES
    part = nn(full, w_ref[w_at : w_at + heads * LANES]).astype(BF)
    for m, r in enumerate((p0, p1, p2, p3)):
        r[...] = part[m * block : (m + 1) * block]


def attn_back_kernel(
    heads, s_ref, y0, y1, y2, y3, w_ref, q_ref, k0, k1, k2, k3, att_ref, lse_ref, cos_ref, sin_ref,
    rows_o, dq_o, g0, g1, g2, g3, do_s, de_s, dqt_s, dk_s, dv_s
):
    c, t, prefix = s_ref[0], s_ref[1], s_ref[2]
    block = q_ref.shape[2]
    keys = 4 * block
    wide = heads * block
    for m, y in enumerate((y0, y1, y2, y3)):
        rows_o[m] = y[...]
    w_at = (heads + 2) * LANES
    do = nt(rows_o[...].reshape(keys, y0.shape[1]), w_ref[w_at : w_at + heads * LANES]).astype(BF)
    for m in range(4):
        for h in range(heads):
            do_s[m, h * block : (h + 1) * block] = do[m * block : (m + 1) * block, h * LANES : (h + 1) * LANES]
    mask = side_mask(c, heads, block)
    for cq in range(4):
        m = c ^ cq
        a = att_ref[m]
        a = jnp.concatenate([a[:, h * LANES : (h + 1) * LANES] for h in range(heads)], axis=0)
        prod = a.astype(F32) * do_s[m].astype(F32)
        de_s[cq] = jnp.sum(jnp.transpose(prod), axis=0, keepdims=True)
    dqt_s[...] = jnp.zeros_like(dqt_s)
    q_at = lax.broadcasted_iota(jnp.int32, (1, wide), 1) % block + t * block
    for ck in range(4):
        mk = c ^ ck
        k = jnp.concatenate([r[mk, :, :LANES] for r in (k0, k1, k2, k3)], axis=0)
        v = jnp.concatenate([r[mk, :, LANES:] for r in (k0, k1, k2, k3)], axis=0)
        kt = jnp.transpose(k.astype(F32)).astype(BF)
        dk_s[...] = jnp.zeros_like(dk_s)
        dv_s[...] = jnp.zeros_like(dv_s)

        def step(cq, k=k, v=v, kt=kt, ck=ck):
            m = c ^ cq
            q = q_ref[m].reshape(wide, LANES)
            d_out = do_s[m]
            p = jnp.exp(nt(k, q) - lse_ref[cq])
            if ck >= cq:
                at = key_positions(t, block, ck * keys, keys)
                seen = (at <= q_at + cq * keys) | (at < prefix)
                p = jnp.where(seen, p, 0.0)
            ds = (p * (nt(v, d_out) - de_s[cq])).astype(BF)
            dk_s[...] += nn(ds, q)
            dv_s[...] += nn(p.astype(BF), d_out)
            dqt_s[cq] += nn(kt, ds)

        for cq in range(4):
            if cq >= ck:
                step(cq)
            else:
                pl.when(ck * keys < prefix)(functools.partial(step, cq))
        for i, r in enumerate((g0, g1, g2, g3)):
            r[mk, :, :LANES] = dk_s[i * block : (i + 1) * block].astype(BF)
            r[mk, :, LANES:] = dv_s[i * block : (i + 1) * block].astype(BF)
    for cq in range(4):
        m = c ^ cq
        dq = jnp.transpose(dqt_s[cq]) * 0.125
        turned = half_turn(dq)
        cos, sin = cos_ref[m], sin_ref[m]
        for h in range(heads):
            own = slice(h * block, (h + 1) * block)
            back = dq[own] * cos - turned[own] * sin
            dq_o[m, :, h * LANES : (h + 1) * LANES] = jnp.where(mask[own], back, 0.0).astype(BF)


def proj_back_kernel(heads, g0, g1, g2, g3, dq_ref, w_ref, cos_ref, sin_ref, d_o, p0, p1, p2, p3):
    block = dq_ref.shape[1]
    low = heads * LANES
    for m in range(4):
        d_o[m, :, :low] = dq_ref[m]
        total = (
            g0[m].astype(F32) + g1[m].astype(F32) + g2[m].astype(F32) + g3[m].astype(F32)
        )
        dk = total[:, :LANES]
        dk = dk * cos_ref[m] - half_turn(dk) * sin_ref[m]
        d_o[m, :, low : low + LANES] = dk.astype(BF)
        d_o[m, :, low + LANES :] = total[:, LANES:].astype(BF)
    full = d_o[...].reshape(4 * block, low + 2 * LANES)
    part = nn(full, w_ref[: low + 2 * LANES]).astype(BF)
    for m, r in enumerate((p0, p1, p2, p3)):
        r[...] = part[m * block : (m + 1) * block]


def chunks(width, step=256):
    return [(at, min(step, width - at)) for at in range(0, width, step)]


def ffn_kernel(x0, x1, x2, x3, w_ref, rows_o, gate_o, up_o, p0, p1, p2, p3, acc):
    block = x0.shape[0]
    for m, x in enumerate((x0, x1, x2, x3)):
        rows_o[m] = x[...]
    rows = rows_o[...].reshape(4 * block, x0.shape[1])
    for at, width in chunks(w_ref.shape[1]):
        g = nt(rows, w_ref[0, at : at + width])
        u = nt(rows, w_ref[1, at : at + width])
        gate_o[:, at : at + width] = g.astype(BF)
        up_o[:, at : at + width] = u.astype(BF)
        hidden = (g / (1.0 + jnp.exp(-g)) * u).astype(BF)
        term = nn(hidden, w_ref[2, at : at + width])
        if at == 0:
            acc[...] = term
        else:
            acc[...] += term
    for m, r in enumerate((p0, p1, p2, p3)):
        r[...] = acc[m * block : (m + 1) * block].astype(BF)


def ffn_back_kernel(
    y0, y1, y2, y3, w_ref, gate_ref, up_ref, rows_o, dg_o, du_o, h_o, p0, p1, p2, p3, acc
):
    block = y0.shape[0]
    for m, y in enumerate((y0, y1, y2, y3)):
        rows_o[m] = y[...]
    rows = rows_o[...].reshape(4 * block, y0.shape[1])
    for at, width in chunks(w_ref.shape[1]):
        own = slice(at, at + width)
        dh = nt(rows, w_ref[2, own])
        g = gate_ref[:, own].astype(F32)
        u = up_ref[:, own].astype(F32)
        s = 1.0 / (1.0 + jnp.exp(-g))
        dg = (dh * u * s * (1.0 + g * (1.0 - s))).astype(BF)
        du = (dh * g * s).astype(BF)
        dg_o[:, own] = dg
        du_o[:, own] = du
        h_o[:, own] = (g * s * u).astype(BF)
        term = nn(dg, w_ref[0, own]) + nn(du, w_ref[1, own])
        if at == 0:
            acc[...] = term
        else:
            acc[...] += term
    for m, r in enumerate((p0, p1, p2, p3)):
        r[...] = acc[m * block : (m + 1) * block].astype(BF)


def weight_grad_kernel(parts, count, *refs):
    lefts, rights, outs = refs[:count], refs[count : 2 * count], refs[2 * count :]
    cols = rights[0].shape[-1] // parts
    rows = lefts[0].shape[0]
    for x in range(parts):
        for at, width in chunks(lefts[0].shape[1]):
            total = None
            for left, right in zip(lefts, rights):
                r = right[:, :, x * cols : (x + 1) * cols].reshape(rows, cols)
                term = tn(left[:, at : at + width], r)
                total = term if total is None else total + term
            outs[x][at : at + width] = total.astype(BF)


def pad_kernel(heads, s_ref, w_ref, o_ref):
    c = s_ref[0]
    o_ref[...] = jnp.zeros_like(o_ref)
    for h in range(heads):
        side = head_side(c, heads, h) * D
        o_ref[pl.ds(pl.multiple_of(h * LANES + side, D), D)] = w_ref[h * D : (h + 1) * D]
        o_ref[pl.ds(pl.multiple_of((heads + 2 + h) * LANES + side, D), D)] = w_ref[
            heads * D + 2 * LANES + h * D : heads * D + 2 * LANES + (h + 1) * D
        ]
    o_ref[heads * LANES : (heads + 2) * LANES] = w_ref[heads * D : heads * D + 2 * LANES]


def unpad_kernel(heads, s_ref, a_ref, b_ref, o_ref):
    c = s_ref[0]
    for h in range(heads):
        at = pl.multiple_of(h * LANES + head_side(c, heads, h) * D, D)
        o_ref[h * D : (h + 1) * D] = a_ref[pl.ds(at, D)]
        lo = heads * D + 2 * LANES + h * D
        o_ref[lo : lo + D] = b_ref[pl.ds(at, D)]
    o_ref[heads * D : heads * D + 2 * LANES] = a_ref[heads * LANES : (heads + 2) * LANES]


def xor(a, b):
    return lax.rem(a + b, 2) + 2 * lax.rem(lax.div(a, 2) + lax.div(b, 2), 2)


class Net:
    def __init__(self, r):
        self.r = r
        self.sems = (r.send, r.recv, r.loc)
        self.remote, self.local_at = 0, 0
        self.x, self.c, self.t = (lax.axis_index(a) for a in (DP, CTX, TP))
        self.inner = (self.t == 1) | (self.t == 2)

    def barrier(self):
        sem = pltpu.get_barrier_semaphore()
        peers = [(CTX, 1), (CTX, 2), (CTX, 3), (TP, 1), (TP, 2), (TP, 3), (DP, 1)]
        for axis, m in peers:
            pl.semaphore_signal(
                sem, inc=1, device_id={axis: self.peer(axis, m)}, device_id_type=pl.DeviceIdType.MESH
            )
        pl.semaphore_wait(sem, len(peers))

    def peer(self, axis, m):
        if axis == DP:
            return 1 - self.x
        return xor(self.c if axis == CTX else self.t, m)

    def make(self, src, dst, axis, m):
        i = self.remote
        self.remote += 1
        return pltpu.make_async_remote_copy(
            src_ref=src,
            dst_ref=dst,
            send_sem=self.sems[0].at[i],
            recv_sem=self.sems[1].at[i],
            device_id={axis: self.peer(axis, m)},
            device_id_type=pl.DeviceIdType.MESH,
        )

    def send(self, src, dst, axis, m=1):
        copy = self.make(src, dst, axis, m)
        copy.start()
        return copy

    def local(self, src, dst):
        i = self.local_at
        self.local_at += 1
        copy = pltpu.make_async_copy(src, dst, self.sems[2].at[i])
        copy.start()
        return copy

    def close(self, copies):
        for copy in copies:
            copy.wait_send()

    def spread_tp(self, src, slots):
        two = self.send(src, slots[2], TP, 2)
        one = self.send(src, slots[1], TP, 1)
        mid = self.make(src, slots[3], TP, 3)
        end = self.make(slots[2], slots[3], TP, 1)
        return one, two, mid, end

    def spread_tp_on(self, copies):
        _, two, mid, end = copies
        two.wait_recv()

        @pl.when(self.inner)
        def _():
            end.start()
            mid.start()

    def spread_tp_last(self, copies):
        _, _, mid, end = copies
        pl.when(self.inner)(mid.wait_recv)
        pl.when(jnp.logical_not(self.inner))(end.wait_recv)

    def spread_tp_close(self, copies):
        one, two, mid, end = copies
        self.close([one, two])

        @pl.when(self.inner)
        def _():
            mid.wait_send()
            end.wait_send()


def run(tasks):
    for task in tasks:
        next(task, None)


def forward_kernel(cfg, r):
    layers, seqs, block, width, heads, units, share = cfg
    part, quarter, keys = 4 * share, units // 4, 4 * block
    net = Net(r)
    x, c, t = net.x, net.c, net.t
    low = lax.div(c * heads, GROUP)
    half = pl.ds(pl.multiple_of(x * part, LANES), part)
    prefix = [r.prefix[s] for s in range(seqs)]
    kept = []
    gu_copy = []

    net.barrier()

    def attn_weights(l):
        qz, qc, kvl, own, tmp, wa = r.qz.at[l], r.qc.at[l], r.kvl.at[l], r.own, r.tmp, r.wa
        mine = [net.local(r.qo.at[l], qz.at[0]), net.local(r.kvw.at[l], kvl.at[c])]
        tp = net.spread_tp(r.qo.at[l], [qz.at[i] for i in range(4)])
        kvs = [net.send(r.kvw.at[l], kvl.at[c], CTX, m) for m in (1, 2, 3)]
        wide = heads * LANES
        wa[l, :wide] = jnp.zeros((wide, width), BF)
        wa[l, wide + 2 * LANES :] = jnp.zeros((wide, width), BF)
        yield
        net.spread_tp_on(tp)
        yield
        mine[0].wait()
        tp[0].wait_recv()
        net.spread_tp_last(tp)
        mine.append(net.local(qz.at[xor(t, c)], qc.at[c]))
        ctx = [net.send(qz.at[xor(t, xor(c, m))], qc.at[c], CTX, m) for m in (1, 2, 3)]
        yield
        for copy in kvs + ctx:
            copy.wait_recv()
        mine[1].wait()
        mine[2].wait()
        stage = [net.local(qc, r.st_q), net.local(kvl, r.st_k)]
        stage[0].wait()
        for at in range(0, 2 * heads * D, LANES):
            got = jnp.transpose(r.st_q[:, :, at : at + LANES].reshape(part, LANES).astype(F32)).astype(BF)
            for k in range(0, LANES, D):
                to = at + k if at + k < heads * D else at + k + 2 * LANES
                own[to : to + D] = got[k : k + D]
        stage[1].wait()
        for at in range(0, 2 * KEY_VALUE_HEADS * D, LANES):
            got = r.st_k[:, :, at : at + LANES].reshape(part, LANES)
            tmp[at : at + LANES] = jnp.transpose(got.astype(F32)).astype(BF)
        own[heads * D : heads * D + LANES] = tmp[pl.ds(pl.multiple_of(low * D, D), LANES)]
        own[heads * D + LANES : heads * D + 2 * LANES] = tmp[
            pl.ds(pl.multiple_of((KEY_VALUE_HEADS + low) * D, D), LANES)
        ]
        dp = net.send(own, r.wc.at[l, :, half], DP)
        mine.append(net.local(own, r.wc.at[l, :, half]))
        yield
        dp.wait_recv()
        mine[3].wait()
        pads = []
        for h in range(heads):
            side = (lax.div(c * heads + h, GROUP) - low) * D
            for src, dst in ((h * D, h * LANES), (heads * D + 2 * LANES + h * D, (heads + 2 + h) * LANES)):
                pads.append(
                    net.local(
                        r.wc.at[l, src : src + D],
                        wa.at[l, pl.ds(pl.multiple_of(dst + side, D), D)],
                    )
                )
        pads.append(
            net.local(r.wc.at[l, heads * D : heads * D + 2 * LANES], wa.at[l, wide : wide + 2 * LANES])
        )
        yield
        for copy in pads:
            copy.wait()
        net.close(kvs + ctx + [dp])
        net.spread_tp_close(tp)
        kept.append(net.local(wa.at[l], r.wa_o.at[l]))
        yield

    def ffn_weights(l):
        fc, wf = r.fc.at[l], r.wf
        ctx = [net.send(r.fp.at[l, xor(c, m)], fc.at[c], CTX, m) for m in (1, 2, 3)]
        mine = net.local(r.fp.at[l, c], fc.at[c])
        yield
        for copy in ctx:
            copy.wait_recv()
        mine.wait()
        stage = net.local(fc, r.st_f)
        stage.wait()
        for i in range(3):
            piece = [r.st_f[k][:, i * share : (i + 1) * share] for k in range(4)]
            wf[l, i, :quarter, half] = jnp.concatenate(piece, axis=1)
        yield
        slots = [wf.at[l, :, i * quarter : (i + 1) * quarter, half] for i in range(4)]
        tp = net.spread_tp(slots[0], slots)
        dp = [net.send(slots[0], slots[0], DP)]
        yield
        net.spread_tp_on(tp)
        dp.append(net.send(slots[2], slots[2], DP))
        tp[0].wait_recv()
        dp.append(net.send(slots[1], slots[1], DP))
        yield
        net.spread_tp_last(tp)
        dp.append(net.send(slots[3], slots[3], DP))
        yield
        for copy in dp:
            copy.wait_recv()
        net.close(ctx + dp)
        net.spread_tp_close(tp)
        kept.append(net.local(wf.at[l], r.wf_o.at[l]))
        yield

    def gather_start(v, gain, s, rows):
        u = v * lax.rsqrt(jnp.mean(v * v, axis=-1, keepdims=True) + EPS)
        rows[s, 0] = (u * gain).astype(BF)
        return [
            net.send(rows.at[s, 0], rows.at[s, 2], CTX, 2),
            net.send(rows.at[s, 0], rows.at[s, 1], CTX, 1),
        ]

    def gather_on(copies, s, rows):
        copies[0].wait_recv()
        copies.append(net.send(rows.at[s, 2], rows.at[s, 3], CTX, 1))

    def gather_end(copies):
        copies[1].wait_recv()
        copies[2].wait_recv()

    def reduce_start(s):
        pt, rn = r.pt, r.rn
        return [
            net.send(pt.at[s, 3], rn.at[s, 1], CTX, 1),
            net.send(pt.at[s, 1], rn.at[s, 0], CTX, 1),
        ]

    def reduce_on(copies, s):
        copies[0].wait_recv()
        r.far[s] = (r.pt[s, 2].astype(F32) + r.rn[s, 1].astype(F32)).astype(BF)
        copies.append(net.send(r.far.at[s], r.rf.at[s], CTX, 2))

    def reduce_end(copies, s):
        copies[1].wait_recv()
        copies[2].wait_recv()
        total = r.pt[s, 0].astype(F32) + r.rn[s, 0].astype(F32) + r.rf[s].astype(F32)
        net.close(copies)
        return total

    def sequence(s):
        rows, frows, q, att, pt, gu = r.rows, r.frows, r.q, r.att, r.pt, r.gu
        carry = []
        for l in range(layers):
            kv = r.kv
            gather = gather_start(r.stream[s], r.gain[l : l + 1], s, rows)
            yield
            gather_on(gather, s, rows)
            yield
            gather_end(gather)
            qkv_body(heads, rows.at[s], r.wa.at[l], r.cos, r.sin, q.at[s], kv.at[l, s, 0])
            tp = net.spread_tp(kv.at[l, s, 0], [kv.at[l, s, i] for i in range(4)])
            outs = [net.local(rows.at[s], r.rows_o.at[l, s]), net.local(q.at[s], r.q_o.at[l, s])] + carry
            yield
            net.spread_tp_on(tp)
            yield
            tp[0].wait_recv()
            net.spread_tp_last(tp)
            outs.append(net.local(kv.at[l, s], r.kv_o.at[l, s]))
            attn_body(
                heads, c, t, prefix[s], q.at[s], kv.at[l, s], r.wa.at[l], att.at[s], r.lse.at[s],
                pt.at[s], r.k_s, r.vt_s, r.m_s, r.l_s, r.a_s,
            )
            reduce = reduce_start(s)
            outs.append(net.local(att.at[s], r.att_o.at[l, s]))
            outs.append(net.local(r.lse.at[s], r.lse_o.at[l, s]))
            net.close(gather)
            yield
            reduce_on(reduce, s)
            yield
            r.middle[s] = r.stream[s] + reduce_end(reduce, s)
            outs.append(net.local(r.middle.at[s], r.middle_o.at[l, s]))
            gather = gather_start(r.middle[s], r.gain[layers + l : layers + l + 1], s, frows)
            yield
            gather_on(gather, s, frows)
            yield
            gather_end(gather)
            outs.pop(0).wait()
            if gu_copy:
                gu_copy.pop().wait()
            ffn_body(frows.at[s], r.wf.at[l], gu, pt.at[s], r.hid)
            reduce = reduce_start(s)
            outs.append(net.local(frows.at[s], r.frows_o.at[l, s]))
            gu_copy.append(net.local(gu, r.gu_o.at[l, s]))
            net.close(gather)
            net.spread_tp_close(tp)
            yield
            reduce_on(reduce, s)
            yield
            for copy in outs:
                copy.wait()
            r.stream[s] = r.middle[s] + reduce_end(reduce, s)
            if l + 1 < layers:
                carry = [net.local(r.stream.at[s], r.stream_o.at[l, s])]
            else:
                r.far[s] = r.stream[s].astype(BF)
                kept.append(net.local(r.far.at[s], r.out_o.at[s]))
            yield

    gl = r.gl
    start = net.local(r.tokens, r.far)
    gl[x, c] = r.gains[...]
    near = [net.send(gl.at[x, c], gl.at[x, c], CTX, m) for m in (1, 2, 3)]
    (w0, w1), (f0, f1) = [attn_weights(l) for l in range(layers)], [ffn_weights(l) for l in range(layers)]
    run([f0, w0])
    start.wait()
    r.stream[...] = r.far[...].astype(F32)
    for copy in near:
        copy.wait_recv()
    over = net.send(gl.at[x], gl.at[x], DP)
    over.wait_recv()
    pieces = [gl[k, i][: 2 * layers, :share] for k in range(2) for i in range(4)]
    r.gain[...] = jnp.concatenate(pieces, axis=1)
    kept.append(net.local(r.gain, r.gain_o))

    def cotangent():
        cot, dy = r.cot, r.dy_o
        mine = [net.local(cot.at[s], dy.at[s, 0]) for s in range(seqs)]
        far = [net.send(cot.at[s], dy.at[s, 2], CTX, 2) for s in range(seqs)]
        side = [net.send(cot.at[s], dy.at[s, 1], CTX, 1) for s in range(seqs)]
        yield
        for s in range(seqs):
            far[s].wait_recv()
            side.append(net.send(dy.at[s, 2], dy.at[s, 3], CTX, 1))
        yield
        for copy in side:
            copy.wait_recv()
        for copy in mine:
            copy.wait()
        net.close(far + side)
        yield

    a, b, extra = sequence(0), sequence(1), cotangent()
    order = (
        w0, f0, a, f0, w0, w0, b, f0, b, f1, w0, w0, b, b,
        f1, a, w1, a, f0, b, b, w1, a, f1, w1, b, a, f0,
        a, b, w1, b, a, b, a, f1, a, b, b, a, w1, w1,
        b, b, a, a, b, extra, f1, a, a, b, extra, a, b, a,
        b, a, b, extra, a, f1, b, a, b, a, a, b, a,
    )
    run(order)
    net.close(near + [over])
    for copy in kept + gu_copy:
        copy.wait()


def qkv_body(heads, rows_ref, w_ref, cos_ref, sin_ref, q_o, kv_o):
    block, width = rows_ref.shape[1], rows_ref.shape[2]
    rows = rows_ref[...].reshape(4 * block, width)
    cos, sin = cos_ref[...], sin_ref[...]
    at = 0
    total = (heads + 2) * LANES
    while at < total:
        wide = min(3 * LANES, total - at)
        lin = nt(rows, w_ref[at : at + wide])
        for j in range(wide // LANES):
            slot = at // LANES + j
            v = lin[:, j * LANES : (j + 1) * LANES]
            if slot <= heads:
                v = v * cos + half_turn(v) * sin
            if slot < heads:
                v = (v * 0.125).astype(BF)
                for m in range(4):
                    q_o[m, slot] = v[m * block : (m + 1) * block]
            else:
                v = v.astype(BF)
                lo = (slot - heads) * LANES
                for m in range(4):
                    kv_o[m, :, lo : lo + LANES] = v[m * block : (m + 1) * block]
        at += wide


def attn_body(heads, c, t, prefix, q_ref, kv_ref, w_ref, att_o, lse_o, pt_o, k_s, vt_s, m_s, l_s, a_s):
    block = q_ref.shape[2]
    keys = 4 * block
    wide = heads * block
    for ck in range(4):
        m = xor(c, ck)
        v = jnp.concatenate([kv_ref[i, m, :, LANES:] for i in range(4)], axis=0)
        vt_s[ck] = jnp.transpose(v.astype(F32)).astype(BF)
        for i in range(4):
            k_s[ck, i * block : (i + 1) * block] = kv_ref[i, m, :, :LANES]
    mask = side_mask(c, heads, block)
    q_at = lax.broadcasted_iota(jnp.int32, (1, wide), 1) % block + t * block
    for cq in range(4):
        m = xor(c, cq)
        q_all = q_ref[m].reshape(wide, LANES)
        for first, span in chunks(wide, 3 * LANES):
            own = slice(first, first + span)
            q = q_all[own]
            for ck in range(4):
                if ck > cq and ck * keys >= PREFIX_MAX:
                    continue
                s = nt(k_s[ck], q)
                if ck >= cq:
                    at = key_positions(t, block, ck * keys, keys)
                    seen = (at <= q_at[:, own] + cq * keys) | (at < prefix)
                    s = jnp.where(seen, s, MASKED)
                top = jnp.max(s, axis=0, keepdims=True)
                if ck:
                    old = m_s[:, own]
                    top = jnp.maximum(old, top)
                    decay = jnp.exp(old - top)
                p = jnp.exp(s - top)
                add, term = jnp.sum(p, axis=0, keepdims=True), nn(vt_s[ck], p.astype(BF))
                l_s[:, own] = l_s[:, own] * decay + add if ck else add
                a_s[:, own] = a_s[:, own] * decay + term if ck else term
                m_s[:, own] = top
        o = jnp.transpose(a_s[...] / l_s[...])
        o = jnp.where(mask, o, 0.0).astype(BF)
        for h in range(heads):
            att_o[m, :, h * LANES : (h + 1) * LANES] = o[h * block : (h + 1) * block]
        lse_o[cq] = m_s[...] + jnp.log(l_s[...])
    full = att_o[...].reshape(4 * block, heads * LANES)
    w_at = (heads + 2) * LANES
    for at, span in chunks(w_ref.shape[1]):
        own = slice(at, at + span)
        part = nn(full, w_ref[w_at : w_at + heads * LANES, own]).astype(BF)
        for m in range(4):
            pt_o[m, :, own] = part[m * block : (m + 1) * block]


def ffn_body(rows_ref, w_ref, gu_o, pt_o, hid):
    block, width = rows_ref.shape[1], rows_ref.shape[2]
    rows = rows_ref[...].reshape(4 * block, width)
    for at, wide in chunks(w_ref.shape[1]):
        own = slice(at, at + wide)
        g = nt(rows, w_ref[0, own])
        u = nt(rows, w_ref[1, own])
        gu_o[0, :, own] = g.astype(BF)
        gu_o[1, :, own] = u.astype(BF)
        hid[:, own] = (g / (1.0 + jnp.exp(-g)) * u).astype(BF)
    for at, wide in chunks(width):
        own = slice(at, at + wide)
        part = nn(hid[...], w_ref[2, :, own]).astype(BF)
        for m in range(4):
            pt_o[m, :, own] = part[m * block : (m + 1) * block]


def launch(kernel, number, ins, outs, scratch, sems=(80, 90), vmem=62):
    sem = pltpu.SemaphoreType.DMA
    scratch = {k: pltpu.VMEM(*v) for k, v in scratch.items()}
    scratch.update(send=sem((sems[0],)), recv=sem((sems[0],)), loc=sem((sems[1],)))
    names = [*ins, *outs, *scratch]

    def body(*refs):
        kernel(types.SimpleNamespace(**dict(zip(names, refs))))

    got = pl.pallas_call(
        body,
        out_shape=[jax.ShapeDtypeStruct(v[0], v[1]) for v in outs.values()],
        in_specs=[pl.BlockSpec(memory_space=v[1]) for v in ins.values()],
        out_specs=[pl.BlockSpec(memory_space=v[2]) for v in outs.values()],
        scratch_shapes=list(scratch.values()),
        compiler_params=pltpu.CompilerParams(
            collective_id=number, has_side_effects=True, vmem_limit_bytes=vmem * 2**20
        ),
        cost_estimate=pl.CostEstimate(flops=10**11, bytes_accessed=10**8, transcendentals=10**7),
    )(*[v[0] for v in ins.values()])
    return types.SimpleNamespace(**dict(zip(outs, got)))


def forward_pass(cfg, tokens, cot, prefix, gains, qo, kvw, fp, cos, sin):
    layers, seqs, block, width, heads, units, share = cfg
    hbm, vm = pl.ANY, pltpu.VMEM
    keys, part = 4 * block, 4 * share
    rows = (seqs, 4, block, width)
    own = (seqs, block, width)
    size = 2 * (heads + 1) * LANES
    compact = 2 * heads * D + 2 * LANES
    q_s = (4, heads, block, LANES)
    kv_s = (4, 4, block, 2 * LANES)
    raw = (4, share, 2 * heads * D)
    raw_k = (4, share, 2 * KEY_VALUE_HEADS * D)
    raw_f = (4, units // 4, 3 * share)
    return launch(
        functools.partial(forward_kernel, cfg),
        0,
        dict(
            prefix=(prefix, pltpu.SMEM), tokens=(tokens, hbm), cot=(cot, hbm), gains=(gains, vm), qo=(qo, hbm),
            kvw=(kvw, hbm), fp=(fp, hbm), cos=(cos, vm), sin=(sin, vm),
        ),
        dict(
            out_o=(own, BF, hbm),
            wc=((layers, compact, width), BF, hbm),
            wa_o=((layers, size, width), BF, hbm),
            wf_o=((layers, 3, units, width), BF, hbm),
            rows_o=((layers, *rows), BF, hbm),
            q_o=((layers, seqs, *q_s), BF, hbm),
            kv_o=((layers, seqs, *kv_s), BF, hbm),
            att_o=((layers, seqs, 4, block, heads * LANES), BF, hbm),
            lse_o=((layers, seqs, 4, 1, heads * block), F32, hbm),
            middle_o=((layers, *own), F32, hbm),
            frows_o=((layers, *rows), BF, hbm),
            gu_o=((layers, seqs, 2, keys, units), BF, hbm),
            stream_o=((layers - 1, *own), F32, hbm),
            gain_o=((2 * layers, width), F32, hbm),
            dy_o=(rows, BF, hbm),
            qz=((layers, *raw), BF, hbm),
            qc=((layers, *raw), BF, hbm),
            kvl=((layers, *raw_k), BF, hbm),
            fc=((layers, *raw_f), BF, hbm),
        ),
        dict(
            stream=(own, F32),
            middle=(own, F32),
            rows=(rows, BF),
            frows=(rows, BF),
            q=((seqs, *q_s), BF),
            kv=((layers, seqs, *kv_s), BF),
            att=((seqs, 4, block, heads * LANES), BF),
            lse=((seqs, 4, 1, heads * block), F32),
            pt=(rows, BF),
            rn=((seqs, 2, block, width), BF),
            far=(own, BF),
            rf=(own, BF),
            gu=((2, keys, units), BF),
            hid=((keys, units), BF),
            k_s=((4, keys, LANES), BF),
            vt_s=((4, LANES, keys), BF),
            m_s=((1, heads * block), F32),
            l_s=((1, heads * block), F32),
            a_s=((LANES, heads * block), F32),
            wa=((layers, size, width), BF),
            wf=((layers, 3, units, width), BF),
            st_q=(raw, BF),
            st_k=(raw_k, BF),
            st_f=(raw_f, BF),
            own=((compact, part), BF),
            tmp=((2 * KEY_VALUE_HEADS * D, part), BF),
            gl=((2, 4, 8, 256), F32),
            gain=((2 * layers, width), F32),
        ),
        sems=(130, 110),
        vmem=63,
    )


class Rows(Net):
    def gather_start(self, v, s, rows):
        rows[s, 0] = v.astype(BF)
        return [
            self.send(rows.at[s, 0], rows.at[s, 2], CTX, 2),
            self.send(rows.at[s, 0], rows.at[s, 1], CTX, 1),
        ]

    def gather_on(self, copies, s, rows):
        copies[0].wait_recv()
        copies.append(self.send(rows.at[s, 2], rows.at[s, 3], CTX, 1))

    def gather_end(self, copies):
        copies[1].wait_recv()
        copies[2].wait_recv()
        self.close(copies)

    def reduce_start(self, s):
        pt, rn = self.r.pt, self.r.rn
        return [
            self.send(pt.at[s, 3], rn.at[s, 1], CTX, 1),
            self.send(pt.at[s, 1], rn.at[s, 0], CTX, 1),
        ]

    def reduce_on(self, copies, s):
        r = self.r
        copies[0].wait_recv()
        r.far[s] = (r.pt[s, 2].astype(F32) + r.rn[s, 1].astype(F32)).astype(BF)
        copies.append(self.send(r.far.at[s], r.rf.at[s], CTX, 2))

    def reduce_end(self, copies, s):
        r = self.r
        copies[1].wait_recv()
        copies[2].wait_recv()
        total = r.pt[s, 0].astype(F32) + r.rn[s, 0].astype(F32) + r.rf[s].astype(F32)
        self.close(copies)
        return total

    def norm_back(self, s, copies, gain, row):
        r = self.r
        local, v = self.reduce_end(copies, s), r.base[s]
        scale = lax.rsqrt(jnp.mean(v * v, axis=-1, keepdims=True) + EPS)
        u = v * scale
        e = local * gain
        r.grad[s] = r.grad[s] + scale * (e - u * jnp.mean(e * u, axis=-1, keepdims=True))
        r.gs_o[row : row + 1] += jnp.sum(local * u, axis=0, keepdims=True)

    def sum_tp(self, parts, lands):
        outer = jnp.logical_not(self.inner)
        one = self.make(parts[1], lands[0], TP, 1)
        two = self.make(parts[2], lands[1], TP, 2)
        hand = self.make(parts[3], lands[2], TP, 1)
        mid = self.make(parts[3], lands[3], TP, 3)

        @pl.when(outer)
        def _():
            hand.start()
            two.start()

        @pl.when(self.inner)
        def _():
            mid.start()
            one.start()

        return one, two, hand, mid

    def sum_tp_on(self, copies, part, land):
        one, two, hand, _ = copies
        pl.when(jnp.logical_not(self.inner))(one.start)

        @pl.when(self.inner)
        def _():
            hand.wait_recv()
            part[...] = (part[...].astype(F32) + land[...].astype(F32)).astype(BF)
            two.start()

    def sum_tp_end(self, copies, own, lands):
        one, two, hand, mid = copies
        outer = jnp.logical_not(self.inner)
        one.wait_recv()
        two.wait_recv()

        @pl.when(self.inner)
        def _():
            mid.wait_recv()
            mid.wait_send()

        @pl.when(outer)
        def _():
            lands[3][...] = jnp.zeros(lands[3].shape, lands[3].dtype)
            hand.wait_send()

        one.wait_send()
        two.wait_send()
        return (
            own[...].astype(F32)
            + lands[0][...].astype(F32)
            + lands[1][...].astype(F32)
            + lands[3][...].astype(F32)
        )


def ffn_back_body(rows_ref, w_ref, gu_ref, hgu, pt_o, waits, between=None):
    block, width = rows_ref.shape[1], rows_ref.shape[2]
    rows = rows_ref[...].reshape(4 * block, width)
    for at, wide in chunks(w_ref.shape[1]):
        own = slice(at, at + wide)
        dh = nt(rows, w_ref[2, own])
        g = gu_ref[0, :, own].astype(F32)
        u = gu_ref[1, :, own].astype(F32)
        s = 1.0 / (1.0 + jnp.exp(-g))
        hgu[0, :, own] = (g * s * u).astype(BF)
        hgu[1, :, own] = (dh * u * s * (1.0 + g * (1.0 - s))).astype(BF)
        hgu[2, :, own] = (dh * g * s).astype(BF)
    for copy in waits:
        copy.wait()
    if between:
        between()
    for at, wide in chunks(width):
        own = slice(at, at + wide)
        part = (nn(hgu[1], w_ref[0, :, own]) + nn(hgu[2], w_ref[1, :, own])).astype(BF)
        for m in range(4):
            pt_o[m, :, own] = part[m * block : (m + 1) * block]


def weight_grad_body(lefts, rights, cols, out):
    rows = lefts[0].shape[0]
    for at, wide in chunks(lefts[0].shape[1]):
        total = None
        for left, right in zip(lefts, rights):
            term = tn(left[:, at : at + wide], right[:, :, cols].reshape(rows, out.shape[1]))
            total = term if total is None else total + term
        out[at : at + wide] = total.astype(BF)


def attn_back_body(
    heads, c, t, prefix, rows_ref, w_ref, q_ref, kv_ref, att_ref, lse_ref, cos_ref, sin_ref, d_o, dkv_o,
    do_s, de_s, dqt_s, dk_s, dv_s
):
    block = q_ref.shape[2]
    keys = 4 * block
    wide = heads * block
    w_at = (heads + 2) * LANES
    rows = rows_ref[...].reshape(keys, rows_ref.shape[2])
    for at, span in chunks(wide):
        do = nt(rows, w_ref[w_at + at : w_at + at + span]).astype(BF)
        for m in range(4):
            for j in range(span // LANES):
                h = at // LANES + j
                do_s[m, h * block : (h + 1) * block] = do[
                    m * block : (m + 1) * block, j * LANES : (j + 1) * LANES
                ]
    mask = side_mask(c, heads, block)
    for cq in range(4):
        m = xor(c, cq)
        for h in range(heads):
            own = slice(h * block, (h + 1) * block)
            prod = att_ref[m, :, h * LANES : (h + 1) * LANES].astype(F32) * do_s[m, own].astype(F32)
            de_s[cq, :, own] = jnp.sum(jnp.transpose(prod), axis=0, keepdims=True)
    dqt_s[...] = jnp.zeros_like(dqt_s)
    q_at = lax.broadcasted_iota(jnp.int32, (1, wide), 1) % block + t * block
    for ck in range(4):
        mk = xor(c, ck)
        k = jnp.concatenate([kv_ref[i, mk, :, :LANES] for i in range(4)], axis=0)
        v = jnp.concatenate([kv_ref[i, mk, :, LANES:] for i in range(4)], axis=0)
        kt = jnp.transpose(k.astype(F32)).astype(BF)
        dk_s[...] = jnp.zeros_like(dk_s)
        dv_s[...] = jnp.zeros_like(dv_s)
        for cq in range(4):
            if ck > cq and ck * keys >= PREFIX_MAX:
                continue
            m = xor(c, cq)
            q_all = q_ref[m].reshape(wide, LANES)
            for first, span in chunks(wide, 3 * LANES):
                own = slice(first, first + span)
                q, d_out = q_all[own], do_s[m, own]
                p = jnp.exp(nt(k, q) - lse_ref[cq, :, own])
                if ck >= cq:
                    at = key_positions(t, block, ck * keys, keys)
                    seen = (at <= q_at[:, own] + cq * keys) | (at < prefix)
                    p = jnp.where(seen, p, 0.0)
                ds = (p * (nt(v, d_out) - de_s[cq, :, own])).astype(BF)
                dk_s[...] += nn(ds, q)
                dv_s[...] += nn(p.astype(BF), d_out)
                dqt_s[cq, :, own] += nn(kt, ds)
        for i in range(4):
            dkv_o[i, mk, :, :LANES] = dk_s[i * block : (i + 1) * block].astype(BF)
            dkv_o[i, mk, :, LANES:] = dv_s[i * block : (i + 1) * block].astype(BF)
    for cq in range(4):
        m = xor(c, cq)
        dq = jnp.transpose(dqt_s[cq]) * 0.125
        turned = half_turn(dq)
        cos, sin = cos_ref[m], sin_ref[m]
        for h in range(heads):
            own = slice(h * block, (h + 1) * block)
            back = dq[own] * cos - turned[own] * sin
            d_o[m, :, h * LANES : (h + 1) * LANES] = jnp.where(mask[own], back, 0.0).astype(BF)


def proj_back_body(heads, total, w_ref, cos_ref, sin_ref, d_o, pt_o):
    block = d_o.shape[1]
    low = heads * LANES
    for m in range(4):
        dk = total[m, :, :LANES]
        dk = dk * cos_ref[m] - half_turn(dk) * sin_ref[m]
        d_o[m, :, low : low + LANES] = dk.astype(BF)
        d_o[m, :, low + LANES :] = total[m, :, LANES:].astype(BF)
    full = d_o[...].reshape(4 * block, low + 2 * LANES)
    for at, span in chunks(w_ref.shape[1]):
        own = slice(at, at + span)
        part = nn(full, w_ref[: low + 2 * LANES, own]).astype(BF)
        for m in range(4):
            pt_o[m, :, own] = part[m * block : (m + 1) * block]


def ffn_sums(net, cfg):
    layers, seqs, block, width, heads, units, share = cfg
    quarter = units // 4
    r, c = net.r, net.c
    parts = [[r.fs.at[i, m * quarter : (m + 1) * quarter] for m in range(4)] for i in range(3)]
    lands = [[r.fz.at[k, i] for k in range(4)] for i in range(3)]
    loads, sends = {}, {}

    def start():
        for i in (2, 0, 1):
            loads[i] = [net.local(r.dwk.at[i], r.fs.at[i])]
        loads[2].append(net.local(r.dwx, r.fx.at[2]))
        for i in (0, 1):
            sends[i] = net.send(r.dws.at[i], r.fx.at[i], DP)
        yield

    def one(i):
        for copy in loads[i]:
            copy.wait()
        if i in sends:
            sends[i].wait_recv()
        for m in (3, 2, 1, 0):
            own = slice(m * quarter, (m + 1) * quarter)
            r.fs[i, own] = (r.fs[i, own].astype(F32) + r.fx[i, own].astype(F32)).astype(BF)
        sums = net.sum_tp(parts[i], lands[i])
        yield
        net.sum_tp_on(sums, parts[i][2], lands[i][2])
        yield
        total = net.sum_tp_end(sums, parts[i][0], lands[i])
        r.fo[i * quarter : (i + 1) * quarter] = total.astype(BF)
        yield

    def piece(i):
        return r.ft.at[pl.ds(pl.multiple_of(i * share, 32), share)]

    def end():
        for at in range(0, 4 * share, LANES):
            r.ft[at : at + LANES] = jnp.transpose(r.fo[:, at : at + LANES].astype(F32)).astype(BF)
        out = [net.send(piece(xor(c, m)), r.fg.at[c], CTX, m) for m in (1, 2, 3)]
        r.fg[c] = r.ft[pl.ds(pl.multiple_of(c * share, 32), share)]
        yield
        for copy in out:
            copy.wait_recv()
        for i, o in enumerate((r.g_o, r.u_o, r.d_o)):
            own = slice(i * quarter, (i + 1) * quarter)
            o[...] = jnp.concatenate([r.fg[k, :, own].astype(F32) for k in range(4)], axis=1)
        net.close(out + list(sends.values()))
        yield

    return start(), one(2), one(0), one(1), end()


def finish_attn(net, cfg, mine, other, waits):
    layers, seqs, block, width, heads, units, share = cfg
    r = net.r
    c, t = net.c, net.t
    wide = 2 * heads * D
    for copy in waits:
        copy.wait()
    for at in range(0, 4 * share, LANES):
        own = slice(at, at + LANES)
        total = mine[:, own].astype(F32) + other[:, own].astype(F32)
        r.at[own] = jnp.transpose(total).astype(BF)

    def piece(i):
        return r.at.at[pl.ds(pl.multiple_of(i * share, 32), share)]

    out = [net.send(piece(xor(c, m)), r.ac.at[c], CTX, m) for m in (1, 2, 3)]
    own = net.local(piece(c), r.ac.at[c])
    yield
    for copy in out:
        copy.wait_recv()
    own.wait()
    net.close(out)
    for m in range(4):
        r.aq[m] = r.ac[xor(t, m), :, :wide]
    parts = [r.aq.at[m] for m in range(4)]
    lands = [r.az.at[k] for k in range(4)]
    sums = net.sum_tp(parts, lands)
    for first, at in ((0, wide), (KEY_VALUE_HEADS * D, wide + LANES)):
        terms = []
        for h in range(KEY_VALUE_HEADS):
            total = None
            for i in range(4):
                j = h - i * heads // GROUP
                if j in (0, 1):
                    term = r.ac[i, :, at + j * D : at + (j + 1) * D].astype(F32)
                    total = term if total is None else total + term
            terms.append(total)
        r.av[:, first : first + KEY_VALUE_HEADS * D] = jnp.concatenate(terms, axis=1)
    r.asum[...] = r.av[...].astype(BF)
    kv = [net.send(r.asum, r.al.at[m - 1], TP, m) for m in (1, 2, 3)]
    yield
    net.sum_tp_on(sums, parts[2], lands[2])
    yield
    r.qo_o[...] = net.sum_tp_end(sums, parts[0], lands)
    for copy in kv:
        copy.wait_recv()
    r.kv_o[...] = r.av[...] + r.al[0].astype(F32) + r.al[1].astype(F32) + r.al[2].astype(F32)
    net.close(kv)
    yield


def finish_gains(net):
    r = net.r
    r.gt[...] = r.gs_o[...]
    for k, axis in enumerate((CTX, TP, DP)):
        ms = (1, 2, 3) if axis != DP else (1,)
        copies = [net.send(r.gt, r.gr.at[k, m - 1], axis, m) for m in ms]
        yield
        for copy in copies:
            copy.wait_recv()
        net.close(copies)
        total = r.gt[...]
        for m in ms:
            total = total + r.gr[k, m - 1]
        r.gt[...] = total
    r.gs_o[...] = r.gt[...]
    yield


def ffn_back_kernel2(cfg, l, tail, r):
    layers, seqs, block, width, heads, units, share = cfg
    net = Rows(r)
    part = 4 * share
    keep = pl.ds(pl.multiple_of(net.x * part, LANES), part)
    away = pl.ds(pl.multiple_of((1 - net.x) * part, LANES), part)
    net.barrier()
    first = [net.local(r.dy_i.at[0], r.dy.at[0]), net.local(r.wf_i.at[l, 2], r.wf.at[2])]
    first.append(net.local(r.gu_i.at[l, 0], r.gu.at[0]))
    second = [net.local(r.wf_i.at[l, i], r.wf.at[i]) for i in (0, 1)]
    later = [net.local(r.dy_i.at[s], r.dy.at[s]) for s in range(1, seqs)]
    later += [net.local(r.gu_i.at[l, s], r.gu.at[s]) for s in range(1, seqs)]
    state = [net.local(r.grad_i, r.grad), net.local(r.base_i.at[l], r.base)]
    state += [net.local(r.frows_i.at[l, s], r.frows.at[s]) for s in range(seqs)]
    r.gs_o[...] = r.gs_i[...]
    row = layers + l
    gain = r.gain[row : row + 1]
    saved, busy = [], {}

    def sequence(s, waits, more):
        rows, hgu, pt = r.dy.at[s], r.hgu.at[s], r.pt.at[s]
        for copy in waits:
            copy.wait()
        ffn_back_body(rows, r.wf, r.gu.at[s], hgu, pt, more)
        red = net.reduce_start(s)
        yield
        net.reduce_on(red, s)
        yield
        while state:
            state.pop().wait()
        net.norm_back(s, red, gain, row)
        gather = net.gather_start(r.grad[s], s, r.dn)
        saved.append(net.local(r.grad.at[s], r.grad_o.at[s]))
        yield
        net.gather_on(gather, s, r.dn)
        yield
        net.gather_end(gather)
        saved.append(net.local(r.dn.at[s], r.dn_o.at[s]))
        yield

    def weights(i, to):
        lefts = [r.hgu.at[s, i] for s in range(seqs)]
        rights = [(r.frows if i else r.dy).at[s] for s in range(seqs)]
        while state:
            state.pop().wait()
        if i:
            if 0 in busy:
                busy.pop(0).wait()
            weight_grad_body(lefts, rights, away, r.ws.at[0])
            busy[0] = net.local(r.ws.at[0], r.dws_o.at[to])
        else:
            weight_grad_body(lefts, rights, away, r.wx)
            cross = net.send(r.wx, r.dwx_o, DP)
        yield
        if 1 in busy:
            busy.pop(1).wait()
        weight_grad_body(lefts, rights, keep, r.ws.at[1])
        busy[1] = net.local(r.ws.at[1], r.dwk_o.at[to])
        yield
        if not i:
            cross.wait()
        yield

    a, b = sequence(0, first, second), sequence(1, later, [])
    w0, w1, w2 = weights(0, 2), weights(1, 0), weights(2, 1)
    if tail:
        loads = [net.local(r.dak, r.ak), net.local(r.dax, r.ax)]
        fa = finish_attn(net, cfg, r.ak, r.ax, loads)
        run((fa, a, b, a, w0, b, fa, w1, w1, w0, a, b, fa, w2, w2, a, fa, w0, b, a, b))
    else:
        run((a, b, a, w0, b, w1, w1, a, w2, w2, w0, b, a, a, b, w0, b))
    for copy in saved + list(busy.values()):
        copy.wait()


def attn_back_kernel2(cfg, l, r):
    layers, seqs, block, width, heads, units, share = cfg
    net = Rows(r)
    c, t = net.c, net.t
    part = 4 * share
    keep = pl.ds(pl.multiple_of(net.x * part, LANES), part)
    away = pl.ds(pl.multiple_of((1 - net.x) * part, LANES), part)
    net.barrier()
    loads = []
    for s in range(seqs):
        loads.append([net.local(r.dy_i.at[s], r.dy.at[s])])
        if s == 0:
            loads[0].append(net.local(r.wa_i.at[l], r.wa))
        for src, dst in ((r.q_i, r.q), (r.kv_i, r.kv), (r.att_i, r.att), (r.lse_i, r.lse)):
            loads[s].append(net.local(src.at[l, s], dst.at[s]))
    x, f0, f1, f2, g = ffn_sums(net, cfg)
    run((x,))
    state = [net.local(r.grad_i, r.grad), net.local(r.base_i.at[l - 1] if l else r.base_i, r.base)]
    state += [net.local(r.rows_i.at[l, s], r.rows.at[s]) for s in range(seqs)]
    r.gs_o[...] = r.gs_i[...]
    gain = r.gain[l : l + 1]
    saved = []

    def sequence(s):
        for copy in loads[s]:
            copy.wait()
        attn_back_body(
            heads, c, t, r.prefix[s], r.dy.at[s], r.wa, r.q.at[s], r.kv.at[s], r.att.at[s],
            r.lse.at[s], r.cos, r.sin, r.dqkv.at[s], r.dkv.at[s], r.do_s, r.de_s, r.dqt_s, r.dk_s, r.dv_s,
        )
        lands = [r.dz.at[k, s] for k in range(4)]
        sums = net.sum_tp([r.dkv.at[s, m] for m in range(4)], lands)
        yield
        net.sum_tp_on(sums, r.dkv.at[s, 2], lands[2])
        yield
        r.dt[...] = net.sum_tp_end(sums, r.dkv.at[s, 0], lands)
        proj_back_body(heads, r.dt, r.wa, r.cos, r.sin, r.dqkv.at[s], r.pt.at[s])
        red = net.reduce_start(s)
        yield
        net.reduce_on(red, s)
        yield
        while state:
            state.pop().wait()
        net.norm_back(s, red, gain, l)
        saved.append(net.local(r.grad.at[s], r.grad_o.at[s]))
        if l:
            gather = net.gather_start(r.grad[s], s, r.dn)
        yield
        if l:
            net.gather_on(gather, s, r.dn)
            yield
            net.gather_end(gather)
            saved.append(net.local(r.dn.at[s], r.dn_o.at[s]))
            yield

    def weights(lefts, rights, cols, out, at):
        while state:
            state.pop().wait()
        low = lax.div(c * heads, GROUP)
        lf = [lefts.at[s] for s in range(seqs)]
        rg = [rights.at[s] for s in range(seqs)]
        for a, wide in chunks(lf[0].shape[-1]):
            total = None
            for left, right in zip(lf, rg):
                term = tn(
                    left[:, :, a : a + wide].reshape(4 * block, wide),
                    right[:, :, cols].reshape(4 * block, part),
                )
                total = term if total is None else total + term
            r.ws[a : a + wide] = total.astype(BF)
        for h in range(heads):
            side = (lax.div(c * heads + h, GROUP) - low) * D
            out[at + h * D : at + (h + 1) * D] = r.ws[pl.ds(pl.multiple_of(h * LANES + side, D), D)]
        if at == 0:
            out[2 * heads * D :] = r.ws[heads * LANES : (heads + 2) * LANES]

    def out_weights():
        weights(r.att, r.dy, away, r.wo.at[0], heads * D)
        yield
        weights(r.att, r.dy, keep, r.wo.at[1], heads * D)
        yield

    cross = []

    def qkv_weights():
        weights(r.dqkv, r.rows, away, r.wo.at[0], 0)
        yield
        cross.append(net.send(r.wo.at[0], r.dax_o if l else r.ax, DP))
        yield
        weights(r.dqkv, r.rows, keep, r.wo.at[1], 0)
        if l:
            saved.append(net.local(r.wo.at[1], r.dak_o))
        yield

    a, b, wo, wq = sequence(0), sequence(1), out_weights(), qkv_weights()
    if l:
        run((f0, a, f0, b, wo, a, b, a, f1, b, wo, f2, a, f0, wq, b, wq, f1, a, f2, b, b, f1, f2, g, b, wq, a, a, g))
        cross[0].wait()
    else:
        gn = finish_gains(net)
        run((f0, a, b, a, b, f1, wo, wo, a, b, wq, wq, b, f2, b, f0, a, f1, f2, a, gn, wq))
        fa = finish_attn(net, cfg, r.wo.at[1], r.ax, cross)
        run((fa, f0, gn, gn, gn, f2, f1, fa, g, fa, g, fa))
    for copy in saved:
        copy.wait()


def backward_pass(cfg, tokens, prefix, cotangent, cos4, sin4, f):
    layers, seqs, block, width, heads, units, share = cfg
    keys, part = 4 * block, 4 * share
    rows = (seqs, 4, block, width)
    size = 2 * (heads + 1) * LANES
    compact = 2 * heads * D + 2 * LANES
    own = (seqs, block, width)
    hbm, vm = pl.ANY, pltpu.VMEM
    grads = ((8, width), F32, vm)
    common = dict(
        pt=(rows, BF), rn=((seqs, 2, block, width), BF), far=(own, BF), rf=(own, BF),
        grad=(own, F32), base=(own, F32), dy=(rows, BF),
    )
    kvs = (share, 2 * KEY_VALUE_HEADS * D)
    qos = (share, 2 * heads * D)
    finish_out = dict(qo_o=(qos, F32, vm), kv_o=(kvs, F32, vm))
    finish_scratch = dict(
        ax=((compact, part), BF), at=((part, compact), BF),
        ac=((4, share, compact), BF), aq=((4, *qos), BF), az=((4, *qos), BF),
        av=(kvs, F32), asum=(kvs, BF), al=((3, *kvs), BF),
    )
    grad, dy = cotangent.astype(F32), f.dy_o
    sums = jnp.zeros((8, width), F32)
    units_of, heads_of = [None] * layers, [None] * layers
    number = 1
    d, finish_in = None, {}
    for l in reversed(range(layers)):
        tail = d is not None
        more = (finish_in, finish_out, finish_scratch) if tail else ({}, {}, {})
        c = launch(
            functools.partial(ffn_back_kernel2, cfg, l, tail),
            number,
            dict(
                dy_i=(dy, hbm), grad_i=(grad, hbm), base_i=(f.middle_o, hbm), gain=(f.gain_o, vm), wf_i=(f.wf_o, hbm),
                frows_i=(f.frows_o, hbm), gu_i=(f.gu_o, hbm), gs_i=(sums, vm), **more[0],
            ),
            dict(
                gs_o=grads, grad_o=(own, F32, hbm), dn_o=(rows, BF, hbm), dwk_o=((3, units, part), BF, hbm),
                dws_o=((2, units, part), BF, hbm), dwx_o=((units, part), BF, hbm), **more[1],
            ),
            dict(
                wf=((3, units, width), BF), frows=(rows, BF), gu=((seqs, 2, keys, units), BF), dn=(rows, BF),
                hgu=((seqs, 3, keys, units), BF), ws=((2, units, part), BF), wx=((units, part), BF),
                **(dict(ak=((compact, part), BF)) if tail else {}), **common, **more[2],
            ),
        )
        if tail:
            heads_of[l + 1] = c
        base = f.stream_o if l else tokens.astype(F32)
        d = launch(
            functools.partial(attn_back_kernel2, cfg, l),
            number + 1,
            dict(
                prefix=(prefix, pltpu.SMEM), dy_i=(c.dn_o, hbm), grad_i=(c.grad_o, hbm), base_i=(base, hbm),
                gain=(f.gain_o, vm), wa_i=(f.wa_o, hbm), rows_i=(f.rows_o, hbm), q_i=(f.q_o, hbm), kv_i=(f.kv_o, hbm),
                att_i=(f.att_o, hbm), lse_i=(f.lse_o, hbm), cos=(cos4, vm), sin=(sin4, vm), gs_i=(c.gs_o, vm),
                dwk=(c.dwk_o, hbm), dws=(c.dws_o, hbm), dwx=(c.dwx_o, hbm),
            ),
            dict(
                gs_o=grads, grad_o=(own, F32, hbm),
                g_o=((share, units), F32, vm), u_o=((share, units), F32, vm), d_o=((share, units), F32, vm),
                **(dict(dn_o=(rows, BF, hbm), dak_o=((compact, part), BF, hbm), dax_o=((compact, part), BF, hbm)) if l else finish_out),
            ),
            dict(
                wa=((size, width), BF), q=((seqs, 4, heads, block, LANES), BF), kv=((seqs, 4, 4, block, 2 * LANES), BF),
                att=((seqs, 4, block, heads * LANES), BF), lse=((seqs, 4, 1, heads * block), F32), rows=(rows, BF),
                dqkv=((seqs, 4, block, (heads + 2) * LANES), BF), dkv=((seqs, 4, 4, block, 2 * LANES), BF),
                do_s=((4, heads * block, LANES), BF), de_s=((4, 1, heads * block), F32),
                dqt_s=((4, LANES, heads * block), F32), dk_s=((keys, LANES), F32), dv_s=((keys, LANES), F32),
                dz=((4, seqs, 4, block, 2 * LANES), BF), dt=((4, block, 2 * LANES), F32),
                ws=(((heads + 2) * LANES, part), BF), wo=((2, compact, part), BF),
                fs=((3, units, part), BF), fx=((3, units, part), BF), fz=((4, 3, units // 4, part), BF),
                fo=((3 * units // 4, part), BF), ft=((part, 3 * units // 4), BF), fg=((4, share, 3 * units // 4), BF),
                **(dict(dn=(rows, BF)) if l else dict(gt=((8, width), F32), gr=((3, 3, 8, width), F32), **finish_scratch)), **common,
            ),
            vmem=63,
        )
        number += 2
        units_of[l] = d
        grad, dy, sums = d.grad_o, d.dn_o if l else None, d.gs_o
        if l:
            finish_in = dict(dak=(d.dak_o, hbm), dax=(d.dax_o, hbm))
    heads_of[0] = d
    return grad, units_of, heads_of


def rms(v):
    r = lax.rsqrt(jnp.mean(v * v, axis=-1, keepdims=True) + EPS)
    return v * r, r


def per_device(
    tokens, prefix, w_query, key_weight, value_weight, w_out, w_gate, w_up, w_down, gain_attn, gain_ffn,
    cotangent,
):
    layers = w_query.shape[0]
    seqs, block, width = tokens.shape
    dps = lax.axis_size(DP)
    x, c, t = (lax.axis_index(a) for a in (DP, CTX, TP))
    heads = w_query.shape[2] // D
    share = w_query.shape[1]
    part = 4 * share
    units = w_gate.shape[2]
    quarter = units // 4
    low = (c * heads) // GROUP
    keys = 4 * block
    long = 4 * keys

    half = D // 2
    freq = jnp.exp(-math.log(10000.0) * jnp.arange(half).astype(F32) / half)
    at = ((c ^ jnp.arange(4)) * keys + t * block)[:, None] + jnp.arange(block)[None, :]
    angle = at.astype(F32).reshape(keys, 1) * freq[None, :]
    cos = jnp.tile(jnp.cos(angle), (1, 4))
    sin = jnp.sin(angle)
    sin = jnp.concatenate([-sin, sin, -sin, sin], axis=1)
    cos4, sin4 = cos.reshape(4, block, LANES), sin.reshape(4, block, LANES)
    scalars = [
        jnp.stack([c, t, prefix[s]]).astype(jnp.int32) for s in range(seqs)
    ]

    shards = jnp.stack([gain_attn, gain_ffn])
    gains = None if dps == 2 else lax.all_gather(shards, (DP, CTX), axis=2, tiled=True).astype(F32)

    def spread_dp(own):
        if dps == 2:
            other = lax.ppermute(own, DP, [(0, 1), (1, 0)])
            return jnp.concatenate(
                [jnp.where(x == 0, own, other), jnp.where(x == 0, other, own)], axis=-1
            )
        return lax.all_gather(own, DP, axis=own.ndim - 1, tiled=True)

    def attn_weights(l):
        qo = jnp.concatenate([w_query[l], w_out[l]], axis=1)
        slots = jnp.stack(tp_gather(qo))
        to_ctx = jnp.stack(
            [lax.dynamic_index_in_dim(slots, t ^ i, 0, keepdims=False) for i in range(4)]
        )
        got = ctx_exchange(to_ctx, True).reshape(part, 2 * heads * D).T
        kv = jnp.concatenate([key_weight[l], value_weight[l]], axis=1)
        kv = by_ctx(jnp.stack([kv] + [flip(kv, CTX, m) for m in (1, 2, 3)]))
        kv = kv.reshape(part, 2 * KEY_VALUE_HEADS * D).T
        k = lax.dynamic_slice_in_dim(kv, low * D, 2 * D, 0)
        v = lax.dynamic_slice_in_dim(kv, (KEY_VALUE_HEADS + low) * D, 2 * D, 0)
        own = jnp.concatenate([got[: heads * D], k, v, got[heads * D :]], axis=0)
        full = spread_dp(own)
        return call(
            functools.partial(pad_kernel, heads),
            [scalars[0], full],
            [((2 * (heads + 1) * LANES, width), BF)],
            smem=1,
        )[0]

    def ffn_weights(l):
        raw = jnp.concatenate([w_gate[l], w_up[l], w_down[l]], axis=0).T
        got = ctx_exchange(raw.reshape(4, quarter, 3 * share), True)
        own = jnp.transpose(got.reshape(4, quarter, 3, share), (2, 1, 0, 3)).reshape(
            3, quarter, part
        )
        slots = [spread_dp(s) for s in tp_gather(own)]
        return jnp.concatenate(slots, axis=1)

    if dps == 2:
        cfg = (layers, seqs, block, width, heads, units, share)
        small = jnp.pad(
            shards.astype(F32).reshape(2 * layers, share), ((0, 8 - 2 * layers), (0, 256 - share))
        )
        qo = jnp.concatenate([w_query, w_out], axis=2)
        kvw = jnp.concatenate([key_weight, value_weight], axis=2)
        fp = jnp.concatenate([w_gate, w_up, w_down], axis=1)
        fp = jnp.transpose(fp, (0, 2, 1)).reshape(layers, 4, quarter, 3 * share)
        f = forward_pass(cfg, tokens, cotangent, prefix, small, qo, kvw, fp, cos, sin)
        grad, fd, hd = backward_pass(cfg, tokens, prefix, cotangent, cos4, sin4, f)
        wide = heads * D
        kd = KEY_VALUE_HEADS * D
        qo = jnp.stack([d.qo_o for d in hd])
        kv = jnp.stack([d.kv_o for d in hd])
        sums = lax.dynamic_slice_in_dim(hd[0].gs_o, (x * 4 + c) * share, share, 1)
        return (
            f.out_o, grad, qo[:, :, :wide], kv[:, :, :kd], kv[:, :, kd:], qo[:, :, wide:],
            jnp.stack([d.g_o for d in fd]), jnp.stack([d.u_o for d in fd]), jnp.stack([d.d_o for d in fd]),
            sums[:layers], sums[layers : 2 * layers],
        )
    watt = [None] * layers
    wffn = [None] * layers
    for l in range(layers):
        watt[l] = attn_weights(l)
        wffn[l] = ffn_weights(l)

    stream = [tokens[s].astype(F32) for s in range(seqs)]
    kept = {}
    for l in range(layers):
        for s in range(seqs):
            u, _ = rms(stream[s])
            pieces = ctx_gather((u * gains[0, l]).astype(BF))
            rows, q, kv = call(
                functools.partial(qkv_kernel, heads),
                [scalars[s], *pieces, watt[l], cos, sin],
                [((4, block, width), BF), ((4, heads, block, LANES), BF), ((4, block, 2 * LANES), BF)],
                smem=1,
                flops=2 * keys * width * (heads + 2) * LANES,
            )
            kvs = tp_gather(kv)
            att, lse, *parts = call(
                functools.partial(attn_kernel, heads),
                [scalars[s], q, *kvs, watt[l]],
                [((4, block, heads * LANES), BF), ((4, 1, heads * block), F32)] + [((block, width), BF)] * 4,
                smem=1,
                scratch=[
                    pltpu.VMEM((4, keys, LANES), BF),
                    pltpu.VMEM((4, LANES, keys), BF),
                    pltpu.VMEM((1, heads * block), F32),
                    pltpu.VMEM((1, heads * block), F32),
                    pltpu.VMEM((LANES, heads * block), F32),
                ],
                flops=2 * 2 * keys * long * heads * 256 * 0.7 + 2 * keys * heads * LANES * width,
                exps=keys * long * heads,
            )
            middle = stream[s] + ctx_reduce(parts)
            u, _ = rms(middle)
            pieces = ctx_gather((u * gains[1, l]).astype(BF))
            frows, gate, up, *parts = call(
                ffn_kernel,
                [*pieces, wffn[l]],
                [((4, block, width), BF)] + [((keys, units), BF)] * 2 + [((block, width), BF)] * 4,
                scratch=[pltpu.VMEM((keys, width), F32)],
                flops=2 * keys * width * units * 3,
            )
            kept[l, s] = (stream[s], rows, q, kvs, att, lse, middle, frows, gate, up)
            stream[s] = middle + ctx_reduce(parts)

    output = jnp.stack(stream).astype(BF)

    def norm_back(grad, local, v, gain):
        u, r = rms(v)
        e = local * gain
        grad = grad + r * (e - u * jnp.mean(e * u, axis=-1, keepdims=True))
        return grad, jnp.sum(local * u, axis=0)

    def weight_grad(lefts, rights):
        n = len(lefts)
        u_count = lefts[0].shape[-1]
        return call(
            functools.partial(weight_grad_kernel, dps if dps == 2 else 1, n),
            [a.reshape(keys, u_count) for a in lefts] + list(rights),
            [((u_count, width // dps), BF)] * 2 if dps == 2 else [((u_count, width), BF)],
            flops=2 * n * keys * u_count * width,
        )

    def collect_dp(halves):
        if dps == 2:
            mine = jnp.where(x == 0, halves[0], halves[1])
            other = jnp.where(x == 0, halves[1], halves[0])
            got = lax.ppermute(other, DP, [(0, 1), (1, 0)])
            return mine.astype(F32) + got.astype(F32)
        return lax.psum_scatter(
            halves[0], DP, scatter_dimension=halves[0].ndim - 1, tiled=True
        ).astype(F32)

    grads = {}

    def ffn_grads(l, lefts_rights):
        sums = [collect_dp(weight_grad(a, b)).reshape(4, quarter, part) for a, b in lefts_rights]
        slots = [jnp.stack([s[i] for s in sums]).astype(BF) for i in range(4)]
        own = tp_reduce(slots).reshape(3 * quarter, part).astype(BF)
        got = ctx_exchange(own.T.reshape(4, share, 3 * quarter), False).astype(F32)
        got = jnp.transpose(got.reshape(4, share, 3, quarter), (2, 1, 0, 3)).reshape(3, share, units)
        grads[l, "g"], grads[l, "u"], grads[l, "d"] = got[0], got[1], got[2]

    def attn_grads(l, dqkv, rows, att, drows):
        a = weight_grad(dqkv, rows)
        b = weight_grad(att, drows)
        halves = [
            call(
                functools.partial(unpad_kernel, heads),
                [scalars[0], i, j],
                [((2 * heads * D + 2 * LANES, i.shape[1]), BF)],
                smem=1,
            )[0]
            for i, j in zip(a, b)
        ]
        own = collect_dp(halves).astype(BF).T.reshape(4, share, 2 * heads * D + 2 * LANES)
        got = ctx_exchange(own, False)
        lo, hi = heads * D, heads * D + 2 * LANES
        qo = jnp.concatenate([got[:, :, :lo], got[:, :, hi:]], axis=-1)
        qo = [lax.dynamic_index_in_dim(qo, t ^ i, 0, keepdims=False) for i in range(4)]
        qo = tp_reduce(qo)
        grads[l, "q"], grads[l, "o"] = qo[:, :lo], qo[:, lo:]
        kv = got[:, :, lo:hi].astype(F32)
        both = []
        for first in (0, LANES):
            total = jnp.zeros((share, KEY_VALUE_HEADS * D), F32)
            for i in range(4):
                h = i * heads // GROUP
                term = kv[i, :, first : first + LANES]
                total = total + jnp.pad(term, ((0, 0), (h * D, (KEY_VALUE_HEADS - 2 - h) * D)))
            both.append(total)
        both = jnp.concatenate(both, axis=1)
        sent = both.astype(BF)
        for m in (1, 2, 3):
            both = both + flip(sent, TP, m).astype(F32)
        grads[l, "k"], grads[l, "v"] = (
            both[:, : KEY_VALUE_HEADS * D],
            both[:, KEY_VALUE_HEADS * D :],
        )

    grad = [cotangent[s].astype(F32) for s in range(seqs)]
    gain_sums = {}
    for l in reversed(range(layers)):
        hidden, dgate, dup, dy = [], [], [], []
        gain_sums[1, l] = 0.0
        gain_sums[0, l] = 0.0
        for s in range(seqs):
            _, _, _, _, _, _, middle, frows, gate, up = kept[l, s]
            drows, dg, du, hid, *parts = call(
                ffn_back_kernel,
                [*ctx_gather(grad[s].astype(BF)), wffn[l], gate, up],
                [((4, block, width), BF)] + [((keys, units), BF)] * 3 + [((block, width), BF)] * 4,
                scratch=[pltpu.VMEM((keys, width), F32)],
                flops=2 * keys * width * units * 3,
            )
            hidden.append(hid), dgate.append(dg), dup.append(du), dy.append(drows)
            grad[s], extra = norm_back(grad[s], ctx_reduce(parts), middle, gains[1, l])
            gain_sums[1, l] += extra
        ffn_grads(
            l,
            [
                (dgate, [kept[l, s][7] for s in range(seqs)]),
                (dup, [kept[l, s][7] for s in range(seqs)]),
                (hidden, dy),
            ],
        )
        dqkvs, dys = [], []
        for s in range(seqs):
            start, rows, q, kvs, att, lse, *_ = kept[l, s]
            drows, dq, *dkv = call(
                functools.partial(attn_back_kernel, heads),
                [scalars[s], *ctx_gather(grad[s].astype(BF)), watt[l], q, *kvs, att, lse, cos4, sin4],
                [((4, block, width), BF), ((4, block, heads * LANES), BF)] + [((4, block, 2 * LANES), BF)] * 4,
                smem=1,
                scratch=[
                    pltpu.VMEM((4, heads * block, LANES), BF),
                    pltpu.VMEM((4, 1, heads * block), F32),
                    pltpu.VMEM((4, LANES, heads * block), F32),
                    pltpu.VMEM((keys, LANES), F32),
                    pltpu.VMEM((keys, LANES), F32),
                ],
                flops=2 * 5 * keys * long * heads * 256 * 0.7 + 2 * keys * heads * LANES * width,
                exps=keys * long * heads,
            )
            one = flip(dkv[1], TP, 1)
            handed = lax.ppermute(dkv[3], TP, [(0, 1), (3, 2)])
            mid = lax.ppermute(dkv[3], TP, [(1, 2), (2, 1)])
            two = flip((dkv[2].astype(F32) + handed.astype(F32)).astype(BF), TP, 2)
            dqkv, *parts = call(
                functools.partial(proj_back_kernel, heads),
                [dkv[0], one, two, mid, dq, watt[l], cos4, sin4],
                [((4, block, (heads + 2) * LANES), BF)] + [((block, width), BF)] * 4,
                flops=2 * keys * (heads + 2) * LANES * width,
            )
            dqkvs.append(dqkv), dys.append(drows)
            grad[s], extra = norm_back(grad[s], ctx_reduce(parts), start, gains[0, l])
            gain_sums[0, l] += extra
        attn_grads(
            l,
            dqkvs,
            [kept[l, s][1] for s in range(seqs)],
            [kept[l, s][4] for s in range(seqs)],
            dys,
        )

    sums = jnp.stack([gain_sums[k, l] for k in range(2) for l in range(layers)])
    sums = lax.psum(sums, (DP, CTX, TP))
    sums = lax.dynamic_slice_in_dim(sums, (x * 4 + c) * share, share, 1).reshape(2, layers, share)

    def stacked(name):
        return jnp.stack([grads[l, name] for l in range(layers)])

    return (
        output,
        jnp.stack(grad),
        stacked("q"),
        stacked("k"),
        stacked("v"),
        stacked("o"),
        stacked("g"),
        stacked("u"),
        stacked("d"),
        sums[0],
        sums[1],
    )


def solution(mesh):
    rows = P(DP, (CTX, TP), None)
    sharded = P(None, (DP, CTX), TP)
    heads = P(None, (DP, CTX), None)
    gains = P(None, (DP, CTX))
    in_specs = (rows, P(DP), sharded, heads, heads, sharded, sharded, sharded, sharded, gains, gains, rows)
    out_specs = (rows, rows, sharded, heads, heads, sharded, sharded, sharded, sharded, gains, gains)
    return jax.shard_map(
        per_device, mesh=mesh, in_specs=in_specs, out_specs=out_specs, check_vma=False
    )
```

```python
import functools
import math
import types

import jax
import jax.numpy as jnp
from jax import lax
from jax.experimental import pallas as pl
from jax.experimental.pallas import tpu as pltpu
from jax.sharding import PartitionSpec as P

QUERY_HEADS = 20
KEY_VALUE_HEADS = 5
D = 64
GROUP = QUERY_HEADS // KEY_VALUE_HEADS
EPS = 1e-05
MASKED = -1e30
BF = jnp.bfloat16
F32 = jnp.float32
SLOTS = 4
LANES = 128
DP, CTX, TP = "dp", "ctx", "tp"
PREFIX_MAX = 1024


def nt(a, b):
    return lax.dot_general(a, b, (((1,), (1,)), ((), ())), preferred_element_type=F32)


def nn(a, b):
    return lax.dot_general(a, b, (((1,), (0,)), ((), ())), preferred_element_type=F32)


def tn(a, b):
    return lax.dot_general(a, b, (((0,), (0,)), ((), ())), preferred_element_type=F32)


def half_turn(x):
    lane = lax.broadcasted_iota(jnp.int32, x.shape, 1)
    return jnp.where((lane & 32) == 0, pltpu.roll(x, LANES - 32, 1), pltpu.roll(x, 32, 1))


def call(kernel, ins, outs, smem=0, scratch=(), flops=0, exps=0, vmem=56):
    total = sum(math.prod(a.shape) * a.dtype.itemsize for a in ins) + sum(
        math.prod(s) * jnp.dtype(d).itemsize for s, d in outs
    )
    return pl.pallas_call(
        kernel,
        out_shape=[jax.ShapeDtypeStruct(s, d) for s, d in outs],
        in_specs=[pl.BlockSpec(memory_space=pltpu.SMEM)] * smem
        + [pl.BlockSpec(memory_space=pltpu.VMEM)] * (len(ins) - smem),
        out_specs=[pl.BlockSpec(memory_space=pltpu.VMEM)] * len(outs),
        scratch_shapes=list(scratch),
        compiler_params=pltpu.CompilerParams(vmem_limit_bytes=vmem * 2**20),
        cost_estimate=pl.CostEstimate(
            flops=int(flops), bytes_accessed=int(total), transcendentals=int(exps)
        ),
    )(*ins)


def flip(x, axis, m):
    return lax.ppermute(x, axis, [(i, i ^ m) for i in range(4)])


def ctx_gather(x):
    far = flip(x, CTX, 2)
    return [x, flip(x, CTX, 1), far, flip(far, CTX, 1)]


def ctx_reduce(parts):
    far = (parts[2].astype(F32) + flip(parts[3], CTX, 1).astype(F32)).astype(BF)
    near = flip(parts[1], CTX, 1)
    return parts[0].astype(F32) + near.astype(F32) + flip(far, CTX, 2).astype(F32)


def inner(t):
    return (t == 1) | (t == 2)


def tp_gather(x):
    t = lax.axis_index(TP)
    two = flip(x, TP, 2)
    mid = lax.ppermute(x, TP, [(1, 2), (2, 1)])
    end = lax.ppermute(two, TP, [(1, 0), (2, 3)])
    return [x, flip(x, TP, 1), two, jnp.where(inner(t), mid, end)]


def tp_reduce(parts):
    one = flip(parts[1], TP, 1)
    handed = lax.ppermute(parts[3], TP, [(0, 1), (3, 2)])
    mid = lax.ppermute(parts[3], TP, [(1, 2), (2, 1)])
    two = flip((parts[2].astype(F32) + handed.astype(F32)).astype(BF), TP, 2)
    return (
        parts[0].astype(F32) + one.astype(F32) + two.astype(F32) + mid.astype(F32)
    )


def ctx_exchange(stacked, own_first):
    c = lax.axis_index(CTX)
    got = []
    for m in range(4):
        piece = lax.dynamic_index_in_dim(stacked, c ^ m, 0, keepdims=False)
        got.append(piece if m == 0 else flip(piece, CTX, m))
    return by_ctx(jnp.stack(got))


def by_ctx(stacked):
    c = lax.axis_index(CTX)
    return jnp.stack(
        [lax.dynamic_index_in_dim(stacked, c ^ i, 0, keepdims=False) for i in range(4)]
    )


def head_side(c, heads, h):
    return (c * heads + h) // GROUP - (c * heads) // GROUP


def qkv_kernel(heads, s_ref, x0, x1, x2, x3, w_ref, cos_ref, sin_ref, rows_o, q_o, kv_o):
    del s_ref
    block = x0.shape[0]
    for m, x in enumerate((x0, x1, x2, x3)):
        rows_o[m] = x[...]
    rows = rows_o[...].reshape(4 * block, x0.shape[1])
    cos, sin = cos_ref[...], sin_ref[...]
    at = 0
    total = (heads + 2) * LANES
    while at < total:
        width = min(3 * LANES, total - at)
        lin = nt(rows, w_ref[at : at + width])
        for j in range(width // LANES):
            slot = at // LANES + j
            v = lin[:, j * LANES : (j + 1) * LANES]
            if slot <= heads:
                v = v * cos + half_turn(v) * sin
            if slot < heads:
                v = (v * 0.125).astype(BF)
                for m in range(4):
                    q_o[m, slot] = v[m * block : (m + 1) * block]
            else:
                v = v.astype(BF)
                lo = (slot - heads) * LANES
                for m in range(4):
                    kv_o[m, :, lo : lo + LANES] = v[m * block : (m + 1) * block]
        at += width


def side_mask(c, heads, block):
    head = lax.broadcasted_iota(jnp.int32, (heads * block, LANES), 0) // block
    lane = lax.broadcasted_iota(jnp.int32, (heads * block, LANES), 1)
    return (lane // D) == ((c * heads + head) // GROUP - (c * heads) // GROUP)


def key_positions(t, block, first, count):
    row = lax.broadcasted_iota(jnp.int32, (count, 1), 0)
    return first + ((row // block) ^ t) * block + row % block


def attn_kernel(
    heads, s_ref, q_ref, k0, k1, k2, k3, w_ref, att_o, lse_o, p0, p1, p2, p3, k_s, vt_s, m_s, l_s, a_s
):
    c, t, prefix = s_ref[0], s_ref[1], s_ref[2]
    block = q_ref.shape[2]
    keys = 4 * block
    wide = heads * block
    for ck in range(4):
        m = c ^ ck
        v = jnp.concatenate([r[m, :, LANES:] for r in (k0, k1, k2, k3)], axis=0)
        vt_s[ck] = jnp.transpose(v.astype(F32)).astype(BF)
        for i, r in enumerate((k0, k1, k2, k3)):
            k_s[ck, i * block : (i + 1) * block] = r[m, :, :LANES]
    mask = side_mask(c, heads, block)
    q_at = lax.broadcasted_iota(jnp.int32, (1, wide), 1) % block + t * block

    for cq in range(4):
        m = c ^ cq
        q = q_ref[m].reshape(wide, LANES)
        m_s[...] = jnp.full_like(m_s, MASKED)
        l_s[...] = jnp.zeros_like(l_s)
        a_s[...] = jnp.zeros_like(a_s)

        def step(ck, q=q, cq=cq):
            s = nt(k_s[ck], q)
            if ck >= cq:
                at = key_positions(t, block, ck * keys, keys)
                seen = (at <= q_at + cq * keys) | (at < prefix)
                s = jnp.where(seen, s, MASKED)
            old = m_s[...]
            top = jnp.maximum(old, jnp.max(s, axis=0, keepdims=True))
            p = jnp.exp(s - top)
            decay = jnp.exp(old - top)
            l_s[...] = l_s[...] * decay + jnp.sum(p, axis=0, keepdims=True)
            a_s[...] = a_s[...] * decay + nn(vt_s[ck], p.astype(BF))
            m_s[...] = top

        for ck in range(4):
            if ck <= cq:
                step(ck)
            else:
                pl.when(ck * keys < prefix)(functools.partial(step, ck))
        o = jnp.transpose(a_s[...] / l_s[...])
        o = jnp.where(mask, o, 0.0).astype(BF)
        for h in range(heads):
            att_o[m, :, h * LANES : (h + 1) * LANES] = o[h * block : (h + 1) * block]
        lse_o[cq] = m_s[...] + jnp.log(l_s[...])
    full = att_o[...].reshape(4 * block, heads * LANES)
    w_at = (heads + 2) * LANES
    part = nn(full, w_ref[w_at : w_at + heads * LANES]).astype(BF)
    for m, r in enumerate((p0, p1, p2, p3)):
        r[...] = part[m * block : (m + 1) * block]


def attn_back_kernel(
    heads, s_ref, y0, y1, y2, y3, w_ref, q_ref, k0, k1, k2, k3, att_ref, lse_ref, cos_ref, sin_ref,
    rows_o, dq_o, g0, g1, g2, g3, do_s, de_s, dqt_s, dk_s, dv_s
):
    c, t, prefix = s_ref[0], s_ref[1], s_ref[2]
    block = q_ref.shape[2]
    keys = 4 * block
    wide = heads * block
    for m, y in enumerate((y0, y1, y2, y3)):
        rows_o[m] = y[...]
    w_at = (heads + 2) * LANES
    do = nt(rows_o[...].reshape(keys, y0.shape[1]), w_ref[w_at : w_at + heads * LANES]).astype(BF)
    for m in range(4):
        for h in range(heads):
            do_s[m, h * block : (h + 1) * block] = do[m * block : (m + 1) * block, h * LANES : (h + 1) * LANES]
    mask = side_mask(c, heads, block)
    for cq in range(4):
        m = c ^ cq
        a = att_ref[m]
        a = jnp.concatenate([a[:, h * LANES : (h + 1) * LANES] for h in range(heads)], axis=0)
        prod = a.astype(F32) * do_s[m].astype(F32)
        de_s[cq] = jnp.sum(jnp.transpose(prod), axis=0, keepdims=True)
    dqt_s[...] = jnp.zeros_like(dqt_s)
    q_at = lax.broadcasted_iota(jnp.int32, (1, wide), 1) % block + t * block
    for ck in range(4):
        mk = c ^ ck
        k = jnp.concatenate([r[mk, :, :LANES] for r in (k0, k1, k2, k3)], axis=0)
        v = jnp.concatenate([r[mk, :, LANES:] for r in (k0, k1, k2, k3)], axis=0)
        kt = jnp.transpose(k.astype(F32)).astype(BF)
        dk_s[...] = jnp.zeros_like(dk_s)
        dv_s[...] = jnp.zeros_like(dv_s)

        def step(cq, k=k, v=v, kt=kt, ck=ck):
            m = c ^ cq
            q = q_ref[m].reshape(wide, LANES)
            d_out = do_s[m]
            p = jnp.exp(nt(k, q) - lse_ref[cq])
            if ck >= cq:
                at = key_positions(t, block, ck * keys, keys)
                seen = (at <= q_at + cq * keys) | (at < prefix)
                p = jnp.where(seen, p, 0.0)
            ds = (p * (nt(v, d_out) - de_s[cq])).astype(BF)
            dk_s[...] += nn(ds, q)
            dv_s[...] += nn(p.astype(BF), d_out)
            dqt_s[cq] += nn(kt, ds)

        for cq in range(4):
            if cq >= ck:
                step(cq)
            else:
                pl.when(ck * keys < prefix)(functools.partial(step, cq))
        for i, r in enumerate((g0, g1, g2, g3)):
            r[mk, :, :LANES] = dk_s[i * block : (i + 1) * block].astype(BF)
            r[mk, :, LANES:] = dv_s[i * block : (i + 1) * block].astype(BF)
    for cq in range(4):
        m = c ^ cq
        dq = jnp.transpose(dqt_s[cq]) * 0.125
        turned = half_turn(dq)
        cos, sin = cos_ref[m], sin_ref[m]
        for h in range(heads):
            own = slice(h * block, (h + 1) * block)
            back = dq[own] * cos - turned[own] * sin
            dq_o[m, :, h * LANES : (h + 1) * LANES] = jnp.where(mask[own], back, 0.0).astype(BF)


def proj_back_kernel(heads, g0, g1, g2, g3, dq_ref, w_ref, cos_ref, sin_ref, d_o, p0, p1, p2, p3):
    block = dq_ref.shape[1]
    low = heads * LANES
    for m in range(4):
        d_o[m, :, :low] = dq_ref[m]
        total = (
            g0[m].astype(F32) + g1[m].astype(F32) + g2[m].astype(F32) + g3[m].astype(F32)
        )
        dk = total[:, :LANES]
        dk = dk * cos_ref[m] - half_turn(dk) * sin_ref[m]
        d_o[m, :, low : low + LANES] = dk.astype(BF)
        d_o[m, :, low + LANES :] = total[:, LANES:].astype(BF)
    full = d_o[...].reshape(4 * block, low + 2 * LANES)
    part = nn(full, w_ref[: low + 2 * LANES]).astype(BF)
    for m, r in enumerate((p0, p1, p2, p3)):
        r[...] = part[m * block : (m + 1) * block]


def chunks(width, step=256):
    return [(at, min(step, width - at)) for at in range(0, width, step)]


def ffn_kernel(x0, x1, x2, x3, w_ref, rows_o, gate_o, up_o, p0, p1, p2, p3, acc):
    block = x0.shape[0]
    for m, x in enumerate((x0, x1, x2, x3)):
        rows_o[m] = x[...]
    rows = rows_o[...].reshape(4 * block, x0.shape[1])
    for at, width in chunks(w_ref.shape[1]):
        g = nt(rows, w_ref[0, at : at + width])
        u = nt(rows, w_ref[1, at : at + width])
        gate_o[:, at : at + width] = g.astype(BF)
        up_o[:, at : at + width] = u.astype(BF)
        hidden = (g / (1.0 + jnp.exp(-g)) * u).astype(BF)
        term = nn(hidden, w_ref[2, at : at + width])
        if at == 0:
            acc[...] = term
        else:
            acc[...] += term
    for m, r in enumerate((p0, p1, p2, p3)):
        r[...] = acc[m * block : (m + 1) * block].astype(BF)


def ffn_back_kernel(
    y0, y1, y2, y3, w_ref, gate_ref, up_ref, rows_o, dg_o, du_o, h_o, p0, p1, p2, p3, acc
):
    block = y0.shape[0]
    for m, y in enumerate((y0, y1, y2, y3)):
        rows_o[m] = y[...]
    rows = rows_o[...].reshape(4 * block, y0.shape[1])
    for at, width in chunks(w_ref.shape[1]):
        own = slice(at, at + width)
        dh = nt(rows, w_ref[2, own])
        g = gate_ref[:, own].astype(F32)
        u = up_ref[:, own].astype(F32)
        s = 1.0 / (1.0 + jnp.exp(-g))
        dg = (dh * u * s * (1.0 + g * (1.0 - s))).astype(BF)
        du = (dh * g * s).astype(BF)
        dg_o[:, own] = dg
        du_o[:, own] = du
        h_o[:, own] = (g * s * u).astype(BF)
        term = nn(dg, w_ref[0, own]) + nn(du, w_ref[1, own])
        if at == 0:
            acc[...] = term
        else:
            acc[...] += term
    for m, r in enumerate((p0, p1, p2, p3)):
        r[...] = acc[m * block : (m + 1) * block].astype(BF)


def weight_grad_kernel(parts, count, *refs):
    lefts, rights, outs = refs[:count], refs[count : 2 * count], refs[2 * count :]
    cols = rights[0].shape[-1] // parts
    rows = lefts[0].shape[0]
    for x in range(parts):
        for at, width in chunks(lefts[0].shape[1]):
            total = None
            for left, right in zip(lefts, rights):
                r = right[:, :, x * cols : (x + 1) * cols].reshape(rows, cols)
                term = tn(left[:, at : at + width], r)
                total = term if total is None else total + term
            outs[x][at : at + width] = total.astype(BF)


def pad_kernel(heads, s_ref, w_ref, o_ref):
    c = s_ref[0]
    o_ref[...] = jnp.zeros_like(o_ref)
    for h in range(heads):
        side = head_side(c, heads, h) * D
        o_ref[pl.ds(pl.multiple_of(h * LANES + side, D), D)] = w_ref[h * D : (h + 1) * D]
        o_ref[pl.ds(pl.multiple_of((heads + 2 + h) * LANES + side, D), D)] = w_ref[
            heads * D + 2 * LANES + h * D : heads * D + 2 * LANES + (h + 1) * D
        ]
    o_ref[heads * LANES : (heads + 2) * LANES] = w_ref[heads * D : heads * D + 2 * LANES]


def unpad_kernel(heads, s_ref, a_ref, b_ref, o_ref):
    c = s_ref[0]
    for h in range(heads):
        at = pl.multiple_of(h * LANES + head_side(c, heads, h) * D, D)
        o_ref[h * D : (h + 1) * D] = a_ref[pl.ds(at, D)]
        lo = heads * D + 2 * LANES + h * D
        o_ref[lo : lo + D] = b_ref[pl.ds(at, D)]
    o_ref[heads * D : heads * D + 2 * LANES] = a_ref[heads * LANES : (heads + 2) * LANES]


def xor(a, b):
    return lax.rem(a + b, 2) + 2 * lax.rem(lax.div(a, 2) + lax.div(b, 2), 2)


class Net:
    def __init__(self, r):
        self.r = r
        self.sems = (r.send, r.recv, r.loc)
        self.remote, self.local_at = 0, 0
        self.x, self.c, self.t = (lax.axis_index(a) for a in (DP, CTX, TP))
        self.inner = (self.t == 1) | (self.t == 2)

    def barrier(self):
        sem = pltpu.get_barrier_semaphore()
        peers = [(CTX, 1), (CTX, 2), (CTX, 3), (TP, 1), (TP, 2), (TP, 3), (DP, 1)]
        for axis, m in peers:
            pl.semaphore_signal(
                sem, inc=1, device_id={axis: self.peer(axis, m)}, device_id_type=pl.DeviceIdType.MESH
            )
        pl.semaphore_wait(sem, len(peers))

    def peer(self, axis, m):
        if axis == DP:
            return 1 - self.x
        return xor(self.c if axis == CTX else self.t, m)

    def make(self, src, dst, axis, m):
        i = self.remote
        self.remote += 1
        return pltpu.make_async_remote_copy(
            src_ref=src,
            dst_ref=dst,
            send_sem=self.sems[0].at[i],
            recv_sem=self.sems[1].at[i],
            device_id={axis: self.peer(axis, m)},
            device_id_type=pl.DeviceIdType.MESH,
        )

    def send(self, src, dst, axis, m=1):
        copy = self.make(src, dst, axis, m)
        copy.start()
        return copy

    def local(self, src, dst):
        i = self.local_at
        self.local_at += 1
        copy = pltpu.make_async_copy(src, dst, self.sems[2].at[i])
        copy.start()
        return copy

    def close(self, copies):
        for copy in copies:
            copy.wait_send()

    def spread_tp(self, src, slots):
        two = self.send(src, slots[2], TP, 2)
        one = self.send(src, slots[1], TP, 1)
        mid = self.make(src, slots[3], TP, 3)
        end = self.make(slots[2], slots[3], TP, 1)
        return one, two, mid, end

    def spread_tp_on(self, copies):
        _, two, mid, end = copies
        two.wait_recv()

        @pl.when(self.inner)
        def _():
            end.start()
            mid.start()

    def spread_tp_last(self, copies):
        _, _, mid, end = copies
        pl.when(self.inner)(mid.wait_recv)
        pl.when(jnp.logical_not(self.inner))(end.wait_recv)

    def spread_tp_close(self, copies):
        one, two, mid, end = copies
        self.close([one, two])

        @pl.when(self.inner)
        def _():
            mid.wait_send()
            end.wait_send()


def run(tasks):
    for task in tasks:
        next(task, None)


def forward_kernel(cfg, r):
    layers, seqs, block, width, heads, units, share = cfg
    part, quarter, keys = 4 * share, units // 4, 4 * block
    net = Net(r)
    x, c, t = net.x, net.c, net.t
    low = lax.div(c * heads, GROUP)
    half = pl.ds(pl.multiple_of(x * part, LANES), part)
    prefix = [r.prefix[s] for s in range(seqs)]
    kept = []
    gu_copy = []

    net.barrier()

    def attn_weights(l):
        qz, qc, kvl, own, tmp, wa = r.qz.at[l], r.qc.at[l], r.kvl.at[l], r.own, r.tmp, r.wa
        mine = [net.local(r.qo.at[l], qz.at[0]), net.local(r.kvw.at[l], kvl.at[c])]
        tp = net.spread_tp(r.qo.at[l], [qz.at[i] for i in range(4)])
        kvs = [net.send(r.kvw.at[l], kvl.at[c], CTX, m) for m in (1, 2, 3)]
        wide = heads * LANES
        wa[l, :wide] = jnp.zeros((wide, width), BF)
        wa[l, wide + 2 * LANES :] = jnp.zeros((wide, width), BF)
        yield
        net.spread_tp_on(tp)
        yield
        mine[0].wait()
        tp[0].wait_recv()
        net.spread_tp_last(tp)
        mine.append(net.local(qz.at[xor(t, c)], qc.at[c]))
        ctx = [net.send(qz.at[xor(t, xor(c, m))], qc.at[c], CTX, m) for m in (1, 2, 3)]
        yield
        for copy in kvs + ctx:
            copy.wait_recv()
        mine[1].wait()
        mine[2].wait()
        stage = [net.local(qc, r.st_q), net.local(kvl, r.st_k)]
        stage[0].wait()
        for at in range(0, 2 * heads * D, LANES):
            got = jnp.transpose(r.st_q[:, :, at : at + LANES].reshape(part, LANES).astype(F32)).astype(BF)
            for k in range(0, LANES, D):
                to = at + k if at + k < heads * D else at + k + 2 * LANES
                own[to : to + D] = got[k : k + D]
        stage[1].wait()
        for at in range(0, 2 * KEY_VALUE_HEADS * D, LANES):
            got = r.st_k[:, :, at : at + LANES].reshape(part, LANES)
            tmp[at : at + LANES] = jnp.transpose(got.astype(F32)).astype(BF)
        own[heads * D : heads * D + LANES] = tmp[pl.ds(pl.multiple_of(low * D, D), LANES)]
        own[heads * D + LANES : heads * D + 2 * LANES] = tmp[
            pl.ds(pl.multiple_of((KEY_VALUE_HEADS + low) * D, D), LANES)
        ]
        dp = net.send(own, r.wc.at[l, :, half], DP)
        mine.append(net.local(own, r.wc.at[l, :, half]))
        yield
        dp.wait_recv()
        mine[3].wait()
        pads = []
        for h in range(heads):
            side = (lax.div(c * heads + h, GROUP) - low) * D
            for src, dst in ((h * D, h * LANES), (heads * D + 2 * LANES + h * D, (heads + 2 + h) * LANES)):
                pads.append(
                    net.local(
                        r.wc.at[l, src : src + D],
                        wa.at[l, pl.ds(pl.multiple_of(dst + side, D), D)],
                    )
                )
        pads.append(
            net.local(r.wc.at[l, heads * D : heads * D + 2 * LANES], wa.at[l, wide : wide + 2 * LANES])
        )
        yield
        for copy in pads:
            copy.wait()
        net.close(kvs + ctx + [dp])
        net.spread_tp_close(tp)
        kept.append(net.local(wa.at[l], r.wa_o.at[l]))
        yield

    def ffn_weights(l):
        fc, wf = r.fc.at[l], r.wf
        ctx = [net.send(r.fp.at[l, xor(c, m)], fc.at[c], CTX, m) for m in (1, 2, 3)]
        mine = net.local(r.fp.at[l, c], fc.at[c])
        yield
        for copy in ctx:
            copy.wait_recv()
        mine.wait()
        stage = net.local(fc, r.st_f)
        stage.wait()
        for i in range(3):
            piece = [r.st_f[k][:, i * share : (i + 1) * share] for k in range(4)]
            wf[l, i, :quarter, half] = jnp.concatenate(piece, axis=1)
        yield
        slots = [wf.at[l, :, i * quarter : (i + 1) * quarter, half] for i in range(4)]
        tp = net.spread_tp(slots[0], slots)
        dp = [net.send(slots[0], slots[0], DP)]
        yield
        net.spread_tp_on(tp)
        dp.append(net.send(slots[2], slots[2], DP))
        tp[0].wait_recv()
        dp.append(net.send(slots[1], slots[1], DP))
        yield
        net.spread_tp_last(tp)
        dp.append(net.send(slots[3], slots[3], DP))
        yield
        for copy in dp:
            copy.wait_recv()
        net.close(ctx + dp)
        net.spread_tp_close(tp)
        kept.append(net.local(wf.at[l], r.wf_o.at[l]))
        yield

    def gather_start(v, gain, s, rows):
        u = v * lax.rsqrt(jnp.mean(v * v, axis=-1, keepdims=True) + EPS)
        rows[s, 0] = (u * gain).astype(BF)
        return [
            net.send(rows.at[s, 0], rows.at[s, 2], CTX, 2),
            net.send(rows.at[s, 0], rows.at[s, 1], CTX, 1),
        ]

    def gather_on(copies, s, rows):
        copies[0].wait_recv()
        copies.append(net.send(rows.at[s, 2], rows.at[s, 3], CTX, 1))

    def gather_end(copies):
        copies[1].wait_recv()
        copies[2].wait_recv()

    def reduce_start(s):
        pt, rn = r.pt, r.rn
        return [
            net.send(pt.at[s, 3], rn.at[s, 1], CTX, 1),
            net.send(pt.at[s, 1], rn.at[s, 0], CTX, 1),
        ]

    def reduce_on(copies, s):
        copies[0].wait_recv()
        r.far[s] = (r.pt[s, 2].astype(F32) + r.rn[s, 1].astype(F32)).astype(BF)
        copies.append(net.send(r.far.at[s], r.rf.at[s], CTX, 2))

    def reduce_end(copies, s):
        copies[1].wait_recv()
        copies[2].wait_recv()
        total = r.pt[s, 0].astype(F32) + r.rn[s, 0].astype(F32) + r.rf[s].astype(F32)
        net.close(copies)
        return total

    def sequence(s):
        rows, frows, q, att, pt, gu = r.rows, r.frows, r.q, r.att, r.pt, r.gu
        carry = []
        for l in range(layers):
            kv = r.kv
            gather = gather_start(r.stream[s], r.gain[l : l + 1], s, rows)
            yield
            gather_on(gather, s, rows)
            yield
            gather_end(gather)
            tp = []
            qkv_body(
                heads, rows.at[s], r.wa.at[l], r.cos, r.sin, q.at[s], kv.at[l, s, 0],
                lambda: tp.append(net.spread_tp(kv.at[l, s, 0], [kv.at[l, s, i] for i in range(4)])),
            )
            tp = tp[0]
            outs = [net.local(rows.at[s], r.rows_o.at[l, s]), net.local(q.at[s], r.q_o.at[l, s])] + carry
            yield
            net.spread_tp_on(tp)
            yield
            tp[0].wait_recv()
            net.spread_tp_last(tp)
            outs.append(net.local(kv.at[l, s], r.kv_o.at[l, s]))
            attn_body(
                heads, c, t, prefix[s], q.at[s], kv.at[l, s], r.wa.at[l], att.at[s], r.lse.at[s],
                pt.at[s], r.k_s, r.vt_s, r.m_s, r.l_s, r.a_s,
            )
            reduce = reduce_start(s)
            outs.append(net.local(att.at[s], r.att_o.at[l, s]))
            outs.append(net.local(r.lse.at[s], r.lse_o.at[l, s]))
            net.close(gather)
            yield
            reduce_on(reduce, s)
            yield
            r.middle[s] = r.stream[s] + reduce_end(reduce, s)
            outs.append(net.local(r.middle.at[s], r.middle_o.at[l, s]))
            gather = gather_start(r.middle[s], r.gain[layers + l : layers + l + 1], s, frows)
            yield
            gather_on(gather, s, frows)
            yield
            gather_end(gather)
            outs.pop(0).wait()
            if gu_copy:
                gu_copy.pop().wait()
            ffn_body(frows.at[s], r.wf.at[l], gu, pt.at[s], r.hid)
            reduce = reduce_start(s)
            outs.append(net.local(frows.at[s], r.frows_o.at[l, s]))
            gu_copy.append(net.local(gu, r.gu_o.at[l, s]))
            net.close(gather)
            net.spread_tp_close(tp)
            yield
            reduce_on(reduce, s)
            yield
            for copy in outs:
                copy.wait()
            r.stream[s] = r.middle[s] + reduce_end(reduce, s)
            if l + 1 < layers:
                carry = [net.local(r.stream.at[s], r.stream_o.at[l, s])]
            else:
                r.far[s] = r.stream[s].astype(BF)
                kept.append(net.local(r.far.at[s], r.out_o.at[s]))
            yield

    gl = r.gl
    start = net.local(r.tokens, r.far)
    gl[x, c] = r.gains[...]
    near = [net.send(gl.at[x, c], gl.at[x, c], CTX, m) for m in (1, 2, 3)]
    (w0, w1), (f0, f1) = [attn_weights(l) for l in range(layers)], [ffn_weights(l) for l in range(layers)]
    run([f0, w0])
    start.wait()
    r.stream[...] = r.far[...].astype(F32)
    for copy in near:
        copy.wait_recv()
    over = net.send(gl.at[x], gl.at[x], DP)
    over.wait_recv()
    pieces = [gl[k, i][: 2 * layers, :share] for k in range(2) for i in range(4)]
    r.gain[...] = jnp.concatenate(pieces, axis=1)
    kept.append(net.local(r.gain, r.gain_o))

    def cotangent():
        cot, dy = r.cot, r.dy_o
        mine = [net.local(cot.at[s], dy.at[s, 0]) for s in range(seqs)]
        far = [net.send(cot.at[s], dy.at[s, 2], CTX, 2) for s in range(seqs)]
        side = [net.send(cot.at[s], dy.at[s, 1], CTX, 1) for s in range(seqs)]
        yield
        for s in range(seqs):
            far[s].wait_recv()
            side.append(net.send(dy.at[s, 2], dy.at[s, 3], CTX, 1))
        yield
        for copy in side:
            copy.wait_recv()
        for copy in mine:
            copy.wait()
        net.close(far + side)
        yield

    a, b, extra = sequence(0), sequence(1), cotangent()
    order = (
        w0, f0, a, f0, w0, w0, b, f0, b, f1, w0, w0, b, b,
        f1, a, w1, a, f0, b, b, w1, a, f1, w1, b, a, f0,
        a, b, w1, b, a, b, a, f1, a, b, b, a, w1, w1,
        b, b, a, a, b, extra, f1, a, a, b, extra, a, b, a,
        b, a, b, extra, a, f1, b, a, b, a, a, b, a,
    )
    run(order)
    net.close(near + [over])
    for copy in kept + gu_copy:
        copy.wait()


def qkv_body(heads, rows_ref, w_ref, cos_ref, sin_ref, q_o, kv_o, between=None):
    block, width = rows_ref.shape[1], rows_ref.shape[2]
    rows = rows_ref[...].reshape(4 * block, width)
    cos, sin = cos_ref[...], sin_ref[...]
    for at, wide in [(heads * LANES, 2 * LANES)] + chunks(heads * LANES):
        lin = nt(rows, w_ref[at : at + wide])
        for j in range(wide // LANES):
            slot = at // LANES + j
            v = lin[:, j * LANES : (j + 1) * LANES]
            if slot <= heads:
                v = v * cos + half_turn(v) * sin
            if slot < heads:
                v = (v * 0.125).astype(BF)
                for m in range(4):
                    q_o[m, slot] = v[m * block : (m + 1) * block]
            else:
                v = v.astype(BF)
                lo = (slot - heads) * LANES
                for m in range(4):
                    kv_o[m, :, lo : lo + LANES] = v[m * block : (m + 1) * block]
        if at == heads * LANES and between:
            between()


def attn_body(heads, c, t, prefix, q_ref, kv_ref, w_ref, att_o, lse_o, pt_o, k_s, vt_s, m_s, l_s, a_s):
    block = q_ref.shape[2]
    keys = 4 * block
    wide = heads * block
    for ck in range(4):
        m = xor(c, ck)
        v = jnp.concatenate([kv_ref[i, m, :, LANES:] for i in range(4)], axis=0)
        vt_s[ck] = jnp.transpose(v.astype(F32)).astype(BF)
        for i in range(4):
            k_s[ck, i * block : (i + 1) * block] = kv_ref[i, m, :, :LANES]
    mask = side_mask(c, heads, block)
    q_at = lax.broadcasted_iota(jnp.int32, (1, wide), 1) % block + t * block
    for cq in range(4):
        m = xor(c, cq)
        q_all = q_ref[m].reshape(wide, LANES)
        for first, span in chunks(wide, 3 * LANES):
            own = slice(first, first + span)
            q = q_all[own]
            for ck in range(4):
                if ck > cq and ck * keys >= PREFIX_MAX:
                    continue
                s = nt(k_s[ck], q)
                if ck >= cq:
                    at = key_positions(t, block, ck * keys, keys)
                    seen = (at <= q_at[:, own] + cq * keys) | (at < prefix)
                    s = jnp.where(seen, s, MASKED)
                top = jnp.max(s, axis=0, keepdims=True)
                if ck:
                    old = m_s[:, own]
                    top = jnp.maximum(old, top)
                    decay = jnp.exp(old - top)
                p = jnp.exp(s - top)
                add, term = jnp.sum(p, axis=0, keepdims=True), nn(vt_s[ck], p.astype(BF))
                l_s[:, own] = l_s[:, own] * decay + add if ck else add
                a_s[:, own] = a_s[:, own] * decay + term if ck else term
                m_s[:, own] = top
        o = jnp.transpose(a_s[...] / l_s[...])
        o = jnp.where(mask, o, 0.0).astype(BF)
        for h in range(heads):
            att_o[m, :, h * LANES : (h + 1) * LANES] = o[h * block : (h + 1) * block]
        lse_o[cq] = m_s[...] + jnp.log(l_s[...])
    full = att_o[...].reshape(4 * block, heads * LANES)
    w_at = (heads + 2) * LANES
    for at, span in chunks(w_ref.shape[1]):
        own = slice(at, at + span)
        part = nn(full, w_ref[w_at : w_at + heads * LANES, own]).astype(BF)
        for m in range(4):
            pt_o[m, :, own] = part[m * block : (m + 1) * block]


def ffn_body(rows_ref, w_ref, gu_o, pt_o, hid):
    block, width = rows_ref.shape[1], rows_ref.shape[2]
    rows = rows_ref[...].reshape(4 * block, width)
    for at, wide in chunks(w_ref.shape[1]):
        own = slice(at, at + wide)
        g = nt(rows, w_ref[0, own])
        u = nt(rows, w_ref[1, own])
        gu_o[0, :, own] = g.astype(BF)
        gu_o[1, :, own] = u.astype(BF)
        hid[:, own] = (g / (1.0 + jnp.exp(-g)) * u).astype(BF)
    for at, wide in chunks(width):
        own = slice(at, at + wide)
        part = nn(hid[...], w_ref[2, :, own]).astype(BF)
        for m in range(4):
            pt_o[m, :, own] = part[m * block : (m + 1) * block]


def launch(kernel, number, ins, outs, scratch, sems=(80, 90), vmem=62):
    sem = pltpu.SemaphoreType.DMA
    scratch = {k: pltpu.VMEM(*v) for k, v in scratch.items()}
    scratch.update(send=sem((sems[0],)), recv=sem((sems[0],)), loc=sem((sems[1],)))
    names = [*ins, *outs, *scratch]

    def body(*refs):
        kernel(types.SimpleNamespace(**dict(zip(names, refs))))

    got = pl.pallas_call(
        body,
        out_shape=[jax.ShapeDtypeStruct(v[0], v[1]) for v in outs.values()],
        in_specs=[pl.BlockSpec(memory_space=v[1]) for v in ins.values()],
        out_specs=[pl.BlockSpec(memory_space=v[2]) for v in outs.values()],
        scratch_shapes=list(scratch.values()),
        compiler_params=pltpu.CompilerParams(
            collective_id=number, has_side_effects=True, vmem_limit_bytes=vmem * 2**20
        ),
        cost_estimate=pl.CostEstimate(flops=10**11, bytes_accessed=10**8, transcendentals=10**7),
    )(*[v[0] for v in ins.values()])
    return types.SimpleNamespace(**dict(zip(outs, got)))


def forward_pass(cfg, tokens, cot, prefix, gains, qo, kvw, fp, cos, sin):
    layers, seqs, block, width, heads, units, share = cfg
    hbm, vm = pl.ANY, pltpu.VMEM
    keys, part = 4 * block, 4 * share
    rows = (seqs, 4, block, width)
    own = (seqs, block, width)
    size = 2 * (heads + 1) * LANES
    compact = 2 * heads * D + 2 * LANES
    q_s = (4, heads, block, LANES)
    kv_s = (4, 4, block, 2 * LANES)
    raw = (4, share, 2 * heads * D)
    raw_k = (4, share, 2 * KEY_VALUE_HEADS * D)
    raw_f = (4, units // 4, 3 * share)
    return launch(
        functools.partial(forward_kernel, cfg),
        0,
        dict(
            prefix=(prefix, pltpu.SMEM), tokens=(tokens, hbm), cot=(cot, hbm), gains=(gains, vm), qo=(qo, hbm),
            kvw=(kvw, hbm), fp=(fp, hbm), cos=(cos, vm), sin=(sin, vm),
        ),
        dict(
            out_o=(own, BF, hbm),
            wc=((layers, compact, width), BF, hbm),
            wa_o=((layers, size, width), BF, hbm),
            wf_o=((layers, 3, units, width), BF, hbm),
            rows_o=((layers, *rows), BF, hbm),
            q_o=((layers, seqs, *q_s), BF, hbm),
            kv_o=((layers, seqs, *kv_s), BF, hbm),
            att_o=((layers, seqs, 4, block, heads * LANES), BF, hbm),
            lse_o=((layers, seqs, 4, 1, heads * block), F32, hbm),
            middle_o=((layers, *own), F32, hbm),
            frows_o=((layers, *rows), BF, hbm),
            gu_o=((layers, seqs, 2, keys, units), BF, hbm),
            stream_o=((layers - 1, *own), F32, hbm),
            gain_o=((2 * layers, width), F32, hbm),
            dy_o=(rows, BF, hbm),
            qz=((layers, *raw), BF, hbm),
            qc=((layers, *raw), BF, hbm),
            kvl=((layers, *raw_k), BF, hbm),
            fc=((layers, *raw_f), BF, hbm),
        ),
        dict(
            stream=(own, F32),
            middle=(own, F32),
            rows=(rows, BF),
            frows=(rows, BF),
            q=((seqs, *q_s), BF),
            kv=((layers, seqs, *kv_s), BF),
            att=((seqs, 4, block, heads * LANES), BF),
            lse=((seqs, 4, 1, heads * block), F32),
            pt=(rows, BF),
            rn=((seqs, 2, block, width), BF),
            far=(own, BF),
            rf=(own, BF),
            gu=((2, keys, units), BF),
            hid=((keys, units), BF),
            k_s=((4, keys, LANES), BF),
            vt_s=((4, LANES, keys), BF),
            m_s=((1, heads * block), F32),
            l_s=((1, heads * block), F32),
            a_s=((LANES, heads * block), F32),
            wa=((layers, size, width), BF),
            wf=((layers, 3, units, width), BF),
            st_q=(raw, BF),
            st_k=(raw_k, BF),
            st_f=(raw_f, BF),
            own=((compact, part), BF),
            tmp=((2 * KEY_VALUE_HEADS * D, part), BF),
            gl=((2, 4, 8, 256), F32),
            gain=((2 * layers, width), F32),
        ),
        sems=(130, 110),
        vmem=63,
    )


class Rows(Net):
    def gather_start(self, v, s, rows):
        rows[s, 0] = v.astype(BF)
        return [
            self.send(rows.at[s, 0], rows.at[s, 2], CTX, 2),
            self.send(rows.at[s, 0], rows.at[s, 1], CTX, 1),
        ]

    def gather_on(self, copies, s, rows):
        copies[0].wait_recv()
        copies.append(self.send(rows.at[s, 2], rows.at[s, 3], CTX, 1))

    def gather_end(self, copies):
        copies[1].wait_recv()
        copies[2].wait_recv()
        self.close(copies)

    def reduce_start(self, s):
        pt, rn = self.r.pt, self.r.rn
        return [
            self.send(pt.at[s, 3], rn.at[s, 1], CTX, 1),
            self.send(pt.at[s, 1], rn.at[s, 0], CTX, 1),
        ]

    def reduce_on(self, copies, s):
        r = self.r
        copies[0].wait_recv()
        r.far[s] = (r.pt[s, 2].astype(F32) + r.rn[s, 1].astype(F32)).astype(BF)
        copies.append(self.send(r.far.at[s], r.rf.at[s], CTX, 2))

    def reduce_end(self, copies, s):
        r = self.r
        copies[1].wait_recv()
        copies[2].wait_recv()
        total = r.pt[s, 0].astype(F32) + r.rn[s, 0].astype(F32) + r.rf[s].astype(F32)
        self.close(copies)
        return total

    def norm_back(self, s, copies, gain, row):
        r = self.r
        local, v = self.reduce_end(copies, s), r.base[s]
        scale = lax.rsqrt(jnp.mean(v * v, axis=-1, keepdims=True) + EPS)
        u = v * scale
        e = local * gain
        r.grad[s] = r.grad[s] + scale * (e - u * jnp.mean(e * u, axis=-1, keepdims=True))
        r.gs_o[row : row + 1] += jnp.sum(local * u, axis=0, keepdims=True)

    def sum_tp(self, parts, lands):
        outer = jnp.logical_not(self.inner)
        one = self.make(parts[1], lands[0], TP, 1)
        two = self.make(parts[2], lands[1], TP, 2)
        hand = self.make(parts[3], lands[2], TP, 1)
        mid = self.make(parts[3], lands[3], TP, 3)

        @pl.when(outer)
        def _():
            hand.start()
            two.start()

        @pl.when(self.inner)
        def _():
            mid.start()
            one.start()

        return one, two, hand, mid

    def sum_tp_on(self, copies, part, land):
        one, two, hand, _ = copies
        pl.when(jnp.logical_not(self.inner))(one.start)

        @pl.when(self.inner)
        def _():
            hand.wait_recv()
            part[...] = (part[...].astype(F32) + land[...].astype(F32)).astype(BF)
            two.start()

    def sum_tp_end(self, copies, own, lands):
        one, two, hand, mid = copies
        outer = jnp.logical_not(self.inner)
        one.wait_recv()
        two.wait_recv()

        @pl.when(self.inner)
        def _():
            mid.wait_recv()
            mid.wait_send()

        @pl.when(outer)
        def _():
            lands[3][...] = jnp.zeros(lands[3].shape, lands[3].dtype)
            hand.wait_send()

        one.wait_send()
        two.wait_send()
        return (
            own[...].astype(F32)
            + lands[0][...].astype(F32)
            + lands[1][...].astype(F32)
            + lands[3][...].astype(F32)
        )


def ffn_back_body(rows_ref, w_ref, gu_ref, hgu, pt_o, waits, between=None):
    block, width = rows_ref.shape[1], rows_ref.shape[2]
    rows = rows_ref[...].reshape(4 * block, width)
    for at, wide in chunks(w_ref.shape[1]):
        own = slice(at, at + wide)
        dh = nt(rows, w_ref[2, own])
        g = gu_ref[0, :, own].astype(F32)
        u = gu_ref[1, :, own].astype(F32)
        s = 1.0 / (1.0 + jnp.exp(-g))
        hgu[0, :, own] = (g * s * u).astype(BF)
        hgu[1, :, own] = (dh * u * s * (1.0 + g * (1.0 - s))).astype(BF)
        hgu[2, :, own] = (dh * g * s).astype(BF)
    for copy in waits:
        copy.wait()
    if between:
        between()
    for at, wide in chunks(width):
        own = slice(at, at + wide)
        part = (nn(hgu[1], w_ref[0, :, own]) + nn(hgu[2], w_ref[1, :, own])).astype(BF)
        for m in range(4):
            pt_o[m, :, own] = part[m * block : (m + 1) * block]


def weight_grad_body(lefts, rights, cols, out):
    rows = lefts[0].shape[0]
    for at, wide in chunks(lefts[0].shape[1]):
        total = None
        for left, right in zip(lefts, rights):
            term = tn(left[:, at : at + wide], right[:, :, cols].reshape(rows, out.shape[1]))
            total = term if total is None else total + term
        out[at : at + wide] = total.astype(BF)


def attn_back_body(
    heads, c, t, prefix, rows_ref, w_ref, q_ref, kv_ref, att_ref, lse_ref, cos_ref, sin_ref, d_o, dkv_o,
    do_s, de_s, dqt_s, dk_s, dv_s
):
    block = q_ref.shape[2]
    keys = 4 * block
    wide = heads * block
    w_at = (heads + 2) * LANES
    rows = rows_ref[...].reshape(keys, rows_ref.shape[2])
    for at, span in chunks(wide):
        do = nt(rows, w_ref[w_at + at : w_at + at + span]).astype(BF)
        for m in range(4):
            for j in range(span // LANES):
                h = at // LANES + j
                do_s[m, h * block : (h + 1) * block] = do[
                    m * block : (m + 1) * block, j * LANES : (j + 1) * LANES
                ]
    mask = side_mask(c, heads, block)
    for cq in range(4):
        m = xor(c, cq)
        for h in range(heads):
            own = slice(h * block, (h + 1) * block)
            prod = att_ref[m, :, h * LANES : (h + 1) * LANES].astype(F32) * do_s[m, own].astype(F32)
            de_s[cq, :, own] = jnp.sum(jnp.transpose(prod), axis=0, keepdims=True)
    dqt_s[...] = jnp.zeros_like(dqt_s)
    q_at = lax.broadcasted_iota(jnp.int32, (1, wide), 1) % block + t * block
    for ck in range(4):
        mk = xor(c, ck)
        k = jnp.concatenate([kv_ref[i, mk, :, :LANES] for i in range(4)], axis=0)
        v = jnp.concatenate([kv_ref[i, mk, :, LANES:] for i in range(4)], axis=0)
        kt = jnp.transpose(k.astype(F32)).astype(BF)
        dk_s[...] = jnp.zeros_like(dk_s)
        dv_s[...] = jnp.zeros_like(dv_s)
        for cq in range(4):
            if ck > cq and ck * keys >= PREFIX_MAX:
                continue
            m = xor(c, cq)
            q_all = q_ref[m].reshape(wide, LANES)
            for first, span in chunks(wide, 3 * LANES):
                own = slice(first, first + span)
                q, d_out = q_all[own], do_s[m, own]
                p = jnp.exp(nt(k, q) - lse_ref[cq, :, own])
                if ck >= cq:
                    at = key_positions(t, block, ck * keys, keys)
                    seen = (at <= q_at[:, own] + cq * keys) | (at < prefix)
                    p = jnp.where(seen, p, 0.0)
                ds = (p * (nt(v, d_out) - de_s[cq, :, own])).astype(BF)
                dk_s[...] += nn(ds, q)
                dv_s[...] += nn(p.astype(BF), d_out)
                dqt_s[cq, :, own] += nn(kt, ds)
        for i in range(4):
            dkv_o[i, mk, :, :LANES] = dk_s[i * block : (i + 1) * block].astype(BF)
            dkv_o[i, mk, :, LANES:] = dv_s[i * block : (i + 1) * block].astype(BF)
    for cq in range(4):
        m = xor(c, cq)
        dq = jnp.transpose(dqt_s[cq]) * 0.125
        turned = half_turn(dq)
        cos, sin = cos_ref[m], sin_ref[m]
        for h in range(heads):
            own = slice(h * block, (h + 1) * block)
            back = dq[own] * cos - turned[own] * sin
            d_o[m, :, h * LANES : (h + 1) * LANES] = jnp.where(mask[own], back, 0.0).astype(BF)


def proj_back_body(heads, total, w_ref, cos_ref, sin_ref, d_o, pt_o):
    block = d_o.shape[1]
    low = heads * LANES
    for m in range(4):
        dk = total[m, :, :LANES]
        dk = dk * cos_ref[m] - half_turn(dk) * sin_ref[m]
        d_o[m, :, low : low + LANES] = dk.astype(BF)
        d_o[m, :, low + LANES :] = total[m, :, LANES:].astype(BF)
    full = d_o[...].reshape(4 * block, low + 2 * LANES)
    for at, span in chunks(w_ref.shape[1]):
        own = slice(at, at + span)
        part = nn(full, w_ref[: low + 2 * LANES, own]).astype(BF)
        for m in range(4):
            pt_o[m, :, own] = part[m * block : (m + 1) * block]


def ffn_sums(net, cfg, where):
    layers, seqs, block, width, heads, units, share = cfg
    quarter = units // 4
    r, c = net.r, net.c
    loads, sends = {}, {}

    def start():
        if where == 2:
            loads[1] = [net.local(r.fs_i, r.fs.at[0])]
        else:
            for i in (2, 0, 1):
                loads[i] = [net.local(r.dwk.at[i], r.fs.at[i])]
            loads[2].append(net.local(r.dwx, r.fx.at[2]))
            for i in (0, 1):
                sends[i] = net.send(r.dws.at[i], r.fx.at[i], DP)
        yield

    def one(i):
        at = 0 if where == 2 else i
        parts = [r.fs.at[at, m * quarter : (m + 1) * quarter] for m in range(4)]
        for copy in loads[i]:
            copy.wait()
        if i in sends:
            sends[i].wait_recv()
        if where != 2:
            for m in (3, 2, 1, 0):
                own = slice(m * quarter, (m + 1) * quarter)
                r.fs[i, own] = (r.fs[i, own].astype(F32) + r.fx[i, own].astype(F32)).astype(BF)
        if where == 1 and i == 1:
            out = net.local(r.fs.at[i], r.fs_o)
            yield
            out.wait()
            net.close(list(sends.values()))
            yield
        lands = [r.fz.at[k, at] for k in range(4)]
        sums = net.sum_tp(parts, lands)
        yield
        net.sum_tp_on(sums, parts[2], lands[2])
        yield
        r.fo[...] = net.sum_tp_end(sums, parts[0], lands).astype(BF)
        ft, fg = r.ft.at[at], r.fg.at[at]
        for first in range(0, 4 * share, LANES):
            ft[first : first + LANES] = jnp.transpose(r.fo[:, first : first + LANES].astype(F32)).astype(BF)
        out = [net.send(ft.at[piece(xor(c, m))], fg.at[c], CTX, m) for m in (1, 2, 3)]
        fg[c] = ft[piece(c)]
        yield
        for copy in out:
            copy.wait_recv()
        to = r.u_o if i == 1 else r.d_o if i else r.g_o
        to[...] = jnp.concatenate([fg[k].astype(F32) for k in range(4)], axis=1)
        net.close(out)
        if where == 0 and i in sends:
            net.close([sends[i]])
        yield

    def piece(i):
        return pl.ds(pl.multiple_of(i * share, 32), share)

    return start(), one(2), one(0), one(1)


def finish_attn(net, cfg, mine, other, waits):
    layers, seqs, block, width, heads, units, share = cfg
    r = net.r
    c, t = net.c, net.t
    wide = 2 * heads * D
    for copy in waits:
        copy.wait()
    for at in range(0, 4 * share, LANES):
        own = slice(at, at + LANES)
        total = mine[:, own].astype(F32) + other[:, own].astype(F32)
        r.at[own] = jnp.transpose(total).astype(BF)

    def piece(i):
        return r.at.at[pl.ds(pl.multiple_of(i * share, 32), share)]

    out = [net.send(piece(xor(c, m)), r.ac.at[c], CTX, m) for m in (1, 2, 3)]
    own = net.local(piece(c), r.ac.at[c])
    yield
    for copy in out:
        copy.wait_recv()
    own.wait()
    net.close(out)
    for m in range(4):
        r.aq[m] = r.ac[xor(t, m), :, :wide]
    parts = [r.aq.at[m] for m in range(4)]
    lands = [r.az.at[k] for k in range(4)]
    sums = net.sum_tp(parts, lands)
    for first, at in ((0, wide), (KEY_VALUE_HEADS * D, wide + LANES)):
        terms = []
        for h in range(KEY_VALUE_HEADS):
            total = None
            for i in range(4):
                j = h - i * heads // GROUP
                if j in (0, 1):
                    term = r.ac[i, :, at + j * D : at + (j + 1) * D].astype(F32)
                    total = term if total is None else total + term
            terms.append(total)
        r.av[:, first : first + KEY_VALUE_HEADS * D] = jnp.concatenate(terms, axis=1)
    outer = jnp.logical_not(net.inner)
    r.asum[0] = r.av[...].astype(BF)
    ends = net.make(r.asum.at[0], r.al.at[0], TP, 1)
    swap = net.make(r.asum.at[1], r.al.at[1], TP, 3)
    back = net.make(r.asum.at[2], r.al.at[2], TP, 1)
    pl.when(outer)(ends.start)
    yield

    @pl.when(net.inner)
    def _():
        ends.wait_recv()
        r.asum[1] = (r.av[...] + r.al[0].astype(F32)).astype(BF)
        swap.start()

    yield
    net.sum_tp_on(sums, parts[2], lands[2])
    yield

    @pl.when(net.inner)
    def _():
        swap.wait_recv()
        r.asum[2] = (r.asum[1].astype(F32) + r.al[1].astype(F32)).astype(BF)
        back.start()

    yield
    r.qo_o[...] = net.sum_tp_end(sums, parts[0], lands)

    @pl.when(net.inner)
    def _():
        swap.wait_send()
        back.wait_send()
        r.kv_o[...] = r.asum[2].astype(F32)

    @pl.when(outer)
    def _():
        ends.wait_send()
        back.wait_recv()
        r.kv_o[...] = r.al[2].astype(F32)

    yield


def finish_gains(net):
    r = net.r
    r.gt[...] = r.gs_o[...]
    for k, axis in enumerate((CTX, TP, DP)):
        ms = (1, 2, 3) if axis != DP else (1,)
        copies = [net.send(r.gt, r.gr.at[k, m - 1], axis, m) for m in ms]
        yield
        for copy in copies:
            copy.wait_recv()
        net.close(copies)
        total = r.gt[...]
        for m in ms:
            total = total + r.gr[k, m - 1]
        r.gt[...] = total
    r.gs_o[...] = r.gt[...]
    yield


def ffn_back_kernel2(cfg, l, tail, r):
    layers, seqs, block, width, heads, units, share = cfg
    net = Rows(r)
    part = 4 * share
    keep = pl.ds(pl.multiple_of(net.x * part, LANES), part)
    away = pl.ds(pl.multiple_of((1 - net.x) * part, LANES), part)
    net.barrier()
    loads = [net.local(r.dak, r.ak), net.local(r.dax, r.ax)] if tail else []
    first = [net.local(r.dy_i.at[0], r.dy.at[0]), net.local(r.wf_i.at[l, 2], r.wf.at[2])]
    first.append(net.local(r.gu_i.at[l, 0], r.gu.at[0]))
    second = [net.local(r.wf_i.at[l, i], r.wf.at[i]) for i in (0, 1)]
    later = [net.local(r.dy_i.at[s], r.dy.at[s]) for s in range(1, seqs)]
    later += [net.local(r.gu_i.at[l, s], r.gu.at[s]) for s in range(1, seqs)]
    state = [net.local(r.grad_i, r.grad), net.local(r.base_i.at[l], r.base)]
    state += [net.local(r.frows_i.at[l, s], r.frows.at[s]) for s in range(seqs)]
    r.gs_o[...] = r.gs_i[...]
    row = layers + l
    gain = r.gain[row : row + 1]
    saved, busy = [], {}

    def sequence(s, waits, more):
        rows, hgu, pt = r.dy.at[s], r.hgu.at[s], r.pt.at[s]
        for copy in waits:
            copy.wait()
        ffn_back_body(rows, r.wf, r.gu.at[s], hgu, pt, more)
        red = net.reduce_start(s)
        yield
        net.reduce_on(red, s)
        yield
        while state:
            state.pop().wait()
        net.norm_back(s, red, gain, row)
        gather = net.gather_start(r.grad[s], s, r.dn)
        saved.append(net.local(r.grad.at[s], r.grad_o.at[s]))
        yield
        net.gather_on(gather, s, r.dn)
        yield
        net.gather_end(gather)
        saved.append(net.local(r.dn.at[s], r.dn_o.at[s]))
        yield

    def weights(i, to):
        lefts = [r.hgu.at[s, i] for s in range(seqs)]
        rights = [(r.frows if i else r.dy).at[s] for s in range(seqs)]
        while state:
            state.pop().wait()
        if i:
            if 0 in busy:
                busy.pop(0).wait()
            weight_grad_body(lefts, rights, away, r.ws.at[0])
            busy[0] = net.local(r.ws.at[0], r.dws_o.at[to])
        else:
            weight_grad_body(lefts, rights, away, r.wx)
            cross = net.send(r.wx, r.dwx_o, DP)
        yield
        if 1 in busy:
            busy.pop(1).wait()
        weight_grad_body(lefts, rights, keep, r.ws.at[1])
        busy[1] = net.local(r.ws.at[1], r.dwk_o.at[to])
        yield
        if not i:
            cross.wait()
        yield

    a, b = sequence(0, first, second), sequence(1, later, [])
    w0, w1, w2 = weights(0, 2), weights(1, 0), weights(2, 1)
    if tail:
        fa = finish_attn(net, cfg, r.ak, r.ax, loads)
        x, _, _, f2 = ffn_sums(net, cfg, 2)
        order = (
            x,
            fa, a, f2, a, b, w0, fa, b, w0, w1, a, w1, f2, fa, w2, fa, w2, b,
            fa, a, f2, a, w1, b, w0, fa, w2, f2, b,
        )
    else:
        order = (
            a, b, a, w0, b, a, w1, b, w0, w2, w2, a, a, w2, w1, w1, b, w0,
            b,
        )
    run(order)
    for copy in saved + list(busy.values()):
        copy.wait()


def attn_back_kernel2(cfg, l, r):
    layers, seqs, block, width, heads, units, share = cfg
    net = Rows(r)
    c, t = net.c, net.t
    part = 4 * share
    keep = pl.ds(pl.multiple_of(net.x * part, LANES), part)
    away = pl.ds(pl.multiple_of((1 - net.x) * part, LANES), part)
    net.barrier()
    loads = []
    for s in range(seqs):
        loads.append([net.local(r.dy_i.at[s], r.dy.at[s])])
        if s == 0:
            loads[0].append(net.local(r.wa_i.at[l], r.wa))
        for src, dst in ((r.q_i, r.q), (r.kv_i, r.kv), (r.att_i, r.att), (r.lse_i, r.lse)):
            loads[s].append(net.local(src.at[l, s], dst.at[s]))
    x, f0, f1, f2 = ffn_sums(net, cfg, 1 if l else 0)
    run((x,))
    state = [net.local(r.grad_i, r.grad), net.local(r.base_i.at[l - 1] if l else r.base_i, r.base)]
    state += [net.local(r.rows_i.at[l, s], r.rows.at[s]) for s in range(seqs)]
    r.gs_o[...] = r.gs_i[...]
    gain = r.gain[l : l + 1]
    saved = []

    def sequence(s):
        for copy in loads[s]:
            copy.wait()
        attn_back_body(
            heads, c, t, r.prefix[s], r.dy.at[s], r.wa, r.q.at[s], r.kv.at[s], r.att.at[s],
            r.lse.at[s], r.cos, r.sin, r.dqkv.at[s], r.dkv.at[s], r.do_s, r.de_s, r.dqt_s, r.dk_s, r.dv_s,
        )
        lands = [r.dz.at[k, s] for k in range(4)]
        sums = net.sum_tp([r.dkv.at[s, m] for m in range(4)], lands)
        yield
        net.sum_tp_on(sums, r.dkv.at[s, 2], lands[2])
        yield
        r.dt[...] = net.sum_tp_end(sums, r.dkv.at[s, 0], lands)
        proj_back_body(heads, r.dt, r.wa, r.cos, r.sin, r.dqkv.at[s], r.pt.at[s])
        red = net.reduce_start(s)
        yield
        net.reduce_on(red, s)
        yield
        while state:
            state.pop().wait()
        net.norm_back(s, red, gain, l)
        saved.append(net.local(r.grad.at[s], r.grad_o.at[s]))
        if l:
            gather = net.gather_start(r.grad[s], s, r.dn)
        yield
        if l:
            net.gather_on(gather, s, r.dn)
            yield
            net.gather_end(gather)
            saved.append(net.local(r.dn.at[s], r.dn_o.at[s]))
            yield

    def weights(lefts, rights, cols, out, at):
        while state:
            state.pop().wait()
        low = lax.div(c * heads, GROUP)
        lf = [lefts.at[s] for s in range(seqs)]
        rg = [rights.at[s] for s in range(seqs)]
        for a, wide in chunks(lf[0].shape[-1]):
            total = None
            for left, right in zip(lf, rg):
                term = tn(
                    left[:, :, a : a + wide].reshape(4 * block, wide),
                    right[:, :, cols].reshape(4 * block, part),
                )
                total = term if total is None else total + term
            r.ws[a : a + wide] = total.astype(BF)
        for h in range(heads):
            side = (lax.div(c * heads + h, GROUP) - low) * D
            out[at + h * D : at + (h + 1) * D] = r.ws[pl.ds(pl.multiple_of(h * LANES + side, D), D)]
        if at == 0:
            out[2 * heads * D :] = r.ws[heads * LANES : (heads + 2) * LANES]

    def out_weights():
        weights(r.att, r.dy, away, r.wo.at[0], heads * D)
        yield
        weights(r.att, r.dy, keep, r.wo.at[1], heads * D)
        yield

    cross = []

    def qkv_weights():
        weights(r.dqkv, r.rows, away, r.wo.at[0], 0)
        yield
        cross.append(net.send(r.wo.at[0], r.dax_o if l else r.ax, DP))
        yield
        weights(r.dqkv, r.rows, keep, r.wo.at[1], 0)
        yield

    a, b, wo, wq = sequence(0), sequence(1), out_weights(), qkv_weights()
    if l:
        order = (
            f0, a, b, a, b, a, a, f1, b, wo, wq, b, a, f0, wq, wq, f1, b,
            f1, b, f0, wo, a, b, f1, f2, f2, wq, a, f0,
        )
    else:
        gn, fa = finish_gains(net), finish_attn(net, cfg, r.wo.at[1], r.ax, cross)
        order = (
            f0, a, b, a, wo, b, a, f1, b, wq, wq, wo, wq, f0, f2, b, b, f1,
            a, a, fa, f2, f2, gn, f0, fa, f1, fa, f0, gn, fa, fa, f2, gn, f1, gn,
            fa,
        )
    run(order)
    if l:
        saved.append(net.local(r.wo.at[1], r.dak_o))
        cross[0].wait()
    for copy in saved:
        copy.wait()


def backward_pass(cfg, tokens, prefix, cotangent, cos4, sin4, f):
    layers, seqs, block, width, heads, units, share = cfg
    keys, part = 4 * block, 4 * share
    rows = (seqs, 4, block, width)
    size = 2 * (heads + 1) * LANES
    compact = 2 * heads * D + 2 * LANES
    own = (seqs, block, width)
    hbm, vm = pl.ANY, pltpu.VMEM
    grads = ((8, width), F32, vm)
    common = dict(
        pt=(rows, BF), rn=((seqs, 2, block, width), BF), far=(own, BF), rf=(own, BF),
        grad=(own, F32), base=(own, F32), dy=(rows, BF),
    )
    kvs = (share, 2 * KEY_VALUE_HEADS * D)
    qos = (share, 2 * heads * D)
    one = (share, units)
    finish_out = dict(
        qo_o=(qos, F32, vm), kv_o=(kvs, F32, vm), u_o=(one, F32, vm)
    )
    finish_scratch = dict(
        ax=((compact, part), BF), at=((part, compact), BF),
        ac=((4, share, compact), BF), aq=((4, *qos), BF), az=((4, *qos), BF),
        av=(kvs, F32), asum=((3, *kvs), BF), al=((3, *kvs), BF),
    )
    mid_out = dict(
        dn_o=(rows, BF, hbm), dak_o=((compact, part), BF, hbm), dax_o=((compact, part), BF, hbm),
        fs_o=((units, part), BF, hbm), g_o=(one, F32, vm), d_o=(one, F32, vm),
    )
    grad, dy = cotangent.astype(F32), f.dy_o
    sums = jnp.zeros((8, width), F32)
    done, units_of = [None] * layers, [None] * layers
    number = 1
    d, finish_in = None, {}
    for l in reversed(range(layers)):
        tail = d is not None
        more = (finish_in, finish_out, finish_scratch) if tail else ({}, {}, {})
        c = launch(
            functools.partial(ffn_back_kernel2, cfg, l, tail),
            number,
            dict(
                dy_i=(dy, hbm), grad_i=(grad, hbm), base_i=(f.middle_o, hbm), gain=(f.gain_o, vm), wf_i=(f.wf_o, hbm),
                frows_i=(f.frows_o, hbm), gu_i=(f.gu_o, hbm), gs_i=(sums, vm), **more[0],
            ),
            dict(
                gs_o=grads, grad_o=(own, F32, hbm), dn_o=(rows, BF, hbm), dwk_o=((3, units, part), BF, hbm),
                dws_o=((2, units, part), BF, hbm), dwx_o=((units, part), BF, hbm), **more[1],
            ),
            dict(
                wf=((3, units, width), BF), frows=(rows, BF), gu=((seqs, 2, keys, units), BF), dn=(rows, BF),
                hgu=((seqs, 3, keys, units), BF), ws=((2, units, part), BF), wx=((units, part), BF),
                **(dict(ak=((compact, part), BF), fs=((1, units, part), BF), fz=((4, 1, units // 4, part), BF),
                fo=((units // 4, part), BF), ft=((1, part, units // 4), BF), fg=((1, 4, share, units // 4), BF)) if tail else {}), **common, **more[2],
            ),
        )
        if tail:
            done[l + 1] = c
            units_of[l + 1] = d
        base = f.stream_o if l else tokens.astype(F32)
        d = launch(
            functools.partial(attn_back_kernel2, cfg, l),
            number + 1,
            dict(
                prefix=(prefix, pltpu.SMEM), dy_i=(c.dn_o, hbm), grad_i=(c.grad_o, hbm), base_i=(base, hbm),
                gain=(f.gain_o, vm), wa_i=(f.wa_o, hbm), rows_i=(f.rows_o, hbm), q_i=(f.q_o, hbm), kv_i=(f.kv_o, hbm),
                att_i=(f.att_o, hbm), lse_i=(f.lse_o, hbm), cos=(cos4, vm), sin=(sin4, vm), gs_i=(c.gs_o, vm),
                dwk=(c.dwk_o, hbm), dws=(c.dws_o, hbm), dwx=(c.dwx_o, hbm),
            ),
            dict(
                gs_o=grads, grad_o=(own, F32, hbm),
                **(mid_out if l else dict(g_o=(one, F32, vm), d_o=(one, F32, vm), **finish_out)),
            ),
            dict(
                wa=((size, width), BF), q=((seqs, 4, heads, block, LANES), BF), kv=((seqs, 4, 4, block, 2 * LANES), BF),
                att=((seqs, 4, block, heads * LANES), BF), lse=((seqs, 4, 1, heads * block), F32), rows=(rows, BF),
                dqkv=((seqs, 4, block, (heads + 2) * LANES), BF), dkv=((seqs, 4, 4, block, 2 * LANES), BF),
                do_s=((4, heads * block, LANES), BF), de_s=((4, 1, heads * block), F32),
                dqt_s=((4, LANES, heads * block), F32), dk_s=((keys, LANES), F32), dv_s=((keys, LANES), F32),
                dz=((4, seqs, 4, block, 2 * LANES), BF), dt=((4, block, 2 * LANES), F32),
                ws=(((heads + 2) * LANES, part), BF), wo=((2, compact, part), BF),
                fs=((3, units, part), BF), fx=((3, units, part), BF), fz=((4, 3, units // 4, part), BF),
                fo=((units // 4, part), BF), ft=((3, part, units // 4), BF), fg=((3, 4, share, units // 4), BF),
                **(dict(dn=(rows, BF)) if l else dict(gt=((8, width), F32), gr=((3, 3, 8, width), F32), **finish_scratch)), **common,
            ),
            vmem=63,
        )
        number += 2
        grad, dy, sums = d.grad_o, d.dn_o if l else None, d.gs_o
        if l:
            finish_in = dict(dak=(d.dak_o, hbm), dax=(d.dax_o, hbm), fs_i=(d.fs_o, hbm))
    done[0] = units_of[0] = d
    return grad, done, units_of


def rms(v):
    r = lax.rsqrt(jnp.mean(v * v, axis=-1, keepdims=True) + EPS)
    return v * r, r


def per_device(
    tokens, prefix, w_query, key_weight, value_weight, w_out, w_gate, w_up, w_down, gain_attn, gain_ffn,
    cotangent,
):
    layers = w_query.shape[0]
    seqs, block, width = tokens.shape
    dps = lax.axis_size(DP)
    x, c, t = (lax.axis_index(a) for a in (DP, CTX, TP))
    heads = w_query.shape[2] // D
    share = w_query.shape[1]
    part = 4 * share
    units = w_gate.shape[2]
    quarter = units // 4
    low = (c * heads) // GROUP
    keys = 4 * block
    long = 4 * keys

    half = D // 2
    freq = jnp.exp(-math.log(10000.0) * jnp.arange(half).astype(F32) / half)
    at = ((c ^ jnp.arange(4)) * keys + t * block)[:, None] + jnp.arange(block)[None, :]
    angle = at.astype(F32).reshape(keys, 1) * freq[None, :]
    cos = jnp.tile(jnp.cos(angle), (1, 4))
    sin = jnp.sin(angle)
    sin = jnp.concatenate([-sin, sin, -sin, sin], axis=1)
    cos4, sin4 = cos.reshape(4, block, LANES), sin.reshape(4, block, LANES)
    scalars = [
        jnp.stack([c, t, prefix[s]]).astype(jnp.int32) for s in range(seqs)
    ]

    shards = jnp.stack([gain_attn, gain_ffn])
    gains = None if dps == 2 else lax.all_gather(shards, (DP, CTX), axis=2, tiled=True).astype(F32)

    def spread_dp(own):
        if dps == 2:
            other = lax.ppermute(own, DP, [(0, 1), (1, 0)])
            return jnp.concatenate(
                [jnp.where(x == 0, own, other), jnp.where(x == 0, other, own)], axis=-1
            )
        return lax.all_gather(own, DP, axis=own.ndim - 1, tiled=True)

    def attn_weights(l):
        qo = jnp.concatenate([w_query[l], w_out[l]], axis=1)
        slots = jnp.stack(tp_gather(qo))
        to_ctx = jnp.stack(
            [lax.dynamic_index_in_dim(slots, t ^ i, 0, keepdims=False) for i in range(4)]
        )
        got = ctx_exchange(to_ctx, True).reshape(part, 2 * heads * D).T
        kv = jnp.concatenate([key_weight[l], value_weight[l]], axis=1)
        kv = by_ctx(jnp.stack([kv] + [flip(kv, CTX, m) for m in (1, 2, 3)]))
        kv = kv.reshape(part, 2 * KEY_VALUE_HEADS * D).T
        k = lax.dynamic_slice_in_dim(kv, low * D, 2 * D, 0)
        v = lax.dynamic_slice_in_dim(kv, (KEY_VALUE_HEADS + low) * D, 2 * D, 0)
        own = jnp.concatenate([got[: heads * D], k, v, got[heads * D :]], axis=0)
        full = spread_dp(own)
        return call(
            functools.partial(pad_kernel, heads),
            [scalars[0], full],
            [((2 * (heads + 1) * LANES, width), BF)],
            smem=1,
        )[0]

    def ffn_weights(l):
        raw = jnp.concatenate([w_gate[l], w_up[l], w_down[l]], axis=0).T
        got = ctx_exchange(raw.reshape(4, quarter, 3 * share), True)
        own = jnp.transpose(got.reshape(4, quarter, 3, share), (2, 1, 0, 3)).reshape(
            3, quarter, part
        )
        slots = [spread_dp(s) for s in tp_gather(own)]
        return jnp.concatenate(slots, axis=1)

    if dps == 2:
        cfg = (layers, seqs, block, width, heads, units, share)
        small = jnp.pad(
            shards.astype(F32).reshape(2 * layers, share), ((0, 8 - 2 * layers), (0, 256 - share))
        )
        qo = jnp.concatenate([w_query, w_out], axis=2)
        kvw = jnp.concatenate([key_weight, value_weight], axis=2)
        fp = jnp.concatenate([w_gate, w_up, w_down], axis=1)
        fp = jnp.transpose(fp, (0, 2, 1)).reshape(layers, 4, quarter, 3 * share)
        f = forward_pass(cfg, tokens, cotangent, prefix, small, qo, kvw, fp, cos, sin)
        grad, done, fd = backward_pass(cfg, tokens, prefix, cotangent, cos4, sin4, f)
        wide = heads * D
        kd = KEY_VALUE_HEADS * D
        qo = jnp.stack([d.qo_o for d in done])
        kv = jnp.stack([d.kv_o for d in done])
        sums = lax.dynamic_slice_in_dim(done[0].gs_o, (x * 4 + c) * share, share, 1)
        return (
            f.out_o, grad, qo[:, :, :wide], kv[:, :, :kd], kv[:, :, kd:], qo[:, :, wide:],
            jnp.stack([d.g_o for d in fd]), jnp.stack([d.u_o for d in done]), jnp.stack([d.d_o for d in fd]),
            sums[:layers], sums[layers : 2 * layers],
        )
    watt = [None] * layers
    wffn = [None] * layers
    for l in range(layers):
        watt[l] = attn_weights(l)
        wffn[l] = ffn_weights(l)

    stream = [tokens[s].astype(F32) for s in range(seqs)]
    kept = {}
    for l in range(layers):
        for s in range(seqs):
            u, _ = rms(stream[s])
            pieces = ctx_gather((u * gains[0, l]).astype(BF))
            rows, q, kv = call(
                functools.partial(qkv_kernel, heads),
                [scalars[s], *pieces, watt[l], cos, sin],
                [((4, block, width), BF), ((4, heads, block, LANES), BF), ((4, block, 2 * LANES), BF)],
                smem=1,
                flops=2 * keys * width * (heads + 2) * LANES,
            )
            kvs = tp_gather(kv)
            att, lse, *parts = call(
                functools.partial(attn_kernel, heads),
                [scalars[s], q, *kvs, watt[l]],
                [((4, block, heads * LANES), BF), ((4, 1, heads * block), F32)] + [((block, width), BF)] * 4,
                smem=1,
                scratch=[
                    pltpu.VMEM((4, keys, LANES), BF),
                    pltpu.VMEM((4, LANES, keys), BF),
                    pltpu.VMEM((1, heads * block), F32),
                    pltpu.VMEM((1, heads * block), F32),
                    pltpu.VMEM((LANES, heads * block), F32),
                ],
                flops=2 * 2 * keys * long * heads * 256 * 0.7 + 2 * keys * heads * LANES * width,
                exps=keys * long * heads,
            )
            middle = stream[s] + ctx_reduce(parts)
            u, _ = rms(middle)
            pieces = ctx_gather((u * gains[1, l]).astype(BF))
            frows, gate, up, *parts = call(
                ffn_kernel,
                [*pieces, wffn[l]],
                [((4, block, width), BF)] + [((keys, units), BF)] * 2 + [((block, width), BF)] * 4,
                scratch=[pltpu.VMEM((keys, width), F32)],
                flops=2 * keys * width * units * 3,
            )
            kept[l, s] = (stream[s], rows, q, kvs, att, lse, middle, frows, gate, up)
            stream[s] = middle + ctx_reduce(parts)

    output = jnp.stack(stream).astype(BF)

    def norm_back(grad, local, v, gain):
        u, r = rms(v)
        e = local * gain
        grad = grad + r * (e - u * jnp.mean(e * u, axis=-1, keepdims=True))
        return grad, jnp.sum(local * u, axis=0)

    def weight_grad(lefts, rights):
        n = len(lefts)
        u_count = lefts[0].shape[-1]
        return call(
            functools.partial(weight_grad_kernel, dps if dps == 2 else 1, n),
            [a.reshape(keys, u_count) for a in lefts] + list(rights),
            [((u_count, width // dps), BF)] * 2 if dps == 2 else [((u_count, width), BF)],
            flops=2 * n * keys * u_count * width,
        )

    def collect_dp(halves):
        if dps == 2:
            mine = jnp.where(x == 0, halves[0], halves[1])
            other = jnp.where(x == 0, halves[1], halves[0])
            got = lax.ppermute(other, DP, [(0, 1), (1, 0)])
            return mine.astype(F32) + got.astype(F32)
        return lax.psum_scatter(
            halves[0], DP, scatter_dimension=halves[0].ndim - 1, tiled=True
        ).astype(F32)

    grads = {}

    def ffn_grads(l, lefts_rights):
        sums = [collect_dp(weight_grad(a, b)).reshape(4, quarter, part) for a, b in lefts_rights]
        slots = [jnp.stack([s[i] for s in sums]).astype(BF) for i in range(4)]
        own = tp_reduce(slots).reshape(3 * quarter, part).astype(BF)
        got = ctx_exchange(own.T.reshape(4, share, 3 * quarter), False).astype(F32)
        got = jnp.transpose(got.reshape(4, share, 3, quarter), (2, 1, 0, 3)).reshape(3, share, units)
        grads[l, "g"], grads[l, "u"], grads[l, "d"] = got[0], got[1], got[2]

    def attn_grads(l, dqkv, rows, att, drows):
        a = weight_grad(dqkv, rows)
        b = weight_grad(att, drows)
        halves = [
            call(
                functools.partial(unpad_kernel, heads),
                [scalars[0], i, j],
                [((2 * heads * D + 2 * LANES, i.shape[1]), BF)],
                smem=1,
            )[0]
            for i, j in zip(a, b)
        ]
        own = collect_dp(halves).astype(BF).T.reshape(4, share, 2 * heads * D + 2 * LANES)
        got = ctx_exchange(own, False)
        lo, hi = heads * D, heads * D + 2 * LANES
        qo = jnp.concatenate([got[:, :, :lo], got[:, :, hi:]], axis=-1)
        qo = [lax.dynamic_index_in_dim(qo, t ^ i, 0, keepdims=False) for i in range(4)]
        qo = tp_reduce(qo)
        grads[l, "q"], grads[l, "o"] = qo[:, :lo], qo[:, lo:]
        kv = got[:, :, lo:hi].astype(F32)
        both = []
        for first in (0, LANES):
            total = jnp.zeros((share, KEY_VALUE_HEADS * D), F32)
            for i in range(4):
                h = i * heads // GROUP
                term = kv[i, :, first : first + LANES]
                total = total + jnp.pad(term, ((0, 0), (h * D, (KEY_VALUE_HEADS - 2 - h) * D)))
            both.append(total)
        both = jnp.concatenate(both, axis=1)
        sent = both.astype(BF)
        for m in (1, 2, 3):
            both = both + flip(sent, TP, m).astype(F32)
        grads[l, "k"], grads[l, "v"] = (
            both[:, : KEY_VALUE_HEADS * D],
            both[:, KEY_VALUE_HEADS * D :],
        )

    grad = [cotangent[s].astype(F32) for s in range(seqs)]
    gain_sums = {}
    for l in reversed(range(layers)):
        hidden, dgate, dup, dy = [], [], [], []
        gain_sums[1, l] = 0.0
        gain_sums[0, l] = 0.0
        for s in range(seqs):
            _, _, _, _, _, _, middle, frows, gate, up = kept[l, s]
            drows, dg, du, hid, *parts = call(
                ffn_back_kernel,
                [*ctx_gather(grad[s].astype(BF)), wffn[l], gate, up],
                [((4, block, width), BF)] + [((keys, units), BF)] * 3 + [((block, width), BF)] * 4,
                scratch=[pltpu.VMEM((keys, width), F32)],
                flops=2 * keys * width * units * 3,
            )
            hidden.append(hid), dgate.append(dg), dup.append(du), dy.append(drows)
            grad[s], extra = norm_back(grad[s], ctx_reduce(parts), middle, gains[1, l])
            gain_sums[1, l] += extra
        ffn_grads(
            l,
            [
                (dgate, [kept[l, s][7] for s in range(seqs)]),
                (dup, [kept[l, s][7] for s in range(seqs)]),
                (hidden, dy),
            ],
        )
        dqkvs, dys = [], []
        for s in range(seqs):
            start, rows, q, kvs, att, lse, *_ = kept[l, s]
            drows, dq, *dkv = call(
                functools.partial(attn_back_kernel, heads),
                [scalars[s], *ctx_gather(grad[s].astype(BF)), watt[l], q, *kvs, att, lse, cos4, sin4],
                [((4, block, width), BF), ((4, block, heads * LANES), BF)] + [((4, block, 2 * LANES), BF)] * 4,
                smem=1,
                scratch=[
                    pltpu.VMEM((4, heads * block, LANES), BF),
                    pltpu.VMEM((4, 1, heads * block), F32),
                    pltpu.VMEM((4, LANES, heads * block), F32),
                    pltpu.VMEM((keys, LANES), F32),
                    pltpu.VMEM((keys, LANES), F32),
                ],
                flops=2 * 5 * keys * long * heads * 256 * 0.7 + 2 * keys * heads * LANES * width,
                exps=keys * long * heads,
            )
            one = flip(dkv[1], TP, 1)
            handed = lax.ppermute(dkv[3], TP, [(0, 1), (3, 2)])
            mid = lax.ppermute(dkv[3], TP, [(1, 2), (2, 1)])
            two = flip((dkv[2].astype(F32) + handed.astype(F32)).astype(BF), TP, 2)
            dqkv, *parts = call(
                functools.partial(proj_back_kernel, heads),
                [dkv[0], one, two, mid, dq, watt[l], cos4, sin4],
                [((4, block, (heads + 2) * LANES), BF)] + [((block, width), BF)] * 4,
                flops=2 * keys * (heads + 2) * LANES * width,
            )
            dqkvs.append(dqkv), dys.append(drows)
            grad[s], extra = norm_back(grad[s], ctx_reduce(parts), start, gains[0, l])
            gain_sums[0, l] += extra
        attn_grads(
            l,
            dqkvs,
            [kept[l, s][1] for s in range(seqs)],
            [kept[l, s][4] for s in range(seqs)],
            dys,
        )

    sums = jnp.stack([gain_sums[k, l] for k in range(2) for l in range(layers)])
    sums = lax.psum(sums, (DP, CTX, TP))
    sums = lax.dynamic_slice_in_dim(sums, (x * 4 + c) * share, share, 1).reshape(2, layers, share)

    def stacked(name):
        return jnp.stack([grads[l, name] for l in range(layers)])

    return (
        output,
        jnp.stack(grad),
        stacked("q"),
        stacked("k"),
        stacked("v"),
        stacked("o"),
        stacked("g"),
        stacked("u"),
        stacked("d"),
        sums[0],
        sums[1],
    )


def solution(mesh):
    rows = P(DP, (CTX, TP), None)
    sharded = P(None, (DP, CTX), TP)
    heads = P(None, (DP, CTX), None)
    gains = P(None, (DP, CTX))
    in_specs = (rows, P(DP), sharded, heads, heads, sharded, sharded, sharded, sharded, gains, gains, rows)
    out_specs = (rows, rows, sharded, heads, heads, sharded, sharded, sharded, sharded, gains, gains)
    return jax.shard_map(
        per_device, mesh=mesh, in_specs=in_specs, out_specs=out_specs, check_vma=False
    )
```

```python
import functools
import math
import types

import jax
import jax.numpy as jnp
from jax import lax
from jax.experimental import pallas as pl
from jax.experimental.pallas import tpu as pltpu
from jax.sharding import PartitionSpec as P

QUERY_HEADS = 20
KEY_VALUE_HEADS = 5
D = 64
GROUP = QUERY_HEADS // KEY_VALUE_HEADS
EPS = 1e-05
MASKED = -1e30
BF = jnp.bfloat16
F32 = jnp.float32
SLOTS = 4
LANES = 128
DP, CTX, TP = "dp", "ctx", "tp"
PREFIX_MAX = 1024


def nt(a, b):
    return lax.dot_general(a, b, (((1,), (1,)), ((), ())), preferred_element_type=F32)


def nn(a, b):
    return lax.dot_general(a, b, (((1,), (0,)), ((), ())), preferred_element_type=F32)


def tn(a, b):
    return lax.dot_general(a, b, (((0,), (0,)), ((), ())), preferred_element_type=F32)


def half_turn(x):
    lane = lax.broadcasted_iota(jnp.int32, x.shape, 1)
    return jnp.where((lane & 32) == 0, pltpu.roll(x, LANES - 32, 1), pltpu.roll(x, 32, 1))


def call(kernel, ins, outs, smem=0, scratch=(), flops=0, exps=0, vmem=56):
    total = sum(math.prod(a.shape) * a.dtype.itemsize for a in ins) + sum(
        math.prod(s) * jnp.dtype(d).itemsize for s, d in outs
    )
    return pl.pallas_call(
        kernel,
        out_shape=[jax.ShapeDtypeStruct(s, d) for s, d in outs],
        in_specs=[pl.BlockSpec(memory_space=pltpu.SMEM)] * smem
        + [pl.BlockSpec(memory_space=pltpu.VMEM)] * (len(ins) - smem),
        out_specs=[pl.BlockSpec(memory_space=pltpu.VMEM)] * len(outs),
        scratch_shapes=list(scratch),
        compiler_params=pltpu.CompilerParams(vmem_limit_bytes=vmem * 2**20),
        cost_estimate=pl.CostEstimate(
            flops=int(flops), bytes_accessed=int(total), transcendentals=int(exps)
        ),
    )(*ins)


def flip(x, axis, m):
    return lax.ppermute(x, axis, [(i, i ^ m) for i in range(4)])


def ctx_gather(x):
    far = flip(x, CTX, 2)
    return [x, flip(x, CTX, 1), far, flip(far, CTX, 1)]


def ctx_reduce(parts):
    far = (parts[2].astype(F32) + flip(parts[3], CTX, 1).astype(F32)).astype(BF)
    near = flip(parts[1], CTX, 1)
    return parts[0].astype(F32) + near.astype(F32) + flip(far, CTX, 2).astype(F32)


def inner(t):
    return (t == 1) | (t == 2)


def tp_gather(x):
    t = lax.axis_index(TP)
    two = flip(x, TP, 2)
    mid = lax.ppermute(x, TP, [(1, 2), (2, 1)])
    end = lax.ppermute(two, TP, [(1, 0), (2, 3)])
    return [x, flip(x, TP, 1), two, jnp.where(inner(t), mid, end)]


def tp_reduce(parts):
    one = flip(parts[1], TP, 1)
    handed = lax.ppermute(parts[3], TP, [(0, 1), (3, 2)])
    mid = lax.ppermute(parts[3], TP, [(1, 2), (2, 1)])
    two = flip((parts[2].astype(F32) + handed.astype(F32)).astype(BF), TP, 2)
    return (
        parts[0].astype(F32) + one.astype(F32) + two.astype(F32) + mid.astype(F32)
    )


def ctx_exchange(stacked, own_first):
    c = lax.axis_index(CTX)
    got = []
    for m in range(4):
        piece = lax.dynamic_index_in_dim(stacked, c ^ m, 0, keepdims=False)
        got.append(piece if m == 0 else flip(piece, CTX, m))
    return by_ctx(jnp.stack(got))


def by_ctx(stacked):
    c = lax.axis_index(CTX)
    return jnp.stack(
        [lax.dynamic_index_in_dim(stacked, c ^ i, 0, keepdims=False) for i in range(4)]
    )


def head_side(c, heads, h):
    return (c * heads + h) // GROUP - (c * heads) // GROUP


def qkv_kernel(heads, s_ref, x0, x1, x2, x3, w_ref, cos_ref, sin_ref, rows_o, q_o, kv_o):
    del s_ref
    block = x0.shape[0]
    for m, x in enumerate((x0, x1, x2, x3)):
        rows_o[m] = x[...]
    rows = rows_o[...].reshape(4 * block, x0.shape[1])
    cos, sin = cos_ref[...], sin_ref[...]
    at = 0
    total = (heads + 2) * LANES
    while at < total:
        width = min(3 * LANES, total - at)
        lin = nt(rows, w_ref[at : at + width])
        for j in range(width // LANES):
            slot = at // LANES + j
            v = lin[:, j * LANES : (j + 1) * LANES]
            if slot <= heads:
                v = v * cos + half_turn(v) * sin
            if slot < heads:
                v = (v * 0.125).astype(BF)
                for m in range(4):
                    q_o[m, slot] = v[m * block : (m + 1) * block]
            else:
                v = v.astype(BF)
                lo = (slot - heads) * LANES
                for m in range(4):
                    kv_o[m, :, lo : lo + LANES] = v[m * block : (m + 1) * block]
        at += width


def side_mask(c, heads, block):
    head = lax.broadcasted_iota(jnp.int32, (heads * block, LANES), 0) // block
    lane = lax.broadcasted_iota(jnp.int32, (heads * block, LANES), 1)
    return (lane // D) == ((c * heads + head) // GROUP - (c * heads) // GROUP)


def key_positions(t, block, first, count):
    row = lax.broadcasted_iota(jnp.int32, (count, 1), 0)
    return first + ((row // block) ^ t) * block + row % block


def attn_kernel(
    heads, s_ref, q_ref, k0, k1, k2, k3, w_ref, att_o, lse_o, p0, p1, p2, p3, k_s, vt_s, m_s, l_s, a_s
):
    c, t, prefix = s_ref[0], s_ref[1], s_ref[2]
    block = q_ref.shape[2]
    keys = 4 * block
    wide = heads * block
    for ck in range(4):
        m = c ^ ck
        v = jnp.concatenate([r[m, :, LANES:] for r in (k0, k1, k2, k3)], axis=0)
        vt_s[ck] = jnp.transpose(v.astype(F32)).astype(BF)
        for i, r in enumerate((k0, k1, k2, k3)):
            k_s[ck, i * block : (i + 1) * block] = r[m, :, :LANES]
    mask = side_mask(c, heads, block)
    q_at = lax.broadcasted_iota(jnp.int32, (1, wide), 1) % block + t * block

    for cq in range(4):
        m = c ^ cq
        q = q_ref[m].reshape(wide, LANES)
        m_s[...] = jnp.full_like(m_s, MASKED)
        l_s[...] = jnp.zeros_like(l_s)
        a_s[...] = jnp.zeros_like(a_s)

        def step(ck, q=q, cq=cq):
            s = nt(k_s[ck], q)
            if ck >= cq:
                at = key_positions(t, block, ck * keys, keys)
                seen = (at <= q_at + cq * keys) | (at < prefix)
                s = jnp.where(seen, s, MASKED)
            old = m_s[...]
            top = jnp.maximum(old, jnp.max(s, axis=0, keepdims=True))
            p = jnp.exp(s - top)
            decay = jnp.exp(old - top)
            l_s[...] = l_s[...] * decay + jnp.sum(p, axis=0, keepdims=True)
            a_s[...] = a_s[...] * decay + nn(vt_s[ck], p.astype(BF))
            m_s[...] = top

        for ck in range(4):
            if ck <= cq:
                step(ck)
            else:
                pl.when(ck * keys < prefix)(functools.partial(step, ck))
        o = jnp.transpose(a_s[...] / l_s[...])
        o = jnp.where(mask, o, 0.0).astype(BF)
        for h in range(heads):
            att_o[m, :, h * LANES : (h + 1) * LANES] = o[h * block : (h + 1) * block]
        lse_o[cq] = m_s[...] + jnp.log(l_s[...])
    full = att_o[...].reshape(4 * block, heads * LANES)
    w_at = (heads + 2) * LANES
    part = nn(full, w_ref[w_at : w_at + heads * LANES]).astype(BF)
    for m, r in enumerate((p0, p1, p2, p3)):
        r[...] = part[m * block : (m + 1) * block]


def attn_back_kernel(
    heads, s_ref, y0, y1, y2, y3, w_ref, q_ref, k0, k1, k2, k3, att_ref, lse_ref, cos_ref, sin_ref,
    rows_o, dq_o, g0, g1, g2, g3, do_s, de_s, dqt_s, dk_s, dv_s
):
    c, t, prefix = s_ref[0], s_ref[1], s_ref[2]
    block = q_ref.shape[2]
    keys = 4 * block
    wide = heads * block
    for m, y in enumerate((y0, y1, y2, y3)):
        rows_o[m] = y[...]
    w_at = (heads + 2) * LANES
    do = nt(rows_o[...].reshape(keys, y0.shape[1]), w_ref[w_at : w_at + heads * LANES]).astype(BF)
    for m in range(4):
        for h in range(heads):
            do_s[m, h * block : (h + 1) * block] = do[m * block : (m + 1) * block, h * LANES : (h + 1) * LANES]
    mask = side_mask(c, heads, block)
    for cq in range(4):
        m = c ^ cq
        a = att_ref[m]
        a = jnp.concatenate([a[:, h * LANES : (h + 1) * LANES] for h in range(heads)], axis=0)
        prod = a.astype(F32) * do_s[m].astype(F32)
        de_s[cq] = jnp.sum(jnp.transpose(prod), axis=0, keepdims=True)
    dqt_s[...] = jnp.zeros_like(dqt_s)
    q_at = lax.broadcasted_iota(jnp.int32, (1, wide), 1) % block + t * block
    for ck in range(4):
        mk = c ^ ck
        k = jnp.concatenate([r[mk, :, :LANES] for r in (k0, k1, k2, k3)], axis=0)
        v = jnp.concatenate([r[mk, :, LANES:] for r in (k0, k1, k2, k3)], axis=0)
        kt = jnp.transpose(k.astype(F32)).astype(BF)
        dk_s[...] = jnp.zeros_like(dk_s)
        dv_s[...] = jnp.zeros_like(dv_s)

        def step(cq, k=k, v=v, kt=kt, ck=ck):
            m = c ^ cq
            q = q_ref[m].reshape(wide, LANES)
            d_out = do_s[m]
            p = jnp.exp(nt(k, q) - lse_ref[cq])
            if ck >= cq:
                at = key_positions(t, block, ck * keys, keys)
                seen = (at <= q_at + cq * keys) | (at < prefix)
                p = jnp.where(seen, p, 0.0)
            ds = (p * (nt(v, d_out) - de_s[cq])).astype(BF)
            dk_s[...] += nn(ds, q)
            dv_s[...] += nn(p.astype(BF), d_out)
            dqt_s[cq] += nn(kt, ds)

        for cq in range(4):
            if cq >= ck:
                step(cq)
            else:
                pl.when(ck * keys < prefix)(functools.partial(step, cq))
        for i, r in enumerate((g0, g1, g2, g3)):
            r[mk, :, :LANES] = dk_s[i * block : (i + 1) * block].astype(BF)
            r[mk, :, LANES:] = dv_s[i * block : (i + 1) * block].astype(BF)
    for cq in range(4):
        m = c ^ cq
        dq = jnp.transpose(dqt_s[cq]) * 0.125
        turned = half_turn(dq)
        cos, sin = cos_ref[m], sin_ref[m]
        for h in range(heads):
            own = slice(h * block, (h + 1) * block)
            back = dq[own] * cos - turned[own] * sin
            dq_o[m, :, h * LANES : (h + 1) * LANES] = jnp.where(mask[own], back, 0.0).astype(BF)


def proj_back_kernel(heads, g0, g1, g2, g3, dq_ref, w_ref, cos_ref, sin_ref, d_o, p0, p1, p2, p3):
    block = dq_ref.shape[1]
    low = heads * LANES
    for m in range(4):
        d_o[m, :, :low] = dq_ref[m]
        total = (
            g0[m].astype(F32) + g1[m].astype(F32) + g2[m].astype(F32) + g3[m].astype(F32)
        )
        dk = total[:, :LANES]
        dk = dk * cos_ref[m] - half_turn(dk) * sin_ref[m]
        d_o[m, :, low : low + LANES] = dk.astype(BF)
        d_o[m, :, low + LANES :] = total[:, LANES:].astype(BF)
    full = d_o[...].reshape(4 * block, low + 2 * LANES)
    part = nn(full, w_ref[: low + 2 * LANES]).astype(BF)
    for m, r in enumerate((p0, p1, p2, p3)):
        r[...] = part[m * block : (m + 1) * block]


def chunks(width, step=256):
    return [(at, min(step, width - at)) for at in range(0, width, step)]


def ffn_kernel(x0, x1, x2, x3, w_ref, rows_o, gate_o, up_o, p0, p1, p2, p3, acc):
    block = x0.shape[0]
    for m, x in enumerate((x0, x1, x2, x3)):
        rows_o[m] = x[...]
    rows = rows_o[...].reshape(4 * block, x0.shape[1])
    for at, width in chunks(w_ref.shape[1]):
        g = nt(rows, w_ref[0, at : at + width])
        u = nt(rows, w_ref[1, at : at + width])
        gate_o[:, at : at + width] = g.astype(BF)
        up_o[:, at : at + width] = u.astype(BF)
        hidden = (g / (1.0 + jnp.exp(-g)) * u).astype(BF)
        term = nn(hidden, w_ref[2, at : at + width])
        if at == 0:
            acc[...] = term
        else:
            acc[...] += term
    for m, r in enumerate((p0, p1, p2, p3)):
        r[...] = acc[m * block : (m + 1) * block].astype(BF)


def ffn_back_kernel(
    y0, y1, y2, y3, w_ref, gate_ref, up_ref, rows_o, dg_o, du_o, h_o, p0, p1, p2, p3, acc
):
    block = y0.shape[0]
    for m, y in enumerate((y0, y1, y2, y3)):
        rows_o[m] = y[...]
    rows = rows_o[...].reshape(4 * block, y0.shape[1])
    for at, width in chunks(w_ref.shape[1]):
        own = slice(at, at + width)
        dh = nt(rows, w_ref[2, own])
        g = gate_ref[:, own].astype(F32)
        u = up_ref[:, own].astype(F32)
        s = 1.0 / (1.0 + jnp.exp(-g))
        dg = (dh * u * s * (1.0 + g * (1.0 - s))).astype(BF)
        du = (dh * g * s).astype(BF)
        dg_o[:, own] = dg
        du_o[:, own] = du
        h_o[:, own] = (g * s * u).astype(BF)
        term = nn(dg, w_ref[0, own]) + nn(du, w_ref[1, own])
        if at == 0:
            acc[...] = term
        else:
            acc[...] += term
    for m, r in enumerate((p0, p1, p2, p3)):
        r[...] = acc[m * block : (m + 1) * block].astype(BF)


def weight_grad_kernel(parts, count, *refs):
    lefts, rights, outs = refs[:count], refs[count : 2 * count], refs[2 * count :]
    cols = rights[0].shape[-1] // parts
    rows = lefts[0].shape[0]
    for x in range(parts):
        for at, width in chunks(lefts[0].shape[1]):
            total = None
            for left, right in zip(lefts, rights):
                r = right[:, :, x * cols : (x + 1) * cols].reshape(rows, cols)
                term = tn(left[:, at : at + width], r)
                total = term if total is None else total + term
            outs[x][at : at + width] = total.astype(BF)


def pad_kernel(heads, s_ref, w_ref, o_ref):
    c = s_ref[0]
    o_ref[...] = jnp.zeros_like(o_ref)
    for h in range(heads):
        side = head_side(c, heads, h) * D
        o_ref[pl.ds(pl.multiple_of(h * LANES + side, D), D)] = w_ref[h * D : (h + 1) * D]
        o_ref[pl.ds(pl.multiple_of((heads + 2 + h) * LANES + side, D), D)] = w_ref[
            heads * D + 2 * LANES + h * D : heads * D + 2 * LANES + (h + 1) * D
        ]
    o_ref[heads * LANES : (heads + 2) * LANES] = w_ref[heads * D : heads * D + 2 * LANES]


def unpad_kernel(heads, s_ref, a_ref, b_ref, o_ref):
    c = s_ref[0]
    for h in range(heads):
        at = pl.multiple_of(h * LANES + head_side(c, heads, h) * D, D)
        o_ref[h * D : (h + 1) * D] = a_ref[pl.ds(at, D)]
        lo = heads * D + 2 * LANES + h * D
        o_ref[lo : lo + D] = b_ref[pl.ds(at, D)]
    o_ref[heads * D : heads * D + 2 * LANES] = a_ref[heads * LANES : (heads + 2) * LANES]


def xor(a, b):
    return lax.rem(a + b, 2) + 2 * lax.rem(lax.div(a, 2) + lax.div(b, 2), 2)


class Net:
    def __init__(self, r):
        self.r = r
        self.sems = (r.send, r.recv, r.loc)
        self.remote, self.local_at = 0, 0
        self.x, self.c, self.t = (lax.axis_index(a) for a in (DP, CTX, TP))
        self.inner = (self.t == 1) | (self.t == 2)

    def barrier(self):
        sem = pltpu.get_barrier_semaphore()
        peers = [(CTX, 1), (CTX, 2), (CTX, 3), (TP, 1), (TP, 2), (TP, 3), (DP, 1)]
        for axis, m in peers:
            pl.semaphore_signal(
                sem, inc=1, device_id={axis: self.peer(axis, m)}, device_id_type=pl.DeviceIdType.MESH
            )
        pl.semaphore_wait(sem, len(peers))

    def peer(self, axis, m):
        if axis == DP:
            return 1 - self.x
        return xor(self.c if axis == CTX else self.t, m)

    def make(self, src, dst, axis, m):
        i = self.remote
        self.remote += 1
        return pltpu.make_async_remote_copy(
            src_ref=src,
            dst_ref=dst,
            send_sem=self.sems[0].at[i],
            recv_sem=self.sems[1].at[i],
            device_id={axis: self.peer(axis, m)},
            device_id_type=pl.DeviceIdType.MESH,
        )

    def send(self, src, dst, axis, m=1):
        copy = self.make(src, dst, axis, m)
        copy.start()
        return copy

    def local(self, src, dst):
        i = self.local_at
        self.local_at += 1
        copy = pltpu.make_async_copy(src, dst, self.sems[2].at[i])
        copy.start()
        return copy

    def close(self, copies):
        for copy in copies:
            copy.wait_send()

    def spread_tp(self, src, slots):
        two = self.send(src, slots[2], TP, 2)
        one = self.send(src, slots[1], TP, 1)
        mid = self.make(src, slots[3], TP, 3)
        end = self.make(slots[2], slots[3], TP, 1)
        return one, two, mid, end

    def spread_tp_on(self, copies):
        _, two, mid, end = copies
        two.wait_recv()

        @pl.when(self.inner)
        def _():
            end.start()
            mid.start()

    def spread_tp_last(self, copies):
        _, _, mid, end = copies
        pl.when(self.inner)(mid.wait_recv)
        pl.when(jnp.logical_not(self.inner))(end.wait_recv)

    def spread_tp_close(self, copies):
        one, two, mid, end = copies
        self.close([one, two])

        @pl.when(self.inner)
        def _():
            mid.wait_send()
            end.wait_send()


def run(tasks):
    for task in tasks:
        next(task, None)


def forward_kernel(cfg, r):
    layers, seqs, block, width, heads, units, share = cfg
    part, quarter, keys = 4 * share, units // 4, 4 * block
    net = Net(r)
    x, c, t = net.x, net.c, net.t
    low = lax.div(c * heads, GROUP)
    half = pl.ds(pl.multiple_of(x * part, LANES), part)
    prefix = [r.prefix[s] for s in range(seqs)]
    kept = []
    gu_copy = []

    net.barrier()

    def attn_weights(l):
        qz, qc, kvl, own, tmp, wa = r.qz.at[l], r.qc.at[l], r.kvl.at[l], r.own, r.tmp, r.wa
        mine = [net.local(r.qo.at[l], qz.at[0]), net.local(r.kvw.at[l], kvl.at[c])]
        tp = net.spread_tp(r.qo.at[l], [qz.at[i] for i in range(4)])
        kvs = [net.send(r.kvw.at[l], kvl.at[c], CTX, m) for m in (1, 2, 3)]
        wide = heads * LANES
        wa[l, :wide] = jnp.zeros((wide, width), BF)
        wa[l, wide + 2 * LANES :] = jnp.zeros((wide, width), BF)
        yield
        net.spread_tp_on(tp)
        yield
        mine[0].wait()
        tp[0].wait_recv()
        net.spread_tp_last(tp)
        mine.append(net.local(qz.at[xor(t, c)], qc.at[c]))
        ctx = [net.send(qz.at[xor(t, xor(c, m))], qc.at[c], CTX, m) for m in (1, 2, 3)]
        yield
        for copy in kvs + ctx:
            copy.wait_recv()
        mine[1].wait()
        mine[2].wait()
        stage = [net.local(qc, r.st_q), net.local(kvl, r.st_k)]
        stage[0].wait()
        for at in range(0, 2 * heads * D, LANES):
            got = jnp.transpose(r.st_q[:, :, at : at + LANES].reshape(part, LANES).astype(F32)).astype(BF)
            for k in range(0, LANES, D):
                to = at + k if at + k < heads * D else at + k + 2 * LANES
                own[to : to + D] = got[k : k + D]
        stage[1].wait()
        for at in range(0, 2 * KEY_VALUE_HEADS * D, LANES):
            got = r.st_k[:, :, at : at + LANES].reshape(part, LANES)
            tmp[at : at + LANES] = jnp.transpose(got.astype(F32)).astype(BF)
        own[heads * D : heads * D + LANES] = tmp[pl.ds(pl.multiple_of(low * D, D), LANES)]
        own[heads * D + LANES : heads * D + 2 * LANES] = tmp[
            pl.ds(pl.multiple_of((KEY_VALUE_HEADS + low) * D, D), LANES)
        ]
        dp = net.send(own, r.wc.at[l, :, half], DP)
        mine.append(net.local(own, r.wc.at[l, :, half]))
        yield
        dp.wait_recv()
        mine[3].wait()
        pads = []
        for h in range(heads):
            side = (lax.div(c * heads + h, GROUP) - low) * D
            for src, dst in ((h * D, h * LANES), (heads * D + 2 * LANES + h * D, (heads + 2 + h) * LANES)):
                pads.append(
                    net.local(
                        r.wc.at[l, src : src + D],
                        wa.at[l, pl.ds(pl.multiple_of(dst + side, D), D)],
                    )
                )
        pads.append(
            net.local(r.wc.at[l, heads * D : heads * D + 2 * LANES], wa.at[l, wide : wide + 2 * LANES])
        )
        yield
        for copy in pads:
            copy.wait()
        net.close(kvs + ctx + [dp])
        net.spread_tp_close(tp)
        kept.append(net.local(wa.at[l], r.wa_o.at[l]))
        yield

    def ffn_weights(l):
        fc, wf = r.fc.at[l], r.wf
        ctx = [net.send(r.fp.at[l, xor(c, m)], fc.at[c], CTX, m) for m in (1, 2, 3)]
        mine = net.local(r.fp.at[l, c], fc.at[c])
        yield
        for copy in ctx:
            copy.wait_recv()
        mine.wait()
        stage = net.local(fc, r.st_f)
        stage.wait()
        for i in range(3):
            piece = [r.st_f[k][:, i * share : (i + 1) * share] for k in range(4)]
            wf[l, i, :quarter, half] = jnp.concatenate(piece, axis=1)
        yield
        slots = [wf.at[l, :, i * quarter : (i + 1) * quarter, half] for i in range(4)]
        tp = net.spread_tp(slots[0], slots)
        dp = [net.send(slots[0], slots[0], DP)]
        yield
        net.spread_tp_on(tp)
        dp.append(net.send(slots[2], slots[2], DP))
        tp[0].wait_recv()
        dp.append(net.send(slots[1], slots[1], DP))
        yield
        net.spread_tp_last(tp)
        dp.append(net.send(slots[3], slots[3], DP))
        yield
        for copy in dp:
            copy.wait_recv()
        net.close(ctx + dp)
        net.spread_tp_close(tp)
        kept.append(net.local(wf.at[l], r.wf_o.at[l]))
        yield

    def gather_start(v, gain, s, rows):
        u = v * lax.rsqrt(jnp.mean(v * v, axis=-1, keepdims=True) + EPS)
        rows[s, 0] = (u * gain).astype(BF)
        return [
            net.send(rows.at[s, 0], rows.at[s, 2], CTX, 2),
            net.send(rows.at[s, 0], rows.at[s, 1], CTX, 1),
        ]

    def gather_on(copies, s, rows):
        copies[0].wait_recv()
        copies.append(net.send(rows.at[s, 2], rows.at[s, 3], CTX, 1))

    def gather_end(copies):
        copies[1].wait_recv()
        copies[2].wait_recv()

    def reduce_start(s):
        pt, rn = r.pt, r.rn
        return [
            net.send(pt.at[s, 3], rn.at[s, 1], CTX, 1),
            net.send(pt.at[s, 1], rn.at[s, 0], CTX, 1),
        ]

    def reduce_on(copies, s):
        copies[0].wait_recv()
        r.far[s] = (r.pt[s, 2].astype(F32) + r.rn[s, 1].astype(F32)).astype(BF)
        copies.append(net.send(r.far.at[s], r.rf.at[s], CTX, 2))

    def reduce_end(copies, s):
        copies[1].wait_recv()
        copies[2].wait_recv()
        total = r.pt[s, 0].astype(F32) + r.rn[s, 0].astype(F32) + r.rf[s].astype(F32)
        net.close(copies)
        return total

    def sequence(s):
        rows, frows, q, att, pt, gu = r.rows, r.frows, r.q, r.att, r.pt, r.gu
        carry = []
        for l in range(layers):
            kv = r.kv
            gather = gather_start(r.stream[s], r.gain[l : l + 1], s, rows)
            yield
            gather_on(gather, s, rows)
            yield
            gather_end(gather)
            tp = []
            qkv_body(
                heads, rows.at[s], r.wa.at[l], r.cos, r.sin, q.at[s], kv.at[l, s, 0],
                lambda: tp.append(net.spread_tp(kv.at[l, s, 0], [kv.at[l, s, i] for i in range(4)])),
            )
            tp = tp[0]
            outs = [net.local(rows.at[s], r.rows_o.at[l, s]), net.local(q.at[s], r.q_o.at[l, s])] + carry
            yield
            net.spread_tp_on(tp)
            yield
            tp[0].wait_recv()
            net.spread_tp_last(tp)
            outs.append(net.local(kv.at[l, s], r.kv_o.at[l, s]))
            attn_body(
                heads, c, t, prefix[s], q.at[s], kv.at[l, s], r.wa.at[l], att.at[s], r.lse.at[s],
                pt.at[s], r.k_s, r.vt_s, r.m_s, r.l_s, r.a_s,
            )
            reduce = reduce_start(s)
            outs.append(net.local(att.at[s], r.att_o.at[l, s]))
            outs.append(net.local(r.lse.at[s], r.lse_o.at[l, s]))
            net.close(gather)
            yield
            reduce_on(reduce, s)
            yield
            r.middle[s] = r.stream[s] + reduce_end(reduce, s)
            outs.append(net.local(r.middle.at[s], r.middle_o.at[l, s]))
            gather = gather_start(r.middle[s], r.gain[layers + l : layers + l + 1], s, frows)
            yield
            gather_on(gather, s, frows)
            yield
            gather_end(gather)
            outs.pop(0).wait()
            if gu_copy:
                gu_copy.pop().wait()
            ffn_body(frows.at[s], r.wf.at[l], gu, pt.at[s], r.hid)
            reduce = reduce_start(s)
            outs.append(net.local(frows.at[s], r.frows_o.at[l, s]))
            gu_copy.append(net.local(gu, r.gu_o.at[l, s]))
            net.close(gather)
            net.spread_tp_close(tp)
            yield
            reduce_on(reduce, s)
            yield
            for copy in outs:
                copy.wait()
            r.stream[s] = r.middle[s] + reduce_end(reduce, s)
            if l + 1 < layers:
                carry = [net.local(r.stream.at[s], r.stream_o.at[l, s])]
            else:
                r.far[s] = r.stream[s].astype(BF)
                kept.append(net.local(r.far.at[s], r.out_o.at[s]))
            yield

    gl = r.gl
    start = net.local(r.tokens, r.far)
    gl[x, c] = r.gains[...]
    near = [net.send(gl.at[x, c], gl.at[x, c], CTX, m) for m in (1, 2, 3)]
    (w0, w1), (f0, f1) = [attn_weights(l) for l in range(layers)], [ffn_weights(l) for l in range(layers)]
    run([f0, w0])
    start.wait()
    r.stream[...] = r.far[...].astype(F32)
    for copy in near:
        copy.wait_recv()
    over = net.send(gl.at[x], gl.at[x], DP)
    over.wait_recv()
    pieces = [gl[k, i][: 2 * layers, :share] for k in range(2) for i in range(4)]
    r.gain[...] = jnp.concatenate(pieces, axis=1)
    kept.append(net.local(r.gain, r.gain_o))

    def cotangent():
        cot, dy = r.cot, r.dy_o
        mine = [net.local(cot.at[s], dy.at[s, 0]) for s in range(seqs)]
        far = [net.send(cot.at[s], dy.at[s, 2], CTX, 2) for s in range(seqs)]
        side = [net.send(cot.at[s], dy.at[s, 1], CTX, 1) for s in range(seqs)]
        yield
        for s in range(seqs):
            far[s].wait_recv()
            side.append(net.send(dy.at[s, 2], dy.at[s, 3], CTX, 1))
        yield
        for copy in side:
            copy.wait_recv()
        for copy in mine:
            copy.wait()
        net.close(far + side)
        yield

    a, b, extra = sequence(0), sequence(1), cotangent()
    order = (
        w0, f0, f0, w0, w0, a, a, b, b, w1, w0, w0, a, w1, a, f0, f1, w1,
        a, a, b, a, f0, b, f1, w1, f1, a, b, f0, a, b, a, b, w1, a,
        f1, w1, b, a, b, b, a, f1, a, b, b, extra, a, b, b, a, extra, b,
        a, b, a, b, a, extra, f1, b, a, b, a, b, a, b, b,
    )
    run(order)
    net.close(near + [over])
    for copy in kept + gu_copy:
        copy.wait()


def qkv_body(heads, rows_ref, w_ref, cos_ref, sin_ref, q_o, kv_o, between=None):
    block, width = rows_ref.shape[1], rows_ref.shape[2]
    rows = rows_ref[...].reshape(4 * block, width)
    cos, sin = cos_ref[...], sin_ref[...]
    for at, wide in [(heads * LANES, 2 * LANES)] + chunks(heads * LANES):
        lin = nt(rows, w_ref[at : at + wide])
        for j in range(wide // LANES):
            slot = at // LANES + j
            v = lin[:, j * LANES : (j + 1) * LANES]
            if slot <= heads:
                v = v * cos + half_turn(v) * sin
            if slot < heads:
                v = (v * 0.125).astype(BF)
                for m in range(4):
                    q_o[m, slot] = v[m * block : (m + 1) * block]
            else:
                v = v.astype(BF)
                lo = (slot - heads) * LANES
                for m in range(4):
                    kv_o[m, :, lo : lo + LANES] = v[m * block : (m + 1) * block]
        if at == heads * LANES and between:
            between()


def attn_body(heads, c, t, prefix, q_ref, kv_ref, w_ref, att_o, lse_o, pt_o, k_s, vt_s, m_s, l_s, a_s):
    block = q_ref.shape[2]
    keys = 4 * block
    wide = heads * block
    for ck in range(4):
        m = xor(c, ck)
        v = jnp.concatenate([kv_ref[i, m, :, LANES:] for i in range(4)], axis=0)
        vt_s[ck] = jnp.transpose(v.astype(F32)).astype(BF)
        for i in range(4):
            k_s[ck, i * block : (i + 1) * block] = kv_ref[i, m, :, :LANES]
    mask = side_mask(c, heads, block)
    q_at = lax.broadcasted_iota(jnp.int32, (1, wide), 1) % block + t * block
    for cq in range(4):
        m = xor(c, cq)
        q_all = q_ref[m].reshape(wide, LANES)
        for first, span in chunks(wide, 3 * LANES):
            own = slice(first, first + span)
            q = q_all[own]
            for ck in range(4):
                if ck > cq and ck * keys >= PREFIX_MAX:
                    continue
                s = nt(k_s[ck], q)
                if ck >= cq:
                    at = key_positions(t, block, ck * keys, keys)
                    seen = (at <= q_at[:, own] + cq * keys) | (at < prefix)
                    s = jnp.where(seen, s, MASKED)
                top = jnp.max(s, axis=0, keepdims=True)
                if ck:
                    old = m_s[:, own]
                    top = jnp.maximum(old, top)
                    decay = jnp.exp(old - top)
                p = jnp.exp(s - top)
                add, term = jnp.sum(p, axis=0, keepdims=True), nn(vt_s[ck], p.astype(BF))
                l_s[:, own] = l_s[:, own] * decay + add if ck else add
                a_s[:, own] = a_s[:, own] * decay + term if ck else term
                m_s[:, own] = top
        o = jnp.transpose(a_s[...] / l_s[...])
        o = jnp.where(mask, o, 0.0).astype(BF)
        for h in range(heads):
            att_o[m, :, h * LANES : (h + 1) * LANES] = o[h * block : (h + 1) * block]
        lse_o[cq] = m_s[...] + jnp.log(l_s[...])
    full = att_o[...].reshape(4 * block, heads * LANES)
    w_at = (heads + 2) * LANES
    for at, span in chunks(w_ref.shape[1]):
        own = slice(at, at + span)
        part = nn(full, w_ref[w_at : w_at + heads * LANES, own]).astype(BF)
        for m in range(4):
            pt_o[m, :, own] = part[m * block : (m + 1) * block]


def ffn_body(rows_ref, w_ref, gu_o, pt_o, hid):
    block, width = rows_ref.shape[1], rows_ref.shape[2]
    rows = rows_ref[...].reshape(4 * block, width)
    for at, wide in chunks(w_ref.shape[1]):
        own = slice(at, at + wide)
        g = nt(rows, w_ref[0, own])
        u = nt(rows, w_ref[1, own])
        gu_o[0, :, own] = g.astype(BF)
        gu_o[1, :, own] = u.astype(BF)
        hid[:, own] = (g / (1.0 + jnp.exp(-g)) * u).astype(BF)
    for at, wide in chunks(width):
        own = slice(at, at + wide)
        part = nn(hid[...], w_ref[2, :, own]).astype(BF)
        for m in range(4):
            pt_o[m, :, own] = part[m * block : (m + 1) * block]


def launch(kernel, number, ins, outs, scratch, sems=(80, 90), vmem=62):
    sem = pltpu.SemaphoreType.DMA
    scratch = {k: pltpu.VMEM(*v) for k, v in scratch.items()}
    scratch.update(send=sem((sems[0],)), recv=sem((sems[0],)), loc=sem((sems[1],)))
    names = [*ins, *outs, *scratch]

    def body(*refs):
        kernel(types.SimpleNamespace(**dict(zip(names, refs))))

    got = pl.pallas_call(
        body,
        out_shape=[jax.ShapeDtypeStruct(v[0], v[1]) for v in outs.values()],
        in_specs=[pl.BlockSpec(memory_space=v[1]) for v in ins.values()],
        out_specs=[pl.BlockSpec(memory_space=v[2]) for v in outs.values()],
        scratch_shapes=list(scratch.values()),
        compiler_params=pltpu.CompilerParams(
            collective_id=number, has_side_effects=True, vmem_limit_bytes=vmem * 2**20
        ),
        cost_estimate=pl.CostEstimate(flops=10**11, bytes_accessed=10**8, transcendentals=10**7),
    )(*[v[0] for v in ins.values()])
    return types.SimpleNamespace(**dict(zip(outs, got)))


def forward_pass(cfg, tokens, cot, prefix, gains, qo, kvw, fp, cos, sin):
    layers, seqs, block, width, heads, units, share = cfg
    hbm, vm = pl.ANY, pltpu.VMEM
    keys, part = 4 * block, 4 * share
    rows = (seqs, 4, block, width)
    own = (seqs, block, width)
    size = 2 * (heads + 1) * LANES
    compact = 2 * heads * D + 2 * LANES
    q_s = (4, heads, block, LANES)
    kv_s = (4, 4, block, 2 * LANES)
    raw = (4, share, 2 * heads * D)
    raw_k = (4, share, 2 * KEY_VALUE_HEADS * D)
    raw_f = (4, units // 4, 3 * share)
    return launch(
        functools.partial(forward_kernel, cfg),
        0,
        dict(
            prefix=(prefix, pltpu.SMEM), tokens=(tokens, hbm), cot=(cot, hbm), gains=(gains, vm), qo=(qo, hbm),
            kvw=(kvw, hbm), fp=(fp, hbm), cos=(cos, vm), sin=(sin, vm),
        ),
        dict(
            out_o=(own, BF, hbm),
            wc=((layers, compact, width), BF, hbm),
            wa_o=((layers, size, width), BF, hbm),
            wf_o=((layers, 3, units, width), BF, hbm),
            rows_o=((layers, *rows), BF, hbm),
            q_o=((layers, seqs, *q_s), BF, hbm),
            kv_o=((layers, seqs, *kv_s), BF, hbm),
            att_o=((layers, seqs, 4, block, heads * LANES), BF, hbm),
            lse_o=((layers, seqs, 4, 1, heads * block), F32, hbm),
            middle_o=((layers, *own), F32, hbm),
            frows_o=((layers, *rows), BF, hbm),
            gu_o=((layers, seqs, 2, keys, units), BF, hbm),
            stream_o=((layers - 1, *own), F32, hbm),
            gain_o=((2 * layers, width), F32, hbm),
            dy_o=(rows, BF, hbm),
            qz=((layers, *raw), BF, hbm),
            qc=((layers, *raw), BF, hbm),
            kvl=((layers, *raw_k), BF, hbm),
            fc=((layers, *raw_f), BF, hbm),
        ),
        dict(
            stream=(own, F32),
            middle=(own, F32),
            rows=(rows, BF),
            frows=(rows, BF),
            q=((seqs, *q_s), BF),
            kv=((layers, seqs, *kv_s), BF),
            att=((seqs, 4, block, heads * LANES), BF),
            lse=((seqs, 4, 1, heads * block), F32),
            pt=(rows, BF),
            rn=((seqs, 2, block, width), BF),
            far=(own, BF),
            rf=(own, BF),
            gu=((2, keys, units), BF),
            hid=((keys, units), BF),
            k_s=((4, keys, LANES), BF),
            vt_s=((4, LANES, keys), BF),
            m_s=((1, heads * block), F32),
            l_s=((1, heads * block), F32),
            a_s=((LANES, heads * block), F32),
            wa=((layers, size, width), BF),
            wf=((layers, 3, units, width), BF),
            st_q=(raw, BF),
            st_k=(raw_k, BF),
            st_f=(raw_f, BF),
            own=((compact, part), BF),
            tmp=((2 * KEY_VALUE_HEADS * D, part), BF),
            gl=((2, 4, 8, 256), F32),
            gain=((2 * layers, width), F32),
        ),
        sems=(130, 110),
        vmem=63,
    )


class Rows(Net):
    def gather_start(self, v, s, rows):
        rows[s, 0] = v.astype(BF)
        return [
            self.send(rows.at[s, 0], rows.at[s, 2], CTX, 2),
            self.send(rows.at[s, 0], rows.at[s, 1], CTX, 1),
        ]

    def gather_on(self, copies, s, rows):
        copies[0].wait_recv()
        copies.append(self.send(rows.at[s, 2], rows.at[s, 3], CTX, 1))

    def gather_end(self, copies):
        copies[1].wait_recv()
        copies[2].wait_recv()
        self.close(copies)

    def reduce_start(self, s):
        pt, rn = self.r.pt, self.r.rn
        return [
            self.send(pt.at[s, 3], rn.at[s, 1], CTX, 1),
            self.send(pt.at[s, 1], rn.at[s, 0], CTX, 1),
        ]

    def reduce_on(self, copies, s):
        r = self.r
        copies[0].wait_recv()
        r.far[s] = (r.pt[s, 2].astype(F32) + r.rn[s, 1].astype(F32)).astype(BF)
        copies.append(self.send(r.far.at[s], r.rf.at[s], CTX, 2))

    def reduce_end(self, copies, s):
        r = self.r
        copies[1].wait_recv()
        copies[2].wait_recv()
        total = r.pt[s, 0].astype(F32) + r.rn[s, 0].astype(F32) + r.rf[s].astype(F32)
        self.close(copies)
        return total

    def norm_back(self, s, copies, gain, row):
        r = self.r
        local, v = self.reduce_end(copies, s), r.base[s]
        scale = lax.rsqrt(jnp.mean(v * v, axis=-1, keepdims=True) + EPS)
        u = v * scale
        e = local * gain
        r.grad[s] = r.grad[s] + scale * (e - u * jnp.mean(e * u, axis=-1, keepdims=True))
        r.gs_o[row : row + 1] += jnp.sum(local * u, axis=0, keepdims=True)

    def sum_tp(self, parts, lands):
        outer = jnp.logical_not(self.inner)
        one = self.make(parts[1], lands[0], TP, 1)
        two = self.make(parts[2], lands[1], TP, 2)
        hand = self.make(parts[3], lands[2], TP, 1)
        mid = self.make(parts[3], lands[3], TP, 3)

        @pl.when(outer)
        def _():
            hand.start()
            two.start()

        @pl.when(self.inner)
        def _():
            mid.start()
            one.start()

        return one, two, hand, mid

    def sum_tp_on(self, copies, part, land):
        one, two, hand, _ = copies
        pl.when(jnp.logical_not(self.inner))(one.start)

        @pl.when(self.inner)
        def _():
            hand.wait_recv()
            part[...] = (part[...].astype(F32) + land[...].astype(F32)).astype(BF)
            two.start()

    def sum_tp_end(self, copies, own, lands):
        one, two, hand, mid = copies
        outer = jnp.logical_not(self.inner)
        one.wait_recv()
        two.wait_recv()

        @pl.when(self.inner)
        def _():
            mid.wait_recv()
            mid.wait_send()

        @pl.when(outer)
        def _():
            lands[3][...] = jnp.zeros(lands[3].shape, lands[3].dtype)
            hand.wait_send()

        one.wait_send()
        two.wait_send()
        return (
            own[...].astype(F32)
            + lands[0][...].astype(F32)
            + lands[1][...].astype(F32)
            + lands[3][...].astype(F32)
        )


def ffn_back_body(rows_ref, w_ref, gu_ref, hgu, pt_o, waits, between=None):
    block, width = rows_ref.shape[1], rows_ref.shape[2]
    rows = rows_ref[...].reshape(4 * block, width)
    for at, wide in chunks(w_ref.shape[1]):
        own = slice(at, at + wide)
        dh = nt(rows, w_ref[2, own])
        g = gu_ref[0, :, own].astype(F32)
        u = gu_ref[1, :, own].astype(F32)
        s = 1.0 / (1.0 + jnp.exp(-g))
        hgu[0, :, own] = (g * s * u).astype(BF)
        hgu[1, :, own] = (dh * u * s * (1.0 + g * (1.0 - s))).astype(BF)
        hgu[2, :, own] = (dh * g * s).astype(BF)
    for copy in waits:
        copy.wait()
    if between:
        between()
    for at, wide in chunks(width):
        own = slice(at, at + wide)
        part = (nn(hgu[1], w_ref[0, :, own]) + nn(hgu[2], w_ref[1, :, own])).astype(BF)
        for m in range(4):
            pt_o[m, :, own] = part[m * block : (m + 1) * block]


def weight_grad_body(lefts, rights, cols, out):
    rows = lefts[0].shape[0]
    for at, wide in chunks(lefts[0].shape[1]):
        total = None
        for left, right in zip(lefts, rights):
            term = tn(left[:, at : at + wide], right[:, :, cols].reshape(rows, out.shape[1]))
            total = term if total is None else total + term
        out[at : at + wide] = total.astype(BF)


def attn_back_body(
    heads, c, t, prefix, rows_ref, w_ref, q_ref, kv_ref, att_ref, lse_ref, cos_ref, sin_ref, d_o, dkv_o,
    do_s, de_s, dqt_s, dk_s, dv_s
):
    block = q_ref.shape[2]
    keys = 4 * block
    wide = heads * block
    w_at = (heads + 2) * LANES
    rows = rows_ref[...].reshape(keys, rows_ref.shape[2])
    for at, span in chunks(wide):
        do = nt(rows, w_ref[w_at + at : w_at + at + span]).astype(BF)
        for m in range(4):
            for j in range(span // LANES):
                h = at // LANES + j
                do_s[m, h * block : (h + 1) * block] = do[
                    m * block : (m + 1) * block, j * LANES : (j + 1) * LANES
                ]
    mask = side_mask(c, heads, block)
    for cq in range(4):
        m = xor(c, cq)
        for h in range(heads):
            own = slice(h * block, (h + 1) * block)
            prod = att_ref[m, :, h * LANES : (h + 1) * LANES].astype(F32) * do_s[m, own].astype(F32)
            de_s[cq, :, own] = jnp.sum(jnp.transpose(prod), axis=0, keepdims=True)
    dqt_s[...] = jnp.zeros_like(dqt_s)
    q_at = lax.broadcasted_iota(jnp.int32, (1, wide), 1) % block + t * block
    for ck in range(4):
        mk = xor(c, ck)
        k = jnp.concatenate([kv_ref[i, mk, :, :LANES] for i in range(4)], axis=0)
        v = jnp.concatenate([kv_ref[i, mk, :, LANES:] for i in range(4)], axis=0)
        kt = jnp.transpose(k.astype(F32)).astype(BF)
        dk_s[...] = jnp.zeros_like(dk_s)
        dv_s[...] = jnp.zeros_like(dv_s)
        for cq in range(4):
            if ck > cq and ck * keys >= PREFIX_MAX:
                continue
            m = xor(c, cq)
            q_all = q_ref[m].reshape(wide, LANES)
            for first, span in chunks(wide, 3 * LANES):
                own = slice(first, first + span)
                q, d_out = q_all[own], do_s[m, own]
                p = jnp.exp(nt(k, q) - lse_ref[cq, :, own])
                if ck >= cq:
                    at = key_positions(t, block, ck * keys, keys)
                    seen = (at <= q_at[:, own] + cq * keys) | (at < prefix)
                    p = jnp.where(seen, p, 0.0)
                ds = (p * (nt(v, d_out) - de_s[cq, :, own])).astype(BF)
                dk_s[...] += nn(ds, q)
                dv_s[...] += nn(p.astype(BF), d_out)
                dqt_s[cq, :, own] += nn(kt, ds)
        for i in range(4):
            dkv_o[i, mk, :, :LANES] = dk_s[i * block : (i + 1) * block].astype(BF)
            dkv_o[i, mk, :, LANES:] = dv_s[i * block : (i + 1) * block].astype(BF)
    for cq in range(4):
        m = xor(c, cq)
        dq = jnp.transpose(dqt_s[cq]) * 0.125
        turned = half_turn(dq)
        cos, sin = cos_ref[m], sin_ref[m]
        for h in range(heads):
            own = slice(h * block, (h + 1) * block)
            back = dq[own] * cos - turned[own] * sin
            d_o[m, :, h * LANES : (h + 1) * LANES] = jnp.where(mask[own], back, 0.0).astype(BF)


def proj_back_body(heads, total, w_ref, cos_ref, sin_ref, d_o, pt_o):
    block = d_o.shape[1]
    low = heads * LANES
    for m in range(4):
        dk = total[m, :, :LANES]
        dk = dk * cos_ref[m] - half_turn(dk) * sin_ref[m]
        d_o[m, :, low : low + LANES] = dk.astype(BF)
        d_o[m, :, low + LANES :] = total[m, :, LANES:].astype(BF)
    full = d_o[...].reshape(4 * block, low + 2 * LANES)
    for at, span in chunks(w_ref.shape[1]):
        own = slice(at, at + span)
        part = nn(full, w_ref[: low + 2 * LANES, own]).astype(BF)
        for m in range(4):
            pt_o[m, :, own] = part[m * block : (m + 1) * block]


def ffn_sums(net, cfg, where):
    layers, seqs, block, width, heads, units, share = cfg
    quarter = units // 4
    r, c = net.r, net.c
    loads, sends = {}, {}

    def start():
        if where == 2:
            loads[1] = [net.local(r.fs_i, r.fs.at[0])]
        else:
            for i in (2, 0, 1):
                loads[i] = [net.local(r.dwk.at[i], r.fs.at[i])]
            loads[2].append(net.local(r.dwx, r.fx.at[2]))
            for i in (0, 1):
                sends[i] = net.send(r.dws.at[i], r.fx.at[i], DP)
        yield

    def one(i):
        at = 0 if where == 2 else i
        parts = [r.fs.at[at, m * quarter : (m + 1) * quarter] for m in range(4)]
        for copy in loads[i]:
            copy.wait()
        if i in sends:
            sends[i].wait_recv()
        if where != 2:
            for m in (3, 2, 1, 0):
                own = slice(m * quarter, (m + 1) * quarter)
                r.fs[i, own] = (r.fs[i, own].astype(F32) + r.fx[i, own].astype(F32)).astype(BF)
        if where == 1 and i == 1:
            out = net.local(r.fs.at[i], r.fs_o)
            yield
            out.wait()
            net.close(list(sends.values()))
            yield
        lands = [r.fz.at[k, at] for k in range(4)]
        sums = net.sum_tp(parts, lands)
        yield
        net.sum_tp_on(sums, parts[2], lands[2])
        yield
        r.fo[...] = net.sum_tp_end(sums, parts[0], lands).astype(BF)
        ft, fg = r.ft.at[at], r.fg.at[at]
        for first in range(0, 4 * share, LANES):
            ft[first : first + LANES] = jnp.transpose(r.fo[:, first : first + LANES].astype(F32)).astype(BF)
        out = [net.send(ft.at[piece(xor(c, m))], fg.at[c], CTX, m) for m in (1, 2, 3)]
        fg[c] = ft[piece(c)]
        yield
        for copy in out:
            copy.wait_recv()
        to = r.u_o if i == 1 else r.d_o if i else r.g_o
        to[...] = jnp.concatenate([fg[k].astype(F32) for k in range(4)], axis=1)
        net.close(out)
        if where == 0 and i in sends:
            net.close([sends[i]])
        yield

    def piece(i):
        return pl.ds(pl.multiple_of(i * share, 32), share)

    return start(), one(2), one(0), one(1)


def finish_out(net, cfg, mine, other, waits):
    layers, seqs, block, width, heads, units, share = cfg
    r = net.r
    c, t = net.c, net.t
    one = slice(heads * D, 2 * heads * D)
    for copy in waits:
        copy.wait()
    for at in range(0, 4 * share, LANES):
        own = slice(at, at + LANES)
        r.ot[own] = jnp.transpose(mine[one, own].astype(F32) + other[one, own].astype(F32)).astype(BF)

    def piece(i):
        return r.ot.at[pl.ds(pl.multiple_of(i * share, 32), share)]

    out = [net.send(piece(xor(c, m)), r.oc.at[c], CTX, m) for m in (1, 2, 3)]
    own = net.local(piece(c), r.oc.at[c])
    yield
    for copy in out:
        copy.wait_recv()
    own.wait()
    net.close(out)
    for m in range(4):
        r.oq[m] = r.oc[xor(t, m)]
    parts = [r.oq.at[m] for m in range(4)]
    lands = [r.oz.at[k] for k in range(4)]
    sums = net.sum_tp(parts, lands)
    yield
    net.sum_tp_on(sums, parts[2], lands[2])
    yield
    r.wo_o[...] = net.sum_tp_end(sums, parts[0], lands)
    yield


def finish_attn(net, cfg, mine, other, waits):
    layers, seqs, block, width, heads, units, share = cfg
    r = net.r
    c, t = net.c, net.t
    one, two = slice(0, heads * D), slice(2 * heads * D, 2 * heads * D + 2 * LANES)
    for copy in waits:
        copy.wait()
    for at in range(0, 4 * share, LANES):
        own = slice(at, at + LANES)
        for units_, to in ((two, slice(0, 2 * LANES)), (one, slice(2 * LANES, 2 * LANES + heads * D))):
            total = mine[units_, own].astype(F32) + other[units_, own].astype(F32)
            r.at[own, to] = jnp.transpose(total).astype(BF)

    def piece(i):
        return r.at.at[pl.ds(pl.multiple_of(i * share, 32), share)]

    out = [net.send(piece(xor(c, m)), r.ac.at[c], CTX, m) for m in (1, 2, 3)]
    own = net.local(piece(c), r.ac.at[c])
    yield
    for copy in out:
        copy.wait_recv()
    own.wait()
    net.close(out)
    for m in range(4):
        r.aq[m] = r.ac[xor(t, m), :, 2 * LANES :]
    parts = [r.aq.at[m] for m in range(4)]
    lands = [r.az.at[k] for k in range(4)]
    for first, at in ((0, 0), (KEY_VALUE_HEADS * D, LANES)):
        terms = []
        for h in range(KEY_VALUE_HEADS):
            total = None
            for i in range(4):
                j = h - i * heads // GROUP
                if j in (0, 1):
                    term = r.ac[i, :, at + j * D : at + (j + 1) * D].astype(F32)
                    total = term if total is None else total + term
            terms.append(total)
        r.av[:, first : first + KEY_VALUE_HEADS * D] = jnp.concatenate(terms, axis=1)
    outer = jnp.logical_not(net.inner)
    r.asum[0] = r.av[...].astype(BF)
    ends = net.make(r.asum.at[0], r.al.at[0], TP, 1)
    swap = net.make(r.asum.at[1], r.al.at[1], TP, 3)
    back = net.make(r.asum.at[2], r.al.at[2], TP, 1)
    pl.when(outer)(ends.start)
    sums = net.sum_tp(parts, lands)
    yield

    @pl.when(net.inner)
    def _():
        ends.wait_recv()
        r.asum[1] = (r.av[...] + r.al[0].astype(F32)).astype(BF)
        swap.start()

    yield
    net.sum_tp_on(sums, parts[2], lands[2])
    yield

    @pl.when(net.inner)
    def _():
        swap.wait_recv()
        r.asum[2] = (r.asum[1].astype(F32) + r.al[1].astype(F32)).astype(BF)
        back.start()

    yield
    r.wq_o[...] = net.sum_tp_end(sums, parts[0], lands)

    @pl.when(net.inner)
    def _():
        swap.wait_send()
        back.wait_send()
        r.kv_o[...] = r.asum[2].astype(F32)

    @pl.when(outer)
    def _():
        ends.wait_send()
        back.wait_recv()
        r.kv_o[...] = r.al[2].astype(F32)

    yield


def finish_gains(net):
    r = net.r
    r.gt[...] = r.gs_o[...]
    for k, axis in enumerate((CTX, TP, DP)):
        ms = (1, 2, 3) if axis != DP else (1,)
        copies = [net.send(r.gt, r.gr.at[k, m - 1], axis, m) for m in ms]
        yield
        for copy in copies:
            copy.wait_recv()
        net.close(copies)
        total = r.gt[...]
        for m in ms:
            total = total + r.gr[k, m - 1]
        r.gt[...] = total
    r.gs_o[...] = r.gt[...]
    yield


def ffn_back_kernel2(cfg, l, tail, r):
    layers, seqs, block, width, heads, units, share = cfg
    net = Rows(r)
    part = 4 * share
    keep = pl.ds(pl.multiple_of(net.x * part, LANES), part)
    away = pl.ds(pl.multiple_of((1 - net.x) * part, LANES), part)
    net.barrier()
    loads = [net.local(r.dak, r.ak), net.local(r.dax, r.ax)] if tail else []
    first = [net.local(r.dy_i.at[0], r.dy.at[0]), net.local(r.wf_i.at[l, 2], r.wf.at[2])]
    first.append(net.local(r.gu_i.at[l, 0], r.gu.at[0]))
    second = [net.local(r.wf_i.at[l, i], r.wf.at[i]) for i in (0, 1)]
    later = [net.local(r.dy_i.at[s], r.dy.at[s]) for s in range(1, seqs)]
    later += [net.local(r.gu_i.at[l, s], r.gu.at[s]) for s in range(1, seqs)]
    state = [net.local(r.grad_i, r.grad), net.local(r.base_i.at[l], r.base)]
    state += [net.local(r.frows_i.at[l, s], r.frows.at[s]) for s in range(seqs)]
    r.gs_o[...] = r.gs_i[...]
    row = layers + l
    gain = r.gain[row : row + 1]
    saved, busy = [], {}

    def sequence(s, waits, more):
        rows, hgu, pt = r.dy.at[s], r.hgu.at[s], r.pt.at[s]
        for copy in waits:
            copy.wait()
        ffn_back_body(rows, r.wf, r.gu.at[s], hgu, pt, more)
        red = net.reduce_start(s)
        yield
        net.reduce_on(red, s)
        yield
        while state:
            state.pop().wait()
        net.norm_back(s, red, gain, row)
        gather = net.gather_start(r.grad[s], s, r.dn)
        saved.append(net.local(r.grad.at[s], r.grad_o.at[s]))
        yield
        net.gather_on(gather, s, r.dn)
        yield
        net.gather_end(gather)
        saved.append(net.local(r.dn.at[s], r.dn_o.at[s]))
        yield

    def weights(i, to):
        lefts = [r.hgu.at[s, i] for s in range(seqs)]
        rights = [(r.frows if i else r.dy).at[s] for s in range(seqs)]
        while state:
            state.pop().wait()
        if i:
            if 0 in busy:
                busy.pop(0).wait()
            weight_grad_body(lefts, rights, away, r.ws.at[0])
            busy[0] = net.local(r.ws.at[0], r.dws_o.at[to])
        else:
            weight_grad_body(lefts, rights, away, r.wx)
            cross = net.send(r.wx, r.dwx_o, DP)
        yield
        if 1 in busy:
            busy.pop(1).wait()
        weight_grad_body(lefts, rights, keep, r.ws.at[1])
        busy[1] = net.local(r.ws.at[1], r.dwk_o.at[to])
        yield
        if not i:
            cross.wait()
        yield

    a, b = sequence(0, first, second), sequence(1, later, [])
    w0, w1, w2 = weights(0, 2), weights(1, 0), weights(2, 1)
    if tail:
        fa, fo = finish_attn(net, cfg, r.ak, r.ax, loads), finish_out(net, cfg, r.ak, r.ax, [])
        x, _, _, f2 = ffn_sums(net, cfg, 2)
        order = (
            x,
            fa, a, fo, f2, fa, a, b, w0, b, a, f2, w1, w1, w2, b, fo, fa, w2,
            w1, a, w2, fa, f2, fa, fo, b, w0, fo, fa, w0, a, f2, b,
        )
    else:
        order = (
            a, b, a, w0, b, a, w1, b, w0, w2, w2, a, a, w2, w1, w1, b, w0,
            b,
        )
    run(order)
    for copy in saved + list(busy.values()):
        copy.wait()


def attn_back_kernel2(cfg, l, r):
    layers, seqs, block, width, heads, units, share = cfg
    net = Rows(r)
    c, t = net.c, net.t
    part = 4 * share
    keep = pl.ds(pl.multiple_of(net.x * part, LANES), part)
    away = pl.ds(pl.multiple_of((1 - net.x) * part, LANES), part)
    net.barrier()
    loads = []
    for s in range(seqs):
        loads.append([net.local(r.dy_i.at[s], r.dy.at[s])])
        if s == 0:
            loads[0].append(net.local(r.wa_i.at[l], r.wa))
        for src, dst in ((r.q_i, r.q), (r.kv_i, r.kv), (r.att_i, r.att), (r.lse_i, r.lse)):
            loads[s].append(net.local(src.at[l, s], dst.at[s]))
    x, f0, f1, f2 = ffn_sums(net, cfg, 1 if l else 0)
    run((x,))
    state = [net.local(r.grad_i, r.grad), net.local(r.base_i.at[l - 1] if l else r.base_i, r.base)]
    state += [net.local(r.rows_i.at[l, s], r.rows.at[s]) for s in range(seqs)]
    r.gs_o[...] = r.gs_i[...]
    gain = r.gain[l : l + 1]
    saved = []

    def sequence(s):
        for copy in loads[s]:
            copy.wait()
        attn_back_body(
            heads, c, t, r.prefix[s], r.dy.at[s], r.wa, r.q.at[s], r.kv.at[s], r.att.at[s],
            r.lse.at[s], r.cos, r.sin, r.dqkv.at[s], r.dkv.at[s], r.do_s, r.de_s, r.dqt_s, r.dk_s, r.dv_s,
        )
        lands = [r.dz.at[k, s] for k in range(4)]
        sums = net.sum_tp([r.dkv.at[s, m] for m in range(4)], lands)
        yield
        net.sum_tp_on(sums, r.dkv.at[s, 2], lands[2])
        yield
        r.dt[...] = net.sum_tp_end(sums, r.dkv.at[s, 0], lands)
        proj_back_body(heads, r.dt, r.wa, r.cos, r.sin, r.dqkv.at[s], r.pt.at[s])
        red = net.reduce_start(s)
        yield
        net.reduce_on(red, s)
        yield
        while state:
            state.pop().wait()
        net.norm_back(s, red, gain, l)
        saved.append(net.local(r.grad.at[s], r.grad_o.at[s]))
        if l:
            gather = net.gather_start(r.grad[s], s, r.dn)
        yield
        if l:
            net.gather_on(gather, s, r.dn)
            yield
            net.gather_end(gather)
            saved.append(net.local(r.dn.at[s], r.dn_o.at[s]))
            yield

    def weights(lefts, rights, cols, out, at):
        while state:
            state.pop().wait()
        low = lax.div(c * heads, GROUP)
        lf = [lefts.at[s] for s in range(seqs)]
        rg = [rights.at[s] for s in range(seqs)]
        for a, wide in chunks(lf[0].shape[-1]):
            total = None
            for left, right in zip(lf, rg):
                term = tn(
                    left[:, :, a : a + wide].reshape(4 * block, wide),
                    right[:, :, cols].reshape(4 * block, part),
                )
                total = term if total is None else total + term
            r.ws[a : a + wide] = total.astype(BF)
        for h in range(heads):
            side = (lax.div(c * heads + h, GROUP) - low) * D
            out[at + h * D : at + (h + 1) * D] = r.ws[pl.ds(pl.multiple_of(h * LANES + side, D), D)]
        if at == 0:
            out[2 * heads * D :] = r.ws[heads * LANES : (heads + 2) * LANES]

    side, cross = [], []
    o_rows, q_rows, kv_rows = (
        slice(a * D, b * D) for a, b in ((heads, 2 * heads), (0, heads), (2 * heads, 2 * heads + 4))
    )

    def out_weights():
        weights(r.att, r.dy, away, r.wo.at[0], heads * D)
        if not l:
            side.append(net.send(r.wo.at[0, o_rows], r.ax.at[o_rows], DP))
        yield
        weights(r.att, r.dy, keep, r.wo.at[1], heads * D)
        yield

    def qkv_weights():
        weights(r.dqkv, r.rows, away, r.wo.at[0], 0)
        if l:
            yield
            cross.append(net.send(r.wo.at[0], r.dax_o, DP))
        else:
            cross.extend(net.send(r.wo.at[0, k], r.ax.at[k], DP) for k in (kv_rows, q_rows))
        yield
        weights(r.dqkv, r.rows, keep, r.wo.at[1], 0)
        yield

    a, b, wo, wq = sequence(0), sequence(1), out_weights(), qkv_weights()
    if l:
        order = (
            f0, a, b, a, b, a, a, f1, b, wo, wq, b, a, f0, wq, wq, f1, b,
            f1, b, f0, wo, a, b, f1, f2, f2, wq, a, f0,
        )
    else:
        gn, fa = finish_gains(net), finish_attn(net, cfg, r.wo.at[1], r.ax, cross)
        fo = finish_out(net, cfg, r.wo.at[1], r.ax, side)
        order = (
            f0, a, b, a, b, wo, f0, a, f2, b, wq, a, wq, f1, f0, b, f2, fa,
            wo, fo, f1, fa, a, b, gn, gn, f2, fo, fa, fa, f1, fa, fo, f2, gn, fa,
            f0, f1, gn, fo,
        )
    run(order)
    if l:
        saved.append(net.local(r.wo.at[1], r.dak_o))
        cross[0].wait()
    for copy in saved:
        copy.wait()


def backward_pass(cfg, tokens, prefix, cotangent, cos4, sin4, f):
    layers, seqs, block, width, heads, units, share = cfg
    keys, part = 4 * block, 4 * share
    rows = (seqs, 4, block, width)
    size = 2 * (heads + 1) * LANES
    compact = 2 * heads * D + 2 * LANES
    own = (seqs, block, width)
    hbm, vm = pl.ANY, pltpu.VMEM
    grads = ((8, width), F32, vm)
    common = dict(
        pt=(rows, BF), rn=((seqs, 2, block, width), BF), far=(own, BF), rf=(own, BF),
        grad=(own, F32), base=(own, F32), dy=(rows, BF),
    )
    kvs = (share, 2 * KEY_VALUE_HEADS * D)
    hs = (share, heads * D)
    mixed = 2 * LANES + heads * D
    one = (share, units)
    finish_out_ = dict(wq_o=(hs, F32, vm), wo_o=(hs, F32, vm), kv_o=(kvs, F32, vm), u_o=(one, F32, vm))
    finish_scratch = dict(
        ax=((compact, part), BF), at=((part, mixed), BF), ac=((4, share, mixed), BF), aq=((4, *hs), BF),
        az=((4, *hs), BF), av=(kvs, F32), asum=((3, *kvs), BF), al=((3, *kvs), BF),
        ot=((part, heads * D), BF), oc=((4, *hs), BF), oq=((4, *hs), BF), oz=((4, *hs), BF),
    )
    mid_out = dict(
        dn_o=(rows, BF, hbm), dak_o=((compact, part), BF, hbm), dax_o=((compact, part), BF, hbm),
        fs_o=((units, part), BF, hbm), g_o=(one, F32, vm), d_o=(one, F32, vm),
    )
    grad, dy = cotangent.astype(F32), f.dy_o
    sums = jnp.zeros((8, width), F32)
    done, units_of = [None] * layers, [None] * layers
    number = 1
    d, finish_in = None, {}
    for l in reversed(range(layers)):
        tail = d is not None
        more = (finish_in, finish_out_, finish_scratch) if tail else ({}, {}, {})
        c = launch(
            functools.partial(ffn_back_kernel2, cfg, l, tail),
            number,
            dict(
                dy_i=(dy, hbm), grad_i=(grad, hbm), base_i=(f.middle_o, hbm), gain=(f.gain_o, vm), wf_i=(f.wf_o, hbm),
                frows_i=(f.frows_o, hbm), gu_i=(f.gu_o, hbm), gs_i=(sums, vm), **more[0],
            ),
            dict(
                gs_o=grads, grad_o=(own, F32, hbm), dn_o=(rows, BF, hbm), dwk_o=((3, units, part), BF, hbm),
                dws_o=((2, units, part), BF, hbm), dwx_o=((units, part), BF, hbm), **more[1],
            ),
            dict(
                wf=((3, units, width), BF), frows=(rows, BF), gu=((seqs, 2, keys, units), BF), dn=(rows, BF),
                hgu=((seqs, 3, keys, units), BF), ws=((2, units, part), BF), wx=((units, part), BF),
                **(dict(ak=((compact, part), BF), fs=((1, units, part), BF), fz=((4, 1, units // 4, part), BF),
                fo=((units // 4, part), BF), ft=((1, part, units // 4), BF), fg=((1, 4, share, units // 4), BF)) if tail else {}), **common, **more[2],
            ),
        )
        if tail:
            done[l + 1] = c
            units_of[l + 1] = d
        base = f.stream_o if l else tokens.astype(F32)
        d = launch(
            functools.partial(attn_back_kernel2, cfg, l),
            number + 1,
            dict(
                prefix=(prefix, pltpu.SMEM), dy_i=(c.dn_o, hbm), grad_i=(c.grad_o, hbm), base_i=(base, hbm),
                gain=(f.gain_o, vm), wa_i=(f.wa_o, hbm), rows_i=(f.rows_o, hbm), q_i=(f.q_o, hbm), kv_i=(f.kv_o, hbm),
                att_i=(f.att_o, hbm), lse_i=(f.lse_o, hbm), cos=(cos4, vm), sin=(sin4, vm), gs_i=(c.gs_o, vm),
                dwk=(c.dwk_o, hbm), dws=(c.dws_o, hbm), dwx=(c.dwx_o, hbm),
            ),
            dict(
                gs_o=grads, grad_o=(own, F32, hbm),
                **(mid_out if l else dict(g_o=(one, F32, vm), d_o=(one, F32, vm), **finish_out_)),
            ),
            dict(
                wa=((size, width), BF), q=((seqs, 4, heads, block, LANES), BF), kv=((seqs, 4, 4, block, 2 * LANES), BF),
                att=((seqs, 4, block, heads * LANES), BF), lse=((seqs, 4, 1, heads * block), F32), rows=(rows, BF),
                dqkv=((seqs, 4, block, (heads + 2) * LANES), BF), dkv=((seqs, 4, 4, block, 2 * LANES), BF),
                do_s=((4, heads * block, LANES), BF), de_s=((4, 1, heads * block), F32),
                dqt_s=((4, LANES, heads * block), F32), dk_s=((keys, LANES), F32), dv_s=((keys, LANES), F32),
                dz=((4, seqs, 4, block, 2 * LANES), BF), dt=((4, block, 2 * LANES), F32),
                ws=(((heads + 2) * LANES, part), BF), wo=((2, compact, part), BF),
                fs=((3, units, part), BF), fx=((3, units, part), BF), fz=((4, 3, units // 4, part), BF),
                fo=((units // 4, part), BF), ft=((3, part, units // 4), BF), fg=((3, 4, share, units // 4), BF),
                **(dict(dn=(rows, BF)) if l else dict(gt=((8, width), F32), gr=((3, 3, 8, width), F32), **finish_scratch)), **common,
            ),
            vmem=63,
        )
        number += 2
        grad, dy, sums = d.grad_o, d.dn_o if l else None, d.gs_o
        if l:
            finish_in = dict(dak=(d.dak_o, hbm), dax=(d.dax_o, hbm), fs_i=(d.fs_o, hbm))
    done[0] = units_of[0] = d
    return grad, done, units_of


def rms(v):
    r = lax.rsqrt(jnp.mean(v * v, axis=-1, keepdims=True) + EPS)
    return v * r, r


def per_device(
    tokens, prefix, w_query, key_weight, value_weight, w_out, w_gate, w_up, w_down, gain_attn, gain_ffn,
    cotangent,
):
    layers = w_query.shape[0]
    seqs, block, width = tokens.shape
    dps = lax.axis_size(DP)
    x, c, t = (lax.axis_index(a) for a in (DP, CTX, TP))
    heads = w_query.shape[2] // D
    share = w_query.shape[1]
    part = 4 * share
    units = w_gate.shape[2]
    quarter = units // 4
    low = (c * heads) // GROUP
    keys = 4 * block
    long = 4 * keys

    half = D // 2
    freq = jnp.exp(-math.log(10000.0) * jnp.arange(half).astype(F32) / half)
    at = ((c ^ jnp.arange(4)) * keys + t * block)[:, None] + jnp.arange(block)[None, :]
    angle = at.astype(F32).reshape(keys, 1) * freq[None, :]
    cos = jnp.tile(jnp.cos(angle), (1, 4))
    sin = jnp.sin(angle)
    sin = jnp.concatenate([-sin, sin, -sin, sin], axis=1)
    cos4, sin4 = cos.reshape(4, block, LANES), sin.reshape(4, block, LANES)
    scalars = [
        jnp.stack([c, t, prefix[s]]).astype(jnp.int32) for s in range(seqs)
    ]

    shards = jnp.stack([gain_attn, gain_ffn])
    gains = None if dps == 2 else lax.all_gather(shards, (DP, CTX), axis=2, tiled=True).astype(F32)

    def spread_dp(own):
        if dps == 2:
            other = lax.ppermute(own, DP, [(0, 1), (1, 0)])
            return jnp.concatenate(
                [jnp.where(x == 0, own, other), jnp.where(x == 0, other, own)], axis=-1
            )
        return lax.all_gather(own, DP, axis=own.ndim - 1, tiled=True)

    def attn_weights(l):
        qo = jnp.concatenate([w_query[l], w_out[l]], axis=1)
        slots = jnp.stack(tp_gather(qo))
        to_ctx = jnp.stack(
            [lax.dynamic_index_in_dim(slots, t ^ i, 0, keepdims=False) for i in range(4)]
        )
        got = ctx_exchange(to_ctx, True).reshape(part, 2 * heads * D).T
        kv = jnp.concatenate([key_weight[l], value_weight[l]], axis=1)
        kv = by_ctx(jnp.stack([kv] + [flip(kv, CTX, m) for m in (1, 2, 3)]))
        kv = kv.reshape(part, 2 * KEY_VALUE_HEADS * D).T
        k = lax.dynamic_slice_in_dim(kv, low * D, 2 * D, 0)
        v = lax.dynamic_slice_in_dim(kv, (KEY_VALUE_HEADS + low) * D, 2 * D, 0)
        own = jnp.concatenate([got[: heads * D], k, v, got[heads * D :]], axis=0)
        full = spread_dp(own)
        return call(
            functools.partial(pad_kernel, heads),
            [scalars[0], full],
            [((2 * (heads + 1) * LANES, width), BF)],
            smem=1,
        )[0]

    def ffn_weights(l):
        raw = jnp.concatenate([w_gate[l], w_up[l], w_down[l]], axis=0).T
        got = ctx_exchange(raw.reshape(4, quarter, 3 * share), True)
        own = jnp.transpose(got.reshape(4, quarter, 3, share), (2, 1, 0, 3)).reshape(
            3, quarter, part
        )
        slots = [spread_dp(s) for s in tp_gather(own)]
        return jnp.concatenate(slots, axis=1)

    if dps == 2:
        cfg = (layers, seqs, block, width, heads, units, share)
        small = jnp.pad(
            shards.astype(F32).reshape(2 * layers, share), ((0, 8 - 2 * layers), (0, 256 - share))
        )
        qo = jnp.concatenate([w_query, w_out], axis=2)
        kvw = jnp.concatenate([key_weight, value_weight], axis=2)
        fp = jnp.concatenate([w_gate, w_up, w_down], axis=1)
        fp = jnp.transpose(fp, (0, 2, 1)).reshape(layers, 4, quarter, 3 * share)
        f = forward_pass(cfg, tokens, cotangent, prefix, small, qo, kvw, fp, cos, sin)
        grad, done, fd = backward_pass(cfg, tokens, prefix, cotangent, cos4, sin4, f)
        wide = heads * D
        kd = KEY_VALUE_HEADS * D
        kv = jnp.stack([d.kv_o for d in done])
        sums = lax.dynamic_slice_in_dim(done[0].gs_o, (x * 4 + c) * share, share, 1)
        return (
            f.out_o, grad, jnp.stack([d.wq_o for d in done]), kv[:, :, :kd], kv[:, :, kd:],
            jnp.stack([d.wo_o for d in done]),
            jnp.stack([d.g_o for d in fd]), jnp.stack([d.u_o for d in done]), jnp.stack([d.d_o for d in fd]),
            sums[:layers], sums[layers : 2 * layers],
        )
    watt = [None] * layers
    wffn = [None] * layers
    for l in range(layers):
        watt[l] = attn_weights(l)
        wffn[l] = ffn_weights(l)

    stream = [tokens[s].astype(F32) for s in range(seqs)]
    kept = {}
    for l in range(layers):
        for s in range(seqs):
            u, _ = rms(stream[s])
            pieces = ctx_gather((u * gains[0, l]).astype(BF))
            rows, q, kv = call(
                functools.partial(qkv_kernel, heads),
                [scalars[s], *pieces, watt[l], cos, sin],
                [((4, block, width), BF), ((4, heads, block, LANES), BF), ((4, block, 2 * LANES), BF)],
                smem=1,
                flops=2 * keys * width * (heads + 2) * LANES,
            )
            kvs = tp_gather(kv)
            att, lse, *parts = call(
                functools.partial(attn_kernel, heads),
                [scalars[s], q, *kvs, watt[l]],
                [((4, block, heads * LANES), BF), ((4, 1, heads * block), F32)] + [((block, width), BF)] * 4,
                smem=1,
                scratch=[
                    pltpu.VMEM((4, keys, LANES), BF),
                    pltpu.VMEM((4, LANES, keys), BF),
                    pltpu.VMEM((1, heads * block), F32),
                    pltpu.VMEM((1, heads * block), F32),
                    pltpu.VMEM((LANES, heads * block), F32),
                ],
                flops=2 * 2 * keys * long * heads * 256 * 0.7 + 2 * keys * heads * LANES * width,
                exps=keys * long * heads,
            )
            middle = stream[s] + ctx_reduce(parts)
            u, _ = rms(middle)
            pieces = ctx_gather((u * gains[1, l]).astype(BF))
            frows, gate, up, *parts = call(
                ffn_kernel,
                [*pieces, wffn[l]],
                [((4, block, width), BF)] + [((keys, units), BF)] * 2 + [((block, width), BF)] * 4,
                scratch=[pltpu.VMEM((keys, width), F32)],
                flops=2 * keys * width * units * 3,
            )
            kept[l, s] = (stream[s], rows, q, kvs, att, lse, middle, frows, gate, up)
            stream[s] = middle + ctx_reduce(parts)

    output = jnp.stack(stream).astype(BF)

    def norm_back(grad, local, v, gain):
        u, r = rms(v)
        e = local * gain
        grad = grad + r * (e - u * jnp.mean(e * u, axis=-1, keepdims=True))
        return grad, jnp.sum(local * u, axis=0)

    def weight_grad(lefts, rights):
        n = len(lefts)
        u_count = lefts[0].shape[-1]
        return call(
            functools.partial(weight_grad_kernel, dps if dps == 2 else 1, n),
            [a.reshape(keys, u_count) for a in lefts] + list(rights),
            [((u_count, width // dps), BF)] * 2 if dps == 2 else [((u_count, width), BF)],
            flops=2 * n * keys * u_count * width,
        )

    def collect_dp(halves):
        if dps == 2:
            mine = jnp.where(x == 0, halves[0], halves[1])
            other = jnp.where(x == 0, halves[1], halves[0])
            got = lax.ppermute(other, DP, [(0, 1), (1, 0)])
            return mine.astype(F32) + got.astype(F32)
        return lax.psum_scatter(
            halves[0], DP, scatter_dimension=halves[0].ndim - 1, tiled=True
        ).astype(F32)

    grads = {}

    def ffn_grads(l, lefts_rights):
        sums = [collect_dp(weight_grad(a, b)).reshape(4, quarter, part) for a, b in lefts_rights]
        slots = [jnp.stack([s[i] for s in sums]).astype(BF) for i in range(4)]
        own = tp_reduce(slots).reshape(3 * quarter, part).astype(BF)
        got = ctx_exchange(own.T.reshape(4, share, 3 * quarter), False).astype(F32)
        got = jnp.transpose(got.reshape(4, share, 3, quarter), (2, 1, 0, 3)).reshape(3, share, units)
        grads[l, "g"], grads[l, "u"], grads[l, "d"] = got[0], got[1], got[2]

    def attn_grads(l, dqkv, rows, att, drows):
        a = weight_grad(dqkv, rows)
        b = weight_grad(att, drows)
        halves = [
            call(
                functools.partial(unpad_kernel, heads),
                [scalars[0], i, j],
                [((2 * heads * D + 2 * LANES, i.shape[1]), BF)],
                smem=1,
            )[0]
            for i, j in zip(a, b)
        ]
        own = collect_dp(halves).astype(BF).T.reshape(4, share, 2 * heads * D + 2 * LANES)
        got = ctx_exchange(own, False)
        lo, hi = heads * D, heads * D + 2 * LANES
        qo = jnp.concatenate([got[:, :, :lo], got[:, :, hi:]], axis=-1)
        qo = [lax.dynamic_index_in_dim(qo, t ^ i, 0, keepdims=False) for i in range(4)]
        qo = tp_reduce(qo)
        grads[l, "q"], grads[l, "o"] = qo[:, :lo], qo[:, lo:]
        kv = got[:, :, lo:hi].astype(F32)
        both = []
        for first in (0, LANES):
            total = jnp.zeros((share, KEY_VALUE_HEADS * D), F32)
            for i in range(4):
                h = i * heads // GROUP
                term = kv[i, :, first : first + LANES]
                total = total + jnp.pad(term, ((0, 0), (h * D, (KEY_VALUE_HEADS - 2 - h) * D)))
            both.append(total)
        both = jnp.concatenate(both, axis=1)
        sent = both.astype(BF)
        for m in (1, 2, 3):
            both = both + flip(sent, TP, m).astype(F32)
        grads[l, "k"], grads[l, "v"] = (
            both[:, : KEY_VALUE_HEADS * D],
            both[:, KEY_VALUE_HEADS * D :],
        )

    grad = [cotangent[s].astype(F32) for s in range(seqs)]
    gain_sums = {}
    for l in reversed(range(layers)):
        hidden, dgate, dup, dy = [], [], [], []
        gain_sums[1, l] = 0.0
        gain_sums[0, l] = 0.0
        for s in range(seqs):
            _, _, _, _, _, _, middle, frows, gate, up = kept[l, s]
            drows, dg, du, hid, *parts = call(
                ffn_back_kernel,
                [*ctx_gather(grad[s].astype(BF)), wffn[l], gate, up],
                [((4, block, width), BF)] + [((keys, units), BF)] * 3 + [((block, width), BF)] * 4,
                scratch=[pltpu.VMEM((keys, width), F32)],
                flops=2 * keys * width * units * 3,
            )
            hidden.append(hid), dgate.append(dg), dup.append(du), dy.append(drows)
            grad[s], extra = norm_back(grad[s], ctx_reduce(parts), middle, gains[1, l])
            gain_sums[1, l] += extra
        ffn_grads(
            l,
            [
                (dgate, [kept[l, s][7] for s in range(seqs)]),
                (dup, [kept[l, s][7] for s in range(seqs)]),
                (hidden, dy),
            ],
        )
        dqkvs, dys = [], []
        for s in range(seqs):
            start, rows, q, kvs, att, lse, *_ = kept[l, s]
            drows, dq, *dkv = call(
                functools.partial(attn_back_kernel, heads),
                [scalars[s], *ctx_gather(grad[s].astype(BF)), watt[l], q, *kvs, att, lse, cos4, sin4],
                [((4, block, width), BF), ((4, block, heads * LANES), BF)] + [((4, block, 2 * LANES), BF)] * 4,
                smem=1,
                scratch=[
                    pltpu.VMEM((4, heads * block, LANES), BF),
                    pltpu.VMEM((4, 1, heads * block), F32),
                    pltpu.VMEM((4, LANES, heads * block), F32),
                    pltpu.VMEM((keys, LANES), F32),
                    pltpu.VMEM((keys, LANES), F32),
                ],
                flops=2 * 5 * keys * long * heads * 256 * 0.7 + 2 * keys * heads * LANES * width,
                exps=keys * long * heads,
            )
            one = flip(dkv[1], TP, 1)
            handed = lax.ppermute(dkv[3], TP, [(0, 1), (3, 2)])
            mid = lax.ppermute(dkv[3], TP, [(1, 2), (2, 1)])
            two = flip((dkv[2].astype(F32) + handed.astype(F32)).astype(BF), TP, 2)
            dqkv, *parts = call(
                functools.partial(proj_back_kernel, heads),
                [dkv[0], one, two, mid, dq, watt[l], cos4, sin4],
                [((4, block, (heads + 2) * LANES), BF)] + [((block, width), BF)] * 4,
                flops=2 * keys * (heads + 2) * LANES * width,
            )
            dqkvs.append(dqkv), dys.append(drows)
            grad[s], extra = norm_back(grad[s], ctx_reduce(parts), start, gains[0, l])
            gain_sums[0, l] += extra
        attn_grads(
            l,
            dqkvs,
            [kept[l, s][1] for s in range(seqs)],
            [kept[l, s][4] for s in range(seqs)],
            dys,
        )

    sums = jnp.stack([gain_sums[k, l] for k in range(2) for l in range(layers)])
    sums = lax.psum(sums, (DP, CTX, TP))
    sums = lax.dynamic_slice_in_dim(sums, (x * 4 + c) * share, share, 1).reshape(2, layers, share)

    def stacked(name):
        return jnp.stack([grads[l, name] for l in range(layers)])

    return (
        output,
        jnp.stack(grad),
        stacked("q"),
        stacked("k"),
        stacked("v"),
        stacked("o"),
        stacked("g"),
        stacked("u"),
        stacked("d"),
        sums[0],
        sums[1],
    )


def solution(mesh):
    rows = P(DP, (CTX, TP), None)
    sharded = P(None, (DP, CTX), TP)
    heads = P(None, (DP, CTX), None)
    gains = P(None, (DP, CTX))
    in_specs = (rows, P(DP), sharded, heads, heads, sharded, sharded, sharded, sharded, gains, gains, rows)
    out_specs = (rows, rows, sharded, heads, heads, sharded, sharded, sharded, sharded, gains, gains)
    return jax.shard_map(
        per_device, mesh=mesh, in_specs=in_specs, out_specs=out_specs, check_vma=False
    )
```

```python
import functools
import math
import types

import jax
import jax.numpy as jnp
from jax import lax
from jax.experimental import pallas as pl
from jax.experimental.pallas import tpu as pltpu
from jax.sharding import PartitionSpec as P

QUERY_HEADS = 20
KEY_VALUE_HEADS = 5
D = 64
GROUP = QUERY_HEADS // KEY_VALUE_HEADS
EPS = 1e-05
MASKED = -1e30
BF = jnp.bfloat16
F32 = jnp.float32
SLOTS = 4
LANES = 128
DP, CTX, TP = "dp", "ctx", "tp"
PREFIX_MAX = 1024


def nt(a, b):
    return lax.dot_general(a, b, (((1,), (1,)), ((), ())), preferred_element_type=F32)


def nn(a, b):
    return lax.dot_general(a, b, (((1,), (0,)), ((), ())), preferred_element_type=F32)


def tn(a, b):
    return lax.dot_general(a, b, (((0,), (0,)), ((), ())), preferred_element_type=F32)


def half_turn(x):
    lane = lax.broadcasted_iota(jnp.int32, x.shape, 1)
    return jnp.where((lane & 32) == 0, pltpu.roll(x, LANES - 32, 1), pltpu.roll(x, 32, 1))


def call(kernel, ins, outs, smem=0, scratch=(), flops=0, exps=0, vmem=56):
    total = sum(math.prod(a.shape) * a.dtype.itemsize for a in ins) + sum(
        math.prod(s) * jnp.dtype(d).itemsize for s, d in outs
    )
    return pl.pallas_call(
        kernel,
        out_shape=[jax.ShapeDtypeStruct(s, d) for s, d in outs],
        in_specs=[pl.BlockSpec(memory_space=pltpu.SMEM)] * smem
        + [pl.BlockSpec(memory_space=pltpu.VMEM)] * (len(ins) - smem),
        out_specs=[pl.BlockSpec(memory_space=pltpu.VMEM)] * len(outs),
        scratch_shapes=list(scratch),
        compiler_params=pltpu.CompilerParams(vmem_limit_bytes=vmem * 2**20),
        cost_estimate=pl.CostEstimate(
            flops=int(flops), bytes_accessed=int(total), transcendentals=int(exps)
        ),
    )(*ins)


def flip(x, axis, m):
    return lax.ppermute(x, axis, [(i, i ^ m) for i in range(4)])


def ctx_gather(x):
    far = flip(x, CTX, 2)
    return [x, flip(x, CTX, 1), far, flip(far, CTX, 1)]


def ctx_reduce(parts):
    far = (parts[2].astype(F32) + flip(parts[3], CTX, 1).astype(F32)).astype(BF)
    near = flip(parts[1], CTX, 1)
    return parts[0].astype(F32) + near.astype(F32) + flip(far, CTX, 2).astype(F32)


def inner(t):
    return (t == 1) | (t == 2)


def tp_gather(x):
    t = lax.axis_index(TP)
    two = flip(x, TP, 2)
    mid = lax.ppermute(x, TP, [(1, 2), (2, 1)])
    end = lax.ppermute(two, TP, [(1, 0), (2, 3)])
    return [x, flip(x, TP, 1), two, jnp.where(inner(t), mid, end)]


def tp_reduce(parts):
    one = flip(parts[1], TP, 1)
    handed = lax.ppermute(parts[3], TP, [(0, 1), (3, 2)])
    mid = lax.ppermute(parts[3], TP, [(1, 2), (2, 1)])
    two = flip((parts[2].astype(F32) + handed.astype(F32)).astype(BF), TP, 2)
    return (
        parts[0].astype(F32) + one.astype(F32) + two.astype(F32) + mid.astype(F32)
    )


def ctx_exchange(stacked, own_first):
    c = lax.axis_index(CTX)
    got = []
    for m in range(4):
        piece = lax.dynamic_index_in_dim(stacked, c ^ m, 0, keepdims=False)
        got.append(piece if m == 0 else flip(piece, CTX, m))
    return by_ctx(jnp.stack(got))


def by_ctx(stacked):
    c = lax.axis_index(CTX)
    return jnp.stack(
        [lax.dynamic_index_in_dim(stacked, c ^ i, 0, keepdims=False) for i in range(4)]
    )


def head_side(c, heads, h):
    return (c * heads + h) // GROUP - (c * heads) // GROUP


def qkv_kernel(heads, s_ref, x0, x1, x2, x3, w_ref, cos_ref, sin_ref, rows_o, q_o, kv_o):
    del s_ref
    block = x0.shape[0]
    for m, x in enumerate((x0, x1, x2, x3)):
        rows_o[m] = x[...]
    rows = rows_o[...].reshape(4 * block, x0.shape[1])
    cos, sin = cos_ref[...], sin_ref[...]
    at = 0
    total = (heads + 2) * LANES
    while at < total:
        width = min(3 * LANES, total - at)
        lin = nt(rows, w_ref[at : at + width])
        for j in range(width // LANES):
            slot = at // LANES + j
            v = lin[:, j * LANES : (j + 1) * LANES]
            if slot <= heads:
                v = v * cos + half_turn(v) * sin
            if slot < heads:
                v = (v * 0.125).astype(BF)
                for m in range(4):
                    q_o[m, slot] = v[m * block : (m + 1) * block]
            else:
                v = v.astype(BF)
                lo = (slot - heads) * LANES
                for m in range(4):
                    kv_o[m, :, lo : lo + LANES] = v[m * block : (m + 1) * block]
        at += width


def side_mask(c, heads, block):
    head = lax.broadcasted_iota(jnp.int32, (heads * block, LANES), 0) // block
    lane = lax.broadcasted_iota(jnp.int32, (heads * block, LANES), 1)
    return (lane // D) == ((c * heads + head) // GROUP - (c * heads) // GROUP)


def key_positions(t, block, first, count):
    row = lax.broadcasted_iota(jnp.int32, (count, 1), 0)
    return first + ((row // block) ^ t) * block + row % block


def attn_kernel(
    heads, s_ref, q_ref, k0, k1, k2, k3, w_ref, att_o, lse_o, p0, p1, p2, p3, k_s, vt_s, m_s, l_s, a_s
):
    c, t, prefix = s_ref[0], s_ref[1], s_ref[2]
    block = q_ref.shape[2]
    keys = 4 * block
    wide = heads * block
    for ck in range(4):
        m = c ^ ck
        v = jnp.concatenate([r[m, :, LANES:] for r in (k0, k1, k2, k3)], axis=0)
        vt_s[ck] = jnp.transpose(v.astype(F32)).astype(BF)
        for i, r in enumerate((k0, k1, k2, k3)):
            k_s[ck, i * block : (i + 1) * block] = r[m, :, :LANES]
    mask = side_mask(c, heads, block)
    q_at = lax.broadcasted_iota(jnp.int32, (1, wide), 1) % block + t * block

    for cq in range(4):
        m = c ^ cq
        q = q_ref[m].reshape(wide, LANES)
        m_s[...] = jnp.full_like(m_s, MASKED)
        l_s[...] = jnp.zeros_like(l_s)
        a_s[...] = jnp.zeros_like(a_s)

        def step(ck, q=q, cq=cq):
            s = nt(k_s[ck], q)
            if ck >= cq:
                at = key_positions(t, block, ck * keys, keys)
                seen = (at <= q_at + cq * keys) | (at < prefix)
                s = jnp.where(seen, s, MASKED)
            old = m_s[...]
            top = jnp.maximum(old, jnp.max(s, axis=0, keepdims=True))
            p = jnp.exp(s - top)
            decay = jnp.exp(old - top)
            l_s[...] = l_s[...] * decay + jnp.sum(p, axis=0, keepdims=True)
            a_s[...] = a_s[...] * decay + nn(vt_s[ck], p.astype(BF))
            m_s[...] = top

        for ck in range(4):
            if ck <= cq:
                step(ck)
            else:
                pl.when(ck * keys < prefix)(functools.partial(step, ck))
        o = jnp.transpose(a_s[...] / l_s[...])
        o = jnp.where(mask, o, 0.0).astype(BF)
        for h in range(heads):
            att_o[m, :, h * LANES : (h + 1) * LANES] = o[h * block : (h + 1) * block]
        lse_o[cq] = m_s[...] + jnp.log(l_s[...])
    full = att_o[...].reshape(4 * block, heads * LANES)
    w_at = (heads + 2) * LANES
    part = nn(full, w_ref[w_at : w_at + heads * LANES]).astype(BF)
    for m, r in enumerate((p0, p1, p2, p3)):
        r[...] = part[m * block : (m + 1) * block]


def attn_back_kernel(
    heads, s_ref, y0, y1, y2, y3, w_ref, q_ref, k0, k1, k2, k3, att_ref, lse_ref, cos_ref, sin_ref,
    rows_o, dq_o, g0, g1, g2, g3, do_s, de_s, dqt_s, dk_s, dv_s
):
    c, t, prefix = s_ref[0], s_ref[1], s_ref[2]
    block = q_ref.shape[2]
    keys = 4 * block
    wide = heads * block
    for m, y in enumerate((y0, y1, y2, y3)):
        rows_o[m] = y[...]
    w_at = (heads + 2) * LANES
    do = nt(rows_o[...].reshape(keys, y0.shape[1]), w_ref[w_at : w_at + heads * LANES]).astype(BF)
    for m in range(4):
        for h in range(heads):
            do_s[m, h * block : (h + 1) * block] = do[m * block : (m + 1) * block, h * LANES : (h + 1) * LANES]
    mask = side_mask(c, heads, block)
    for cq in range(4):
        m = c ^ cq
        a = att_ref[m]
        a = jnp.concatenate([a[:, h * LANES : (h + 1) * LANES] for h in range(heads)], axis=0)
        prod = a.astype(F32) * do_s[m].astype(F32)
        de_s[cq] = jnp.sum(jnp.transpose(prod), axis=0, keepdims=True)
    dqt_s[...] = jnp.zeros_like(dqt_s)
    q_at = lax.broadcasted_iota(jnp.int32, (1, wide), 1) % block + t * block
    for ck in range(4):
        mk = c ^ ck
        k = jnp.concatenate([r[mk, :, :LANES] for r in (k0, k1, k2, k3)], axis=0)
        v = jnp.concatenate([r[mk, :, LANES:] for r in (k0, k1, k2, k3)], axis=0)
        kt = jnp.transpose(k.astype(F32)).astype(BF)
        dk_s[...] = jnp.zeros_like(dk_s)
        dv_s[...] = jnp.zeros_like(dv_s)

        def step(cq, k=k, v=v, kt=kt, ck=ck):
            m = c ^ cq
            q = q_ref[m].reshape(wide, LANES)
            d_out = do_s[m]
            p = jnp.exp(nt(k, q) - lse_ref[cq])
            if ck >= cq:
                at = key_positions(t, block, ck * keys, keys)
                seen = (at <= q_at + cq * keys) | (at < prefix)
                p = jnp.where(seen, p, 0.0)
            ds = (p * (nt(v, d_out) - de_s[cq])).astype(BF)
            dk_s[...] += nn(ds, q)
            dv_s[...] += nn(p.astype(BF), d_out)
            dqt_s[cq] += nn(kt, ds)

        for cq in range(4):
            if cq >= ck:
                step(cq)
            else:
                pl.when(ck * keys < prefix)(functools.partial(step, cq))
        for i, r in enumerate((g0, g1, g2, g3)):
            r[mk, :, :LANES] = dk_s[i * block : (i + 1) * block].astype(BF)
            r[mk, :, LANES:] = dv_s[i * block : (i + 1) * block].astype(BF)
    for cq in range(4):
        m = c ^ cq
        dq = jnp.transpose(dqt_s[cq]) * 0.125
        turned = half_turn(dq)
        cos, sin = cos_ref[m], sin_ref[m]
        for h in range(heads):
            own = slice(h * block, (h + 1) * block)
            back = dq[own] * cos - turned[own] * sin
            dq_o[m, :, h * LANES : (h + 1) * LANES] = jnp.where(mask[own], back, 0.0).astype(BF)


def proj_back_kernel(heads, g0, g1, g2, g3, dq_ref, w_ref, cos_ref, sin_ref, d_o, p0, p1, p2, p3):
    block = dq_ref.shape[1]
    low = heads * LANES
    for m in range(4):
        d_o[m, :, :low] = dq_ref[m]
        total = (
            g0[m].astype(F32) + g1[m].astype(F32) + g2[m].astype(F32) + g3[m].astype(F32)
        )
        dk = total[:, :LANES]
        dk = dk * cos_ref[m] - half_turn(dk) * sin_ref[m]
        d_o[m, :, low : low + LANES] = dk.astype(BF)
        d_o[m, :, low + LANES :] = total[:, LANES:].astype(BF)
    full = d_o[...].reshape(4 * block, low + 2 * LANES)
    part = nn(full, w_ref[: low + 2 * LANES]).astype(BF)
    for m, r in enumerate((p0, p1, p2, p3)):
        r[...] = part[m * block : (m + 1) * block]


def chunks(width, step=256):
    return [(at, min(step, width - at)) for at in range(0, width, step)]


def ffn_kernel(x0, x1, x2, x3, w_ref, rows_o, gate_o, up_o, p0, p1, p2, p3, acc):
    block = x0.shape[0]
    for m, x in enumerate((x0, x1, x2, x3)):
        rows_o[m] = x[...]
    rows = rows_o[...].reshape(4 * block, x0.shape[1])
    for at, width in chunks(w_ref.shape[1]):
        g = nt(rows, w_ref[0, at : at + width])
        u = nt(rows, w_ref[1, at : at + width])
        gate_o[:, at : at + width] = g.astype(BF)
        up_o[:, at : at + width] = u.astype(BF)
        hidden = (g / (1.0 + jnp.exp(-g)) * u).astype(BF)
        term = nn(hidden, w_ref[2, at : at + width])
        if at == 0:
            acc[...] = term
        else:
            acc[...] += term
    for m, r in enumerate((p0, p1, p2, p3)):
        r[...] = acc[m * block : (m + 1) * block].astype(BF)


def ffn_back_kernel(
    y0, y1, y2, y3, w_ref, gate_ref, up_ref, rows_o, dg_o, du_o, h_o, p0, p1, p2, p3, acc
):
    block = y0.shape[0]
    for m, y in enumerate((y0, y1, y2, y3)):
        rows_o[m] = y[...]
    rows = rows_o[...].reshape(4 * block, y0.shape[1])
    for at, width in chunks(w_ref.shape[1]):
        own = slice(at, at + width)
        dh = nt(rows, w_ref[2, own])
        g = gate_ref[:, own].astype(F32)
        u = up_ref[:, own].astype(F32)
        s = 1.0 / (1.0 + jnp.exp(-g))
        dg = (dh * u * s * (1.0 + g * (1.0 - s))).astype(BF)
        du = (dh * g * s).astype(BF)
        dg_o[:, own] = dg
        du_o[:, own] = du
        h_o[:, own] = (g * s * u).astype(BF)
        term = nn(dg, w_ref[0, own]) + nn(du, w_ref[1, own])
        if at == 0:
            acc[...] = term
        else:
            acc[...] += term
    for m, r in enumerate((p0, p1, p2, p3)):
        r[...] = acc[m * block : (m + 1) * block].astype(BF)


def weight_grad_kernel(parts, count, *refs):
    lefts, rights, outs = refs[:count], refs[count : 2 * count], refs[2 * count :]
    cols = rights[0].shape[-1] // parts
    rows = lefts[0].shape[0]
    for x in range(parts):
        for at, width in chunks(lefts[0].shape[1]):
            total = None
            for left, right in zip(lefts, rights):
                r = right[:, :, x * cols : (x + 1) * cols].reshape(rows, cols)
                term = tn(left[:, at : at + width], r)
                total = term if total is None else total + term
            outs[x][at : at + width] = total.astype(BF)


def pad_kernel(heads, s_ref, w_ref, o_ref):
    c = s_ref[0]
    o_ref[...] = jnp.zeros_like(o_ref)
    for h in range(heads):
        side = head_side(c, heads, h) * D
        o_ref[pl.ds(pl.multiple_of(h * LANES + side, D), D)] = w_ref[h * D : (h + 1) * D]
        o_ref[pl.ds(pl.multiple_of((heads + 2 + h) * LANES + side, D), D)] = w_ref[
            heads * D + 2 * LANES + h * D : heads * D + 2 * LANES + (h + 1) * D
        ]
    o_ref[heads * LANES : (heads + 2) * LANES] = w_ref[heads * D : heads * D + 2 * LANES]


def unpad_kernel(heads, s_ref, a_ref, b_ref, o_ref):
    c = s_ref[0]
    for h in range(heads):
        at = pl.multiple_of(h * LANES + head_side(c, heads, h) * D, D)
        o_ref[h * D : (h + 1) * D] = a_ref[pl.ds(at, D)]
        lo = heads * D + 2 * LANES + h * D
        o_ref[lo : lo + D] = b_ref[pl.ds(at, D)]
    o_ref[heads * D : heads * D + 2 * LANES] = a_ref[heads * LANES : (heads + 2) * LANES]


def xor(a, b):
    return lax.rem(a + b, 2) + 2 * lax.rem(lax.div(a, 2) + lax.div(b, 2), 2)


class Net:
    def __init__(self, r):
        self.r = r
        self.sems = (r.send, r.recv, r.loc)
        self.remote, self.local_at = 0, 0
        self.x, self.c, self.t = (lax.axis_index(a) for a in (DP, CTX, TP))
        self.inner = (self.t == 1) | (self.t == 2)

    def barrier(self):
        sem = pltpu.get_barrier_semaphore()
        peers = [(CTX, 1), (CTX, 2), (CTX, 3), (TP, 1), (TP, 2), (TP, 3), (DP, 1)]
        for axis, m in peers:
            pl.semaphore_signal(
                sem, inc=1, device_id={axis: self.peer(axis, m)}, device_id_type=pl.DeviceIdType.MESH
            )
        pl.semaphore_wait(sem, len(peers))

    def peer(self, axis, m):
        if axis == DP:
            return 1 - self.x
        return xor(self.c if axis == CTX else self.t, m)

    def make(self, src, dst, axis, m):
        i = self.remote
        self.remote += 1
        return pltpu.make_async_remote_copy(
            src_ref=src,
            dst_ref=dst,
            send_sem=self.sems[0].at[i],
            recv_sem=self.sems[1].at[i],
            device_id={axis: self.peer(axis, m)},
            device_id_type=pl.DeviceIdType.MESH,
        )

    def send(self, src, dst, axis, m=1):
        copy = self.make(src, dst, axis, m)
        copy.start()
        return copy

    def local(self, src, dst):
        i = self.local_at
        self.local_at += 1
        copy = pltpu.make_async_copy(src, dst, self.sems[2].at[i])
        copy.start()
        return copy

    def close(self, copies):
        for copy in copies:
            copy.wait_send()

    def spread_tp(self, src, slots):
        two = self.send(src, slots[2], TP, 2)
        one = self.send(src, slots[1], TP, 1)
        mid = self.make(src, slots[3], TP, 3)
        end = self.make(slots[2], slots[3], TP, 1)
        return one, two, mid, end

    def spread_tp_on(self, copies):
        _, two, mid, end = copies
        two.wait_recv()

        @pl.when(self.inner)
        def _():
            end.start()
            mid.start()

    def spread_tp_last(self, copies):
        _, _, mid, end = copies
        pl.when(self.inner)(mid.wait_recv)
        pl.when(jnp.logical_not(self.inner))(end.wait_recv)

    def spread_tp_close(self, copies):
        one, two, mid, end = copies
        self.close([one, two])

        @pl.when(self.inner)
        def _():
            mid.wait_send()
            end.wait_send()


def run(tasks):
    for task in tasks:
        next(task, None)


def forward_kernel(cfg, r):
    layers, seqs, block, width, heads, units, share = cfg
    part, quarter, keys = 4 * share, units // 4, 4 * block
    net = Net(r)
    x, c, t = net.x, net.c, net.t
    low = lax.div(c * heads, GROUP)
    half = pl.ds(pl.multiple_of(x * part, LANES), part)
    prefix = [r.prefix[s] for s in range(seqs)]
    kept = []
    gu_copy = []

    net.barrier()

    def attn_weights(l):
        qz, qc, kvl, own, tmp, wa = r.qz.at[l], r.qc.at[l], r.kvl.at[l], r.own, r.tmp, r.wa
        mine = [net.local(r.qo.at[l], qz.at[0]), net.local(r.kvw.at[l], kvl.at[c])]
        tp = net.spread_tp(r.qo.at[l], [qz.at[i] for i in range(4)])
        kvs = [net.send(r.kvw.at[l], kvl.at[c], CTX, m) for m in (1, 2, 3)]
        wide = heads * LANES
        wa[l, :wide] = jnp.zeros((wide, width), BF)
        wa[l, wide + 2 * LANES :] = jnp.zeros((wide, width), BF)
        yield
        net.spread_tp_on(tp)
        yield
        mine[0].wait()
        tp[0].wait_recv()
        net.spread_tp_last(tp)
        mine.append(net.local(qz.at[xor(t, c)], qc.at[c]))
        ctx = [net.send(qz.at[xor(t, xor(c, m))], qc.at[c], CTX, m) for m in (1, 2, 3)]
        yield
        for copy in kvs + ctx:
            copy.wait_recv()
        mine[1].wait()
        mine[2].wait()
        stage = [net.local(qc, r.st_q), net.local(kvl, r.st_k)]
        stage[0].wait()
        for at in range(0, 2 * heads * D, LANES):
            got = jnp.transpose(r.st_q[:, :, at : at + LANES].reshape(part, LANES).astype(F32)).astype(BF)
            for k in range(0, LANES, D):
                to = at + k if at + k < heads * D else at + k + 2 * LANES
                own[to : to + D] = got[k : k + D]
        stage[1].wait()
        for at in range(0, 2 * KEY_VALUE_HEADS * D, LANES):
            got = r.st_k[:, :, at : at + LANES].reshape(part, LANES)
            tmp[at : at + LANES] = jnp.transpose(got.astype(F32)).astype(BF)
        own[heads * D : heads * D + LANES] = tmp[pl.ds(pl.multiple_of(low * D, D), LANES)]
        own[heads * D + LANES : heads * D + 2 * LANES] = tmp[
            pl.ds(pl.multiple_of((KEY_VALUE_HEADS + low) * D, D), LANES)
        ]
        dp = net.send(own, r.wc.at[l, :, half], DP)
        mine.append(net.local(own, r.wc.at[l, :, half]))
        yield
        dp.wait_recv()
        mine[3].wait()
        pads = []
        for h in range(heads):
            side = (lax.div(c * heads + h, GROUP) - low) * D
            for src, dst in ((h * D, h * LANES), (heads * D + 2 * LANES + h * D, (heads + 2 + h) * LANES)):
                pads.append(
                    net.local(
                        r.wc.at[l, src : src + D],
                        wa.at[l, pl.ds(pl.multiple_of(dst + side, D), D)],
                    )
                )
        pads.append(
            net.local(r.wc.at[l, heads * D : heads * D + 2 * LANES], wa.at[l, wide : wide + 2 * LANES])
        )
        yield
        for copy in pads:
            copy.wait()
        net.close(kvs + ctx + [dp])
        net.spread_tp_close(tp)
        kept.append(net.local(wa.at[l], r.wa_o.at[l]))
        yield

    def ffn_weights(l):
        fc, wf = r.fc.at[l], r.wf
        ctx = [net.send(r.fp.at[l, xor(c, m)], fc.at[c], CTX, m) for m in (1, 2, 3)]
        mine = net.local(r.fp.at[l, c], fc.at[c])
        yield
        for copy in ctx:
            copy.wait_recv()
        mine.wait()
        stage = net.local(fc, r.st_f)
        stage.wait()
        for i in range(3):
            piece = [r.st_f[k][:, i * share : (i + 1) * share] for k in range(4)]
            wf[l, i, :quarter, half] = jnp.concatenate(piece, axis=1)
        yield
        slots = [wf.at[l, :, i * quarter : (i + 1) * quarter, half] for i in range(4)]
        tp = net.spread_tp(slots[0], slots)
        dp = [net.send(slots[0], slots[0], DP)]
        yield
        net.spread_tp_on(tp)
        dp.append(net.send(slots[2], slots[2], DP))
        tp[0].wait_recv()
        dp.append(net.send(slots[1], slots[1], DP))
        yield
        net.spread_tp_last(tp)
        dp.append(net.send(slots[3], slots[3], DP))
        yield
        for copy in dp:
            copy.wait_recv()
        net.close(ctx + dp)
        net.spread_tp_close(tp)
        kept.append(net.local(wf.at[l], r.wf_o.at[l]))
        yield

    def gather_start(v, gain, s, rows):
        u = v * lax.rsqrt(jnp.mean(v * v, axis=-1, keepdims=True) + EPS)
        rows[s, 0] = (u * gain).astype(BF)
        return [
            net.send(rows.at[s, 0], rows.at[s, 2], CTX, 2),
            net.send(rows.at[s, 0], rows.at[s, 1], CTX, 1),
        ]

    def gather_on(copies, s, rows):
        copies[0].wait_recv()
        copies.append(net.send(rows.at[s, 2], rows.at[s, 3], CTX, 1))

    def gather_end(copies):
        copies[1].wait_recv()
        copies[2].wait_recv()

    def reduce_start(s):
        pt, rn = r.pt, r.rn
        return [
            net.send(pt.at[s, 3], rn.at[s, 1], CTX, 1),
            net.send(pt.at[s, 1], rn.at[s, 0], CTX, 1),
        ]

    def reduce_on(copies, s):
        copies[0].wait_recv()
        r.far[s] = (r.pt[s, 2].astype(F32) + r.rn[s, 1].astype(F32)).astype(BF)
        copies.append(net.send(r.far.at[s], r.rf.at[s], CTX, 2))

    def reduce_end(copies, s):
        copies[1].wait_recv()
        copies[2].wait_recv()
        total = r.pt[s, 0].astype(F32) + r.rn[s, 0].astype(F32) + r.rf[s].astype(F32)
        net.close(copies)
        return total

    def sequence(s):
        rows, frows, q, att, pt, gu = r.rows, r.frows, r.q, r.att, r.pt, r.gu
        carry = [net.local(r.stream.at[s], r.stream_o.at[0, s])]
        for l in range(layers):
            kv = r.kv
            gather = gather_start(r.stream[s], r.gain[l : l + 1], s, rows)
            yield
            gather_on(gather, s, rows)
            yield
            gather_end(gather)
            tp = []
            qkv_body(
                heads, rows.at[s], r.wa.at[l], r.cos, r.sin, q.at[s], kv.at[l, s, 0],
                lambda: tp.append(net.spread_tp(kv.at[l, s, 0], [kv.at[l, s, i] for i in range(4)])),
            )
            tp = tp[0]
            outs = [net.local(rows.at[s], r.rows_o.at[l, s]), net.local(q.at[s], r.q_o.at[l, s])] + carry
            yield
            net.spread_tp_on(tp)
            yield
            tp[0].wait_recv()
            net.spread_tp_last(tp)
            outs.append(net.local(kv.at[l, s], r.kv_o.at[l, s]))
            attn_body(
                heads, c, t, prefix[s], q.at[s], kv.at[l, s], r.wa.at[l], att.at[s], r.lse.at[s],
                pt.at[s], r.k_s, r.vt_s, r.m_s, r.l_s, r.a_s,
            )
            reduce = reduce_start(s)
            outs.append(net.local(att.at[s], r.att_o.at[l, s]))
            outs.append(net.local(r.lse.at[s], r.lse_o.at[l, s]))
            net.close(gather)
            yield
            reduce_on(reduce, s)
            yield
            r.middle[s] = r.stream[s] + reduce_end(reduce, s)
            outs.append(net.local(r.middle.at[s], r.middle_o.at[l, s]))
            gather = gather_start(r.middle[s], r.gain[layers + l : layers + l + 1], s, frows)
            yield
            gather_on(gather, s, frows)
            yield
            gather_end(gather)
            outs.pop(0).wait()
            if gu_copy:
                gu_copy.pop().wait()
            ffn_body(frows.at[s], r.wf.at[l], gu, pt.at[s], r.hid)
            reduce = reduce_start(s)
            outs.append(net.local(frows.at[s], r.frows_o.at[l, s]))
            gu_copy.append(net.local(gu, r.gu_o.at[l, s]))
            net.close(gather)
            net.spread_tp_close(tp)
            yield
            reduce_on(reduce, s)
            yield
            for copy in outs:
                copy.wait()
            r.stream[s] = r.middle[s] + reduce_end(reduce, s)
            if l + 1 < layers:
                carry = [net.local(r.stream.at[s], r.stream_o.at[l + 1, s])]
            else:
                r.far[s] = r.stream[s].astype(BF)
                kept.append(net.local(r.far.at[s], r.out_o.at[s]))
            yield

    gl = r.gl
    start = net.local(r.tokens, r.far)
    gl[x, c] = r.gains[...]
    near = [net.send(gl.at[x, c], gl.at[x, c], CTX, m) for m in (1, 2, 3)]
    (w0, w1), (f0, f1) = [attn_weights(l) for l in range(layers)], [ffn_weights(l) for l in range(layers)]
    run([f0, w0])
    start.wait()
    r.stream[...] = r.far[...].astype(F32)
    for copy in near:
        copy.wait_recv()
    over = net.send(gl.at[x], gl.at[x], DP)
    over.wait_recv()
    pieces = [gl[k, i][: 2 * layers, :share] for k in range(2) for i in range(4)]
    r.gain[...] = jnp.concatenate(pieces, axis=1)
    kept.append(net.local(r.gain, r.gain_o))

    def cotangent():
        cot, dy = r.cot, r.dy_o
        mine = [net.local(cot.at[s], dy.at[s, 0]) for s in range(seqs)]
        far = [net.send(cot.at[s], dy.at[s, 2], CTX, 2) for s in range(seqs)]
        side = [net.send(cot.at[s], dy.at[s, 1], CTX, 1) for s in range(seqs)]
        yield
        for s in range(seqs):
            far[s].wait_recv()
            side.append(net.send(dy.at[s, 2], dy.at[s, 3], CTX, 1))
        yield
        for copy in side:
            copy.wait_recv()
        for copy in mine:
            copy.wait()
        net.close(far + side)
        yield

    a, b, extra = sequence(0), sequence(1), cotangent()
    order = (
        w0, f0, f0, w0, w0, a, a, b, b, w1, w0, w0, a, w1, a, f0, f1, w1,
        a, a, b, a, f0, b, f1, w1, f1, a, b, f0, a, b, a, b, w1, a,
        f1, w1, b, a, b, b, a, f1, a, b, b, extra, a, b, b, a, extra, b,
        a, b, a, b, a, extra, f1, b, a, b, a, b, a, b, b,
    )
    run(order)
    net.close(near + [over])
    for copy in kept + gu_copy:
        copy.wait()


def qkv_body(heads, rows_ref, w_ref, cos_ref, sin_ref, q_o, kv_o, between=None):
    block, width = rows_ref.shape[1], rows_ref.shape[2]
    rows = rows_ref[...].reshape(4 * block, width)
    cos, sin = cos_ref[...], sin_ref[...]
    for at, wide in [(heads * LANES, 2 * LANES)] + chunks(heads * LANES):
        lin = nt(rows, w_ref[at : at + wide])
        for j in range(wide // LANES):
            slot = at // LANES + j
            v = lin[:, j * LANES : (j + 1) * LANES]
            if slot <= heads:
                v = v * cos + half_turn(v) * sin
            if slot < heads:
                v = (v * 0.125).astype(BF)
                for m in range(4):
                    q_o[m, slot] = v[m * block : (m + 1) * block]
            else:
                v = v.astype(BF)
                lo = (slot - heads) * LANES
                for m in range(4):
                    kv_o[m, :, lo : lo + LANES] = v[m * block : (m + 1) * block]
        if at == heads * LANES and between:
            between()


def attn_body(heads, c, t, prefix, q_ref, kv_ref, w_ref, att_o, lse_o, pt_o, k_s, vt_s, m_s, l_s, a_s):
    block = q_ref.shape[2]
    keys = 4 * block
    wide = heads * block
    for ck in range(4):
        m = xor(c, ck)
        v = jnp.concatenate([kv_ref[i, m, :, LANES:] for i in range(4)], axis=0)
        vt_s[ck] = jnp.transpose(v.astype(F32)).astype(BF)
        for i in range(4):
            k_s[ck, i * block : (i + 1) * block] = kv_ref[i, m, :, :LANES]
    mask = side_mask(c, heads, block)
    q_at = lax.broadcasted_iota(jnp.int32, (1, wide), 1) % block + t * block
    for cq in range(4):
        m = xor(c, cq)
        q_all = q_ref[m].reshape(wide, LANES)
        for first, span in chunks(wide, 3 * LANES):
            own = slice(first, first + span)
            q = q_all[own]
            for ck in range(4):
                if ck > cq and ck * keys >= PREFIX_MAX:
                    continue
                s = nt(k_s[ck], q)
                if ck >= cq:
                    at = key_positions(t, block, ck * keys, keys)
                    seen = (at <= q_at[:, own] + cq * keys) | (at < prefix)
                    s = jnp.where(seen, s, MASKED)
                top = jnp.max(s, axis=0, keepdims=True)
                if ck:
                    old = m_s[:, own]
                    top = jnp.maximum(old, top)
                    decay = jnp.exp(old - top)
                p = jnp.exp(s - top)
                add, term = jnp.sum(p, axis=0, keepdims=True), nn(vt_s[ck], p.astype(BF))
                l_s[:, own] = l_s[:, own] * decay + add if ck else add
                a_s[:, own] = a_s[:, own] * decay + term if ck else term
                m_s[:, own] = top
        o = jnp.transpose(a_s[...] / l_s[...])
        o = jnp.where(mask, o, 0.0).astype(BF)
        for h in range(heads):
            att_o[m, :, h * LANES : (h + 1) * LANES] = o[h * block : (h + 1) * block]
        lse_o[cq] = m_s[...] + jnp.log(l_s[...])
    full = att_o[...].reshape(4 * block, heads * LANES)
    w_at = (heads + 2) * LANES
    for at, span in chunks(w_ref.shape[1]):
        own = slice(at, at + span)
        part = nn(full, w_ref[w_at : w_at + heads * LANES, own]).astype(BF)
        for m in range(4):
            pt_o[m, :, own] = part[m * block : (m + 1) * block]


def ffn_body(rows_ref, w_ref, gu_o, pt_o, hid):
    block, width = rows_ref.shape[1], rows_ref.shape[2]
    rows = rows_ref[...].reshape(4 * block, width)
    for at, wide in chunks(w_ref.shape[1]):
        own = slice(at, at + wide)
        g = nt(rows, w_ref[0, own])
        u = nt(rows, w_ref[1, own])
        gu_o[0, :, own] = g.astype(BF)
        gu_o[1, :, own] = u.astype(BF)
        hid[:, own] = (g / (1.0 + jnp.exp(-g)) * u).astype(BF)
    for at, wide in chunks(width):
        own = slice(at, at + wide)
        part = nn(hid[...], w_ref[2, :, own]).astype(BF)
        for m in range(4):
            pt_o[m, :, own] = part[m * block : (m + 1) * block]


def launch(kernel, number, ins, outs, scratch, sems=(80, 90), vmem=62):
    sem = pltpu.SemaphoreType.DMA
    scratch = {k: pltpu.VMEM(*v) for k, v in scratch.items()}
    scratch.update(send=sem((sems[0],)), recv=sem((sems[0],)), loc=sem((sems[1],)))
    names = [*ins, *outs, *scratch]

    def body(*refs):
        kernel(types.SimpleNamespace(**dict(zip(names, refs))))

    got = pl.pallas_call(
        body,
        out_shape=[jax.ShapeDtypeStruct(v[0], v[1]) for v in outs.values()],
        in_specs=[pl.BlockSpec(memory_space=v[1]) for v in ins.values()],
        out_specs=[pl.BlockSpec(memory_space=v[2]) for v in outs.values()],
        scratch_shapes=list(scratch.values()),
        compiler_params=pltpu.CompilerParams(
            collective_id=number, has_side_effects=True, vmem_limit_bytes=vmem * 2**20
        ),
        cost_estimate=pl.CostEstimate(flops=10**11, bytes_accessed=10**8, transcendentals=10**7),
    )(*[v[0] for v in ins.values()])
    return types.SimpleNamespace(**dict(zip(outs, got)))


def forward_pass(cfg, tokens, cot, prefix, gains, qo, kvw, fp, cos, sin):
    layers, seqs, block, width, heads, units, share = cfg
    hbm, vm = pl.ANY, pltpu.VMEM
    keys, part = 4 * block, 4 * share
    rows = (seqs, 4, block, width)
    own = (seqs, block, width)
    size = 2 * (heads + 1) * LANES
    compact = 2 * heads * D + 2 * LANES
    q_s = (4, heads, block, LANES)
    kv_s = (4, 4, block, 2 * LANES)
    raw = (4, share, 2 * heads * D)
    raw_k = (4, share, 2 * KEY_VALUE_HEADS * D)
    raw_f = (4, units // 4, 3 * share)
    return launch(
        functools.partial(forward_kernel, cfg),
        0,
        dict(
            prefix=(prefix, pltpu.SMEM), tokens=(tokens, hbm), cot=(cot, hbm), gains=(gains, vm), qo=(qo, hbm),
            kvw=(kvw, hbm), fp=(fp, hbm), cos=(cos, vm), sin=(sin, vm),
        ),
        dict(
            out_o=(own, BF, hbm),
            wc=((layers, compact, width), BF, hbm),
            wa_o=((layers, size, width), BF, hbm),
            wf_o=((layers, 3, units, width), BF, hbm),
            rows_o=((layers, *rows), BF, hbm),
            q_o=((layers, seqs, *q_s), BF, hbm),
            kv_o=((layers, seqs, *kv_s), BF, hbm),
            att_o=((layers, seqs, 4, block, heads * LANES), BF, hbm),
            lse_o=((layers, seqs, 4, 1, heads * block), F32, hbm),
            middle_o=((layers, *own), F32, hbm),
            frows_o=((layers, *rows), BF, hbm),
            gu_o=((layers, seqs, 2, keys, units), BF, hbm),
            stream_o=((layers, *own), F32, hbm),
            gain_o=((2 * layers, width), F32, hbm),
            dy_o=(rows, BF, hbm),
            qz=((layers, *raw), BF, hbm),
            qc=((layers, *raw), BF, hbm),
            kvl=((layers, *raw_k), BF, hbm),
            fc=((layers, *raw_f), BF, hbm),
        ),
        dict(
            stream=(own, F32),
            middle=(own, F32),
            rows=(rows, BF),
            frows=(rows, BF),
            q=((seqs, *q_s), BF),
            kv=((layers, seqs, *kv_s), BF),
            att=((seqs, 4, block, heads * LANES), BF),
            lse=((seqs, 4, 1, heads * block), F32),
            pt=(rows, BF),
            rn=((seqs, 2, block, width), BF),
            far=(own, BF),
            rf=(own, BF),
            gu=((2, keys, units), BF),
            hid=((keys, units), BF),
            k_s=((4, keys, LANES), BF),
            vt_s=((4, LANES, keys), BF),
            m_s=((1, heads * block), F32),
            l_s=((1, heads * block), F32),
            a_s=((LANES, heads * block), F32),
            wa=((layers, size, width), BF),
            wf=((layers, 3, units, width), BF),
            st_q=(raw, BF),
            st_k=(raw_k, BF),
            st_f=(raw_f, BF),
            own=((compact, part), BF),
            tmp=((2 * KEY_VALUE_HEADS * D, part), BF),
            gl=((2, 4, 8, 256), F32),
            gain=((2 * layers, width), F32),
        ),
        sems=(130, 110),
        vmem=63,
    )


class Rows(Net):
    def gather_start(self, v, s, rows):
        rows[s, 0] = v.astype(BF)
        return [
            self.send(rows.at[s, 0], rows.at[s, 2], CTX, 2),
            self.send(rows.at[s, 0], rows.at[s, 1], CTX, 1),
        ]

    def gather_on(self, copies, s, rows):
        copies[0].wait_recv()
        copies.append(self.send(rows.at[s, 2], rows.at[s, 3], CTX, 1))

    def gather_end(self, copies):
        copies[1].wait_recv()
        copies[2].wait_recv()
        self.close(copies)

    def reduce_start(self, s):
        pt, rn = self.r.pt, self.r.rn
        return [
            self.send(pt.at[s, 3], rn.at[s, 1], CTX, 1),
            self.send(pt.at[s, 1], rn.at[s, 0], CTX, 1),
        ]

    def reduce_on(self, copies, s):
        r = self.r
        copies[0].wait_recv()
        r.far[s] = (r.pt[s, 2].astype(F32) + r.rn[s, 1].astype(F32)).astype(BF)
        copies.append(self.send(r.far.at[s], r.rf.at[s], CTX, 2))

    def reduce_end(self, copies, s):
        r = self.r
        copies[1].wait_recv()
        copies[2].wait_recv()
        total = r.pt[s, 0].astype(F32) + r.rn[s, 0].astype(F32) + r.rf[s].astype(F32)
        self.close(copies)
        return total

    def norm_back(self, s, copies, gain, row):
        r = self.r
        local, v = self.reduce_end(copies, s), r.base[s]
        scale = lax.rsqrt(jnp.mean(v * v, axis=-1, keepdims=True) + EPS)
        u = v * scale
        e = local * gain
        r.grad[s] = r.grad[s] + scale * (e - u * jnp.mean(e * u, axis=-1, keepdims=True))
        r.gs_o[row : row + 1] += jnp.sum(local * u, axis=0, keepdims=True)

    def sum_tp(self, parts, lands):
        outer = jnp.logical_not(self.inner)
        one = self.make(parts[1], lands[0], TP, 1)
        two = self.make(parts[2], lands[1], TP, 2)
        hand = self.make(parts[3], lands[2], TP, 1)
        mid = self.make(parts[3], lands[3], TP, 3)

        @pl.when(outer)
        def _():
            hand.start()
            two.start()

        @pl.when(self.inner)
        def _():
            mid.start()
            one.start()

        return one, two, hand, mid

    def sum_tp_on(self, copies, part, land):
        one, two, hand, _ = copies
        pl.when(jnp.logical_not(self.inner))(one.start)

        @pl.when(self.inner)
        def _():
            hand.wait_recv()
            part[...] = (part[...].astype(F32) + land[...].astype(F32)).astype(BF)
            two.start()

    def sum_tp_end(self, copies, own, lands):
        one, two, hand, mid = copies
        outer = jnp.logical_not(self.inner)
        one.wait_recv()
        two.wait_recv()

        @pl.when(self.inner)
        def _():
            mid.wait_recv()
            mid.wait_send()

        @pl.when(outer)
        def _():
            lands[3][...] = jnp.zeros(lands[3].shape, lands[3].dtype)
            hand.wait_send()

        one.wait_send()
        two.wait_send()
        return (
            own[...].astype(F32)
            + lands[0][...].astype(F32)
            + lands[1][...].astype(F32)
            + lands[3][...].astype(F32)
        )


def ffn_back_body(rows_ref, w_ref, gu_ref, hgu, pt_o, waits, between=None):
    block, width = rows_ref.shape[1], rows_ref.shape[2]
    rows = rows_ref[...].reshape(4 * block, width)
    for at, wide in chunks(w_ref.shape[1]):
        own = slice(at, at + wide)
        dh = nt(rows, w_ref[2, own])
        g = gu_ref[0, :, own].astype(F32)
        u = gu_ref[1, :, own].astype(F32)
        s = 1.0 / (1.0 + jnp.exp(-g))
        hgu[0, :, own] = (g * s * u).astype(BF)
        hgu[1, :, own] = (dh * u * s * (1.0 + g * (1.0 - s))).astype(BF)
        hgu[2, :, own] = (dh * g * s).astype(BF)
    for copy in waits:
        copy.wait()
    if between:
        between()
    for at, wide in chunks(width):
        own = slice(at, at + wide)
        part = (nn(hgu[1], w_ref[0, :, own]) + nn(hgu[2], w_ref[1, :, own])).astype(BF)
        for m in range(4):
            pt_o[m, :, own] = part[m * block : (m + 1) * block]


def weight_grad_body(lefts, rights, cols, out):
    rows = lefts[0].shape[0]
    for at, wide in chunks(lefts[0].shape[1]):
        total = None
        for left, right in zip(lefts, rights):
            term = tn(left[:, at : at + wide], right[:, :, cols].reshape(rows, out.shape[1]))
            total = term if total is None else total + term
        out[at : at + wide] = total.astype(BF)


def attn_back_body(
    heads, c, t, prefix, rows_ref, w_ref, q_ref, kv_ref, att_ref, lse_ref, cos_ref, sin_ref, d_o, dkv_o,
    do_s, de_s, dqt_s, dk_s, dv_s
):
    block = q_ref.shape[2]
    keys = 4 * block
    wide = heads * block
    w_at = (heads + 2) * LANES
    rows = rows_ref[...].reshape(keys, rows_ref.shape[2])
    for at, span in chunks(wide):
        do = nt(rows, w_ref[w_at + at : w_at + at + span]).astype(BF)
        for m in range(4):
            for j in range(span // LANES):
                h = at // LANES + j
                do_s[m, h * block : (h + 1) * block] = do[
                    m * block : (m + 1) * block, j * LANES : (j + 1) * LANES
                ]
    mask = side_mask(c, heads, block)
    for cq in range(4):
        m = xor(c, cq)
        for h in range(heads):
            own = slice(h * block, (h + 1) * block)
            prod = att_ref[m, :, h * LANES : (h + 1) * LANES].astype(F32) * do_s[m, own].astype(F32)
            de_s[cq, :, own] = jnp.sum(jnp.transpose(prod), axis=0, keepdims=True)
    dqt_s[...] = jnp.zeros_like(dqt_s)
    q_at = lax.broadcasted_iota(jnp.int32, (1, wide), 1) % block + t * block
    for ck in range(4):
        mk = xor(c, ck)
        k = jnp.concatenate([kv_ref[i, mk, :, :LANES] for i in range(4)], axis=0)
        v = jnp.concatenate([kv_ref[i, mk, :, LANES:] for i in range(4)], axis=0)
        kt = jnp.transpose(k.astype(F32)).astype(BF)
        dk_s[...] = jnp.zeros_like(dk_s)
        dv_s[...] = jnp.zeros_like(dv_s)
        for cq in range(4):
            if ck > cq and ck * keys >= PREFIX_MAX:
                continue
            m = xor(c, cq)
            q_all = q_ref[m].reshape(wide, LANES)
            for first, span in chunks(wide, 3 * LANES):
                own = slice(first, first + span)
                q, d_out = q_all[own], do_s[m, own]
                p = jnp.exp(nt(k, q) - lse_ref[cq, :, own])
                if ck >= cq:
                    at = key_positions(t, block, ck * keys, keys)
                    seen = (at <= q_at[:, own] + cq * keys) | (at < prefix)
                    p = jnp.where(seen, p, 0.0)
                ds = (p * (nt(v, d_out) - de_s[cq, :, own])).astype(BF)
                dk_s[...] += nn(ds, q)
                dv_s[...] += nn(p.astype(BF), d_out)
                dqt_s[cq, :, own] += nn(kt, ds)
        for i in range(4):
            dkv_o[i, mk, :, :LANES] = dk_s[i * block : (i + 1) * block].astype(BF)
            dkv_o[i, mk, :, LANES:] = dv_s[i * block : (i + 1) * block].astype(BF)
    for cq in range(4):
        m = xor(c, cq)
        dq = jnp.transpose(dqt_s[cq]) * 0.125
        turned = half_turn(dq)
        cos, sin = cos_ref[m], sin_ref[m]
        for h in range(heads):
            own = slice(h * block, (h + 1) * block)
            back = dq[own] * cos - turned[own] * sin
            d_o[m, :, h * LANES : (h + 1) * LANES] = jnp.where(mask[own], back, 0.0).astype(BF)


def proj_back_body(heads, total, w_ref, cos_ref, sin_ref, d_o, pt_o):
    block = d_o.shape[1]
    low = heads * LANES
    for m in range(4):
        dk = total[m, :, :LANES]
        dk = dk * cos_ref[m] - half_turn(dk) * sin_ref[m]
        d_o[m, :, low : low + LANES] = dk.astype(BF)
        d_o[m, :, low + LANES :] = total[m, :, LANES:].astype(BF)
    full = d_o[...].reshape(4 * block, low + 2 * LANES)
    for at, span in chunks(w_ref.shape[1]):
        own = slice(at, at + span)
        part = nn(full, w_ref[: low + 2 * LANES, own]).astype(BF)
        for m in range(4):
            pt_o[m, :, own] = part[m * block : (m + 1) * block]


def ffn_sums(net, cfg, where):
    layers, seqs, block, width, heads, units, share = cfg
    quarter = units // 4
    r, c = net.r, net.c
    loads, sends = {}, {}

    def start():
        if where == 2:
            loads[1] = [net.local(r.fs_i, r.fs.at[0])]
        else:
            for i in (2, 0, 1):
                loads[i] = [net.local(r.dwk.at[i], r.fs.at[i])]
            loads[2].append(net.local(r.dwx, r.fx.at[2]))
            for i in (0, 1):
                sends[i] = net.send(r.dws.at[i], r.fx.at[i], DP)
        yield

    def one(i):
        at = 0 if where == 2 else i
        parts = [r.fs.at[at, m * quarter : (m + 1) * quarter] for m in range(4)]
        for copy in loads[i]:
            copy.wait()
        if i in sends:
            sends[i].wait_recv()
        if where != 2:
            for m in (3, 2, 1, 0):
                own = slice(m * quarter, (m + 1) * quarter)
                r.fs[i, own] = (r.fs[i, own].astype(F32) + r.fx[i, own].astype(F32)).astype(BF)
        if where == 1 and i == 1:
            out = net.local(r.fs.at[i], r.fs_o)
            yield
            out.wait()
            net.close(list(sends.values()))
            yield
        lands = [r.fz.at[k, at] for k in range(4)]
        sums = net.sum_tp(parts, lands)
        yield
        net.sum_tp_on(sums, parts[2], lands[2])
        yield
        r.fo[...] = net.sum_tp_end(sums, parts[0], lands).astype(BF)
        ft, fg = r.ft.at[at], r.fg.at[at]
        for first in range(0, 4 * share, LANES):
            ft[first : first + LANES] = jnp.transpose(r.fo[:, first : first + LANES].astype(F32)).astype(BF)
        out = [net.send(ft.at[piece(xor(c, m))], fg.at[c], CTX, m) for m in (1, 2, 3)]
        fg[c] = ft[piece(c)]
        yield
        for copy in out:
            copy.wait_recv()
        to = r.u_o if i == 1 else r.d_o if i else r.g_o
        to[...] = jnp.concatenate([fg[k].astype(F32) for k in range(4)], axis=1)
        net.close(out)
        if where == 0 and i in sends:
            net.close([sends[i]])
        yield

    def piece(i):
        return pl.ds(pl.multiple_of(i * share, 32), share)

    return start(), one(2), one(0), one(1)


def finish_out(net, cfg, mine, other, waits):
    layers, seqs, block, width, heads, units, share = cfg
    r = net.r
    c, t = net.c, net.t
    one = slice(heads * D, 2 * heads * D)
    for copy in waits:
        copy.wait()
    for at in range(0, 4 * share, LANES):
        own = slice(at, at + LANES)
        r.ot[own] = jnp.transpose(mine[one, own].astype(F32) + other[one, own].astype(F32)).astype(BF)

    def piece(i):
        return r.ot.at[pl.ds(pl.multiple_of(i * share, 32), share)]

    out = [net.send(piece(xor(c, m)), r.oc.at[c], CTX, m) for m in (1, 2, 3)]
    own = net.local(piece(c), r.oc.at[c])
    yield
    for copy in out:
        copy.wait_recv()
    own.wait()
    net.close(out)
    for m in range(4):
        r.oq[m] = r.oc[xor(t, m)]
    parts = [r.oq.at[m] for m in range(4)]
    lands = [r.oz.at[k] for k in range(4)]
    sums = net.sum_tp(parts, lands)
    yield
    net.sum_tp_on(sums, parts[2], lands[2])
    yield
    r.wo_o[...] = net.sum_tp_end(sums, parts[0], lands)
    yield


def finish_attn(net, cfg, mine, other, waits):
    layers, seqs, block, width, heads, units, share = cfg
    r = net.r
    c, t = net.c, net.t
    one, two = slice(0, heads * D), slice(2 * heads * D, 2 * heads * D + 2 * LANES)
    for copy in waits:
        copy.wait()
    for at in range(0, 4 * share, LANES):
        own = slice(at, at + LANES)
        for units_, to in ((two, slice(0, 2 * LANES)), (one, slice(2 * LANES, 2 * LANES + heads * D))):
            total = mine[units_, own].astype(F32) + other[units_, own].astype(F32)
            r.at[own, to] = jnp.transpose(total).astype(BF)

    def piece(i):
        return r.at.at[pl.ds(pl.multiple_of(i * share, 32), share)]

    out = [net.send(piece(xor(c, m)), r.ac.at[c], CTX, m) for m in (1, 2, 3)]
    own = net.local(piece(c), r.ac.at[c])
    yield
    for copy in out:
        copy.wait_recv()
    own.wait()
    net.close(out)
    for m in range(4):
        r.aq[m] = r.ac[xor(t, m), :, 2 * LANES :]
    parts = [r.aq.at[m] for m in range(4)]
    lands = [r.az.at[k] for k in range(4)]
    for first, at in ((0, 0), (KEY_VALUE_HEADS * D, LANES)):
        terms = []
        for h in range(KEY_VALUE_HEADS):
            total = None
            for i in range(4):
                j = h - i * heads // GROUP
                if j in (0, 1):
                    term = r.ac[i, :, at + j * D : at + (j + 1) * D].astype(F32)
                    total = term if total is None else total + term
            terms.append(total)
        r.av[:, first : first + KEY_VALUE_HEADS * D] = jnp.concatenate(terms, axis=1)
    outer = jnp.logical_not(net.inner)
    r.asum[0] = r.av[...].astype(BF)
    ends = net.make(r.asum.at[0], r.al.at[0], TP, 1)
    swap = net.make(r.asum.at[1], r.al.at[1], TP, 3)
    back = net.make(r.asum.at[2], r.al.at[2], TP, 1)
    pl.when(outer)(ends.start)
    sums = net.sum_tp(parts, lands)
    yield

    @pl.when(net.inner)
    def _():
        ends.wait_recv()
        r.asum[1] = (r.av[...] + r.al[0].astype(F32)).astype(BF)
        swap.start()

    yield
    net.sum_tp_on(sums, parts[2], lands[2])
    yield

    @pl.when(net.inner)
    def _():
        swap.wait_recv()
        r.asum[2] = (r.asum[1].astype(F32) + r.al[1].astype(F32)).astype(BF)
        back.start()

    yield
    r.wq_o[...] = net.sum_tp_end(sums, parts[0], lands)

    @pl.when(net.inner)
    def _():
        swap.wait_send()
        back.wait_send()
        r.kv_o[...] = r.asum[2].astype(F32)

    @pl.when(outer)
    def _():
        ends.wait_send()
        back.wait_recv()
        r.kv_o[...] = r.al[2].astype(F32)

    yield


def finish_gains(net):
    r = net.r
    r.gt[...] = r.gs_o[...]
    for k, axis in enumerate((CTX, TP, DP)):
        ms = (1, 2, 3) if axis != DP else (1,)
        copies = [net.send(r.gt, r.gr.at[k, m - 1], axis, m) for m in ms]
        yield
        for copy in copies:
            copy.wait_recv()
        net.close(copies)
        total = r.gt[...]
        for m in ms:
            total = total + r.gr[k, m - 1]
        r.gt[...] = total
    r.gs_o[...] = r.gt[...]
    yield


def ffn_back_kernel2(cfg, l, tail, r):
    layers, seqs, block, width, heads, units, share = cfg
    net = Rows(r)
    part = 4 * share
    keep = pl.ds(pl.multiple_of(net.x * part, LANES), part)
    away = pl.ds(pl.multiple_of((1 - net.x) * part, LANES), part)
    net.barrier()
    loads = [net.local(r.dak, r.ak), net.local(r.dax, r.ax)] if tail else []
    first = [net.local(r.dy_i.at[0], r.dy.at[0]), net.local(r.wf_i.at[l, 2], r.wf.at[2])]
    first.append(net.local(r.gu_i.at[l, 0], r.gu.at[0]))
    second = [net.local(r.wf_i.at[l, i], r.wf.at[i]) for i in (0, 1)]
    later = [net.local(r.dy_i.at[s], r.dy.at[s]) for s in range(1, seqs)]
    later += [net.local(r.gu_i.at[l, s], r.gu.at[s]) for s in range(1, seqs)]
    top = l + 1 == layers
    state = [net.local(r.base_i.at[l], r.base)] + ([] if top else [net.local(r.grad_i, r.grad)])
    state += [net.local(r.frows_i.at[l, s], r.frows.at[s]) for s in range(seqs)]
    r.gs_o[...] = jnp.zeros_like(r.gs_o) if top else r.gs_i[...]
    row = layers + l
    gain = r.gain[row : row + 1]
    saved, busy = [], {}

    def sequence(s, waits, more):
        rows, hgu, pt = r.dy.at[s], r.hgu.at[s], r.pt.at[s]
        for copy in waits:
            copy.wait()
        if top:
            r.grad[s] = rows[0].astype(F32)
        ffn_back_body(rows, r.wf, r.gu.at[s], hgu, pt, more)
        red = net.reduce_start(s)
        yield
        net.reduce_on(red, s)
        yield
        while state:
            state.pop().wait()
        net.norm_back(s, red, gain, row)
        gather = net.gather_start(r.grad[s], s, r.dn)
        saved.append(net.local(r.grad.at[s], r.grad_o.at[s]))
        yield
        net.gather_on(gather, s, r.dn)
        yield
        net.gather_end(gather)
        saved.append(net.local(r.dn.at[s], r.dn_o.at[s]))
        yield

    def weights(i, to):
        lefts = [r.hgu.at[s, i] for s in range(seqs)]
        rights = [(r.frows if i else r.dy).at[s] for s in range(seqs)]
        while state:
            state.pop().wait()
        if i:
            if 0 in busy:
                busy.pop(0).wait()
            weight_grad_body(lefts, rights, away, r.ws.at[0])
            busy[0] = net.local(r.ws.at[0], r.dws_o.at[to])
        else:
            weight_grad_body(lefts, rights, away, r.wx)
            cross = net.send(r.wx, r.dwx_o, DP)
        yield
        if 1 in busy:
            busy.pop(1).wait()
        weight_grad_body(lefts, rights, keep, r.ws.at[1])
        busy[1] = net.local(r.ws.at[1], r.dwk_o.at[to])
        yield
        if not i:
            cross.wait()
        yield

    a, b = sequence(0, first, second), sequence(1, later, [])
    w0, w1, w2 = weights(0, 2), weights(1, 0), weights(2, 1)
    if tail:
        fa, fo = finish_attn(net, cfg, r.ak, r.ax, loads), finish_out(net, cfg, r.ak, r.ax, [])
        x, _, _, f2 = ffn_sums(net, cfg, 2)
        order = (
            x,
            fa, a, fo, f2, fa, a, b, w0, b, a, f2, w1, w1, w2, b, fo, fa, w2,
            w1, a, w2, fa, f2, fa, fo, b, w0, fo, fa, w0, a, f2, b,
        )
    else:
        order = (
            a, b, a, w0, b, a, w1, b, w0, w2, w2, a, a, w2, w1, w1, b, w0,
            b,
        )
    run(order)
    for copy in saved + list(busy.values()):
        copy.wait()


def attn_back_kernel2(cfg, l, r):
    layers, seqs, block, width, heads, units, share = cfg
    net = Rows(r)
    c, t = net.c, net.t
    part = 4 * share
    keep = pl.ds(pl.multiple_of(net.x * part, LANES), part)
    away = pl.ds(pl.multiple_of((1 - net.x) * part, LANES), part)
    net.barrier()
    loads = []
    for s in range(seqs):
        loads.append([net.local(r.dy_i.at[s], r.dy.at[s])])
        if s == 0:
            loads[0].append(net.local(r.wa_i.at[l], r.wa))
        for src, dst in ((r.q_i, r.q), (r.kv_i, r.kv), (r.att_i, r.att), (r.lse_i, r.lse)):
            loads[s].append(net.local(src.at[l, s], dst.at[s]))
    x, f0, f1, f2 = ffn_sums(net, cfg, 1 if l else 0)
    run((x,))
    state = [net.local(r.grad_i, r.grad), net.local(r.base_i.at[l], r.base)]
    state += [net.local(r.rows_i.at[l, s], r.rows.at[s]) for s in range(seqs)]
    r.gs_o[...] = r.gs_i[...]
    gain = r.gain[l : l + 1]
    saved = []

    def sequence(s):
        for copy in loads[s]:
            copy.wait()
        attn_back_body(
            heads, c, t, r.prefix[s], r.dy.at[s], r.wa, r.q.at[s], r.kv.at[s], r.att.at[s],
            r.lse.at[s], r.cos, r.sin, r.dqkv.at[s], r.dkv.at[s], r.do_s, r.de_s, r.dqt_s, r.dk_s, r.dv_s,
        )
        lands = [r.dz.at[k, s] for k in range(4)]
        sums = net.sum_tp([r.dkv.at[s, m] for m in range(4)], lands)
        yield
        net.sum_tp_on(sums, r.dkv.at[s, 2], lands[2])
        yield
        r.dt[...] = net.sum_tp_end(sums, r.dkv.at[s, 0], lands)
        proj_back_body(heads, r.dt, r.wa, r.cos, r.sin, r.dqkv.at[s], r.pt.at[s])
        red = net.reduce_start(s)
        yield
        net.reduce_on(red, s)
        yield
        while state:
            state.pop().wait()
        net.norm_back(s, red, gain, l)
        saved.append(net.local(r.grad.at[s], r.grad_o.at[s]))
        if l:
            gather = net.gather_start(r.grad[s], s, r.dn)
        yield
        if l:
            net.gather_on(gather, s, r.dn)
            yield
            net.gather_end(gather)
            saved.append(net.local(r.dn.at[s], r.dn_o.at[s]))
            yield

    def weights(lefts, rights, cols, out, at):
        while state:
            state.pop().wait()
        low = lax.div(c * heads, GROUP)
        lf = [lefts.at[s] for s in range(seqs)]
        rg = [rights.at[s] for s in range(seqs)]
        for a, wide in chunks(lf[0].shape[-1]):
            total = None
            for left, right in zip(lf, rg):
                term = tn(
                    left[:, :, a : a + wide].reshape(4 * block, wide),
                    right[:, :, cols].reshape(4 * block, part),
                )
                total = term if total is None else total + term
            r.ws[a : a + wide] = total.astype(BF)
        for h in range(heads):
            side = (lax.div(c * heads + h, GROUP) - low) * D
            out[at + h * D : at + (h + 1) * D] = r.ws[pl.ds(pl.multiple_of(h * LANES + side, D), D)]
        if at == 0:
            out[2 * heads * D :] = r.ws[heads * LANES : (heads + 2) * LANES]

    side, cross = [], []
    o_rows, q_rows, kv_rows = (
        slice(a * D, b * D) for a, b in ((heads, 2 * heads), (0, heads), (2 * heads, 2 * heads + 4))
    )

    def out_weights():
        weights(r.att, r.dy, away, r.wo.at[0], heads * D)
        if not l:
            side.append(net.send(r.wo.at[0, o_rows], r.ax.at[o_rows], DP))
        yield
        weights(r.att, r.dy, keep, r.wo.at[1], heads * D)
        yield

    def qkv_weights():
        weights(r.dqkv, r.rows, away, r.wo.at[0], 0)
        if l:
            yield
            cross.append(net.send(r.wo.at[0], r.dax_o, DP))
        else:
            cross.extend(net.send(r.wo.at[0, k], r.ax.at[k], DP) for k in (kv_rows, q_rows))
        yield
        weights(r.dqkv, r.rows, keep, r.wo.at[1], 0)
        yield

    a, b, wo, wq = sequence(0), sequence(1), out_weights(), qkv_weights()
    if l:
        order = (
            f0, a, b, a, b, a, a, f1, b, wo, wq, b, a, f0, wq, wq, f1, b,
            f1, b, f0, wo, a, b, f1, f2, f2, wq, a, f0,
        )
    else:
        gn, fa = finish_gains(net), finish_attn(net, cfg, r.wo.at[1], r.ax, cross)
        fo = finish_out(net, cfg, r.wo.at[1], r.ax, side)
        order = (
            f0, a, b, a, b, wo, f0, a, f2, b, wq, a, wq, f1, f0, b, f2, fa,
            wo, fo, f1, fa, a, b, gn, gn, f2, fo, fa, fa, f1, fa, fo, f2, gn, fa,
            f0, f1, gn, fo,
        )
    run(order)
    if l:
        saved.append(net.local(r.wo.at[1], r.dak_o))
        cross[0].wait()
    for copy in saved:
        copy.wait()


def backward_pass(cfg, tokens, prefix, cotangent, cos4, sin4, f):
    layers, seqs, block, width, heads, units, share = cfg
    keys, part = 4 * block, 4 * share
    rows = (seqs, 4, block, width)
    size = 2 * (heads + 1) * LANES
    compact = 2 * heads * D + 2 * LANES
    own = (seqs, block, width)
    hbm, vm = pl.ANY, pltpu.VMEM
    grads = ((8, width), F32, vm)
    common = dict(
        pt=(rows, BF), rn=((seqs, 2, block, width), BF), far=(own, BF), rf=(own, BF),
        grad=(own, F32), base=(own, F32), dy=(rows, BF),
    )
    kvs = (share, 2 * KEY_VALUE_HEADS * D)
    hs = (share, heads * D)
    mixed = 2 * LANES + heads * D
    one = (share, units)
    finish_out_ = dict(wq_o=(hs, F32, vm), wo_o=(hs, F32, vm), kv_o=(kvs, F32, vm), u_o=(one, F32, vm))
    finish_scratch = dict(
        ax=((compact, part), BF), at=((part, mixed), BF), ac=((4, share, mixed), BF), aq=((4, *hs), BF),
        az=((4, *hs), BF), av=(kvs, F32), asum=((3, *kvs), BF), al=((3, *kvs), BF),
        ot=((part, heads * D), BF), oc=((4, *hs), BF), oq=((4, *hs), BF), oz=((4, *hs), BF),
    )
    mid_out = dict(
        dn_o=(rows, BF, hbm), dak_o=((compact, part), BF, hbm), dax_o=((compact, part), BF, hbm),
        fs_o=((units, part), BF, hbm), g_o=(one, F32, vm), d_o=(one, F32, vm),
    )
    grad, sums, dy = None, None, f.dy_o
    done, units_of = [None] * layers, [None] * layers
    number = 1
    d, finish_in = None, {}
    for l in reversed(range(layers)):
        tail = d is not None
        more = (finish_in, finish_out_, finish_scratch) if tail else ({}, {}, {})
        c = launch(
            functools.partial(ffn_back_kernel2, cfg, l, tail),
            number,
            dict(
                dy_i=(dy, hbm), base_i=(f.middle_o, hbm), gain=(f.gain_o, vm), wf_i=(f.wf_o, hbm),
                frows_i=(f.frows_o, hbm), gu_i=(f.gu_o, hbm), **more[0], **({} if d is None else dict(grad_i=(grad, hbm), gs_i=(sums, vm))),
            ),
            dict(
                gs_o=grads, grad_o=(own, F32, hbm), dn_o=(rows, BF, hbm), dwk_o=((3, units, part), BF, hbm),
                dws_o=((2, units, part), BF, hbm), dwx_o=((units, part), BF, hbm), **more[1],
            ),
            dict(
                wf=((3, units, width), BF), frows=(rows, BF), gu=((seqs, 2, keys, units), BF), dn=(rows, BF),
                hgu=((seqs, 3, keys, units), BF), ws=((2, units, part), BF), wx=((units, part), BF),
                **(dict(ak=((compact, part), BF), fs=((1, units, part), BF), fz=((4, 1, units // 4, part), BF),
                fo=((units // 4, part), BF), ft=((1, part, units // 4), BF), fg=((1, 4, share, units // 4), BF)) if tail else {}), **common, **more[2],
            ),
        )
        if tail:
            done[l + 1] = c
            units_of[l + 1] = d
        d = launch(
            functools.partial(attn_back_kernel2, cfg, l),
            number + 1,
            dict(
                prefix=(prefix, pltpu.SMEM), dy_i=(c.dn_o, hbm), grad_i=(c.grad_o, hbm), base_i=(f.stream_o, hbm),
                gain=(f.gain_o, vm), wa_i=(f.wa_o, hbm), rows_i=(f.rows_o, hbm), q_i=(f.q_o, hbm), kv_i=(f.kv_o, hbm),
                att_i=(f.att_o, hbm), lse_i=(f.lse_o, hbm), cos=(cos4, vm), sin=(sin4, vm), gs_i=(c.gs_o, vm),
                dwk=(c.dwk_o, hbm), dws=(c.dws_o, hbm), dwx=(c.dwx_o, hbm),
            ),
            dict(
                gs_o=grads, grad_o=(own, F32, hbm),
                **(mid_out if l else dict(g_o=(one, F32, vm), d_o=(one, F32, vm), **finish_out_)),
            ),
            dict(
                wa=((size, width), BF), q=((seqs, 4, heads, block, LANES), BF), kv=((seqs, 4, 4, block, 2 * LANES), BF),
                att=((seqs, 4, block, heads * LANES), BF), lse=((seqs, 4, 1, heads * block), F32), rows=(rows, BF),
                dqkv=((seqs, 4, block, (heads + 2) * LANES), BF), dkv=((seqs, 4, 4, block, 2 * LANES), BF),
                do_s=((4, heads * block, LANES), BF), de_s=((4, 1, heads * block), F32),
                dqt_s=((4, LANES, heads * block), F32), dk_s=((keys, LANES), F32), dv_s=((keys, LANES), F32),
                dz=((4, seqs, 4, block, 2 * LANES), BF), dt=((4, block, 2 * LANES), F32),
                ws=(((heads + 2) * LANES, part), BF), wo=((2, compact, part), BF),
                fs=((3, units, part), BF), fx=((3, units, part), BF), fz=((4, 3, units // 4, part), BF),
                fo=((units // 4, part), BF), ft=((3, part, units // 4), BF), fg=((3, 4, share, units // 4), BF),
                **(dict(dn=(rows, BF)) if l else dict(gt=((8, width), F32), gr=((3, 3, 8, width), F32), **finish_scratch)), **common,
            ),
            vmem=63,
        )
        number += 2
        grad, dy, sums = d.grad_o, d.dn_o if l else None, d.gs_o
        if l:
            finish_in = dict(dak=(d.dak_o, hbm), dax=(d.dax_o, hbm), fs_i=(d.fs_o, hbm))
    done[0] = units_of[0] = d
    return grad, done, units_of


def rms(v):
    r = lax.rsqrt(jnp.mean(v * v, axis=-1, keepdims=True) + EPS)
    return v * r, r


def per_device(
    tokens, prefix, w_query, key_weight, value_weight, w_out, w_gate, w_up, w_down, gain_attn, gain_ffn,
    cotangent,
):
    layers = w_query.shape[0]
    seqs, block, width = tokens.shape
    dps = lax.axis_size(DP)
    x, c, t = (lax.axis_index(a) for a in (DP, CTX, TP))
    heads = w_query.shape[2] // D
    share = w_query.shape[1]
    part = 4 * share
    units = w_gate.shape[2]
    quarter = units // 4
    low = (c * heads) // GROUP
    keys = 4 * block
    long = 4 * keys

    half = D // 2
    lane = jnp.arange(LANES)
    freq = jnp.exp(-math.log(10000.0) * (lane % half).astype(F32) / half)
    at = ((c ^ jnp.arange(4)) * keys + t * block)[:, None] + jnp.arange(block)[None, :]
    angle = at.astype(F32).reshape(keys, 1) * freq[None, :]
    cos = jnp.cos(angle)
    sin = jnp.where(lane % D < half, -1.0, 1.0)[None, :] * jnp.sin(angle)
    cos, sin = lax.optimization_barrier((cos, sin))
    cos4, sin4 = cos.reshape(4, block, LANES), sin.reshape(4, block, LANES)
    scalars = [
        jnp.stack([c, t, prefix[s]]).astype(jnp.int32) for s in range(seqs)
    ]

    shards = jnp.stack([gain_attn, gain_ffn])
    gains = None if dps == 2 else lax.all_gather(shards, (DP, CTX), axis=2, tiled=True).astype(F32)

    def spread_dp(own):
        if dps == 2:
            other = lax.ppermute(own, DP, [(0, 1), (1, 0)])
            return jnp.concatenate(
                [jnp.where(x == 0, own, other), jnp.where(x == 0, other, own)], axis=-1
            )
        return lax.all_gather(own, DP, axis=own.ndim - 1, tiled=True)

    def attn_weights(l):
        qo = jnp.concatenate([w_query[l], w_out[l]], axis=1)
        slots = jnp.stack(tp_gather(qo))
        to_ctx = jnp.stack(
            [lax.dynamic_index_in_dim(slots, t ^ i, 0, keepdims=False) for i in range(4)]
        )
        got = ctx_exchange(to_ctx, True).reshape(part, 2 * heads * D).T
        kv = jnp.concatenate([key_weight[l], value_weight[l]], axis=1)
        kv = by_ctx(jnp.stack([kv] + [flip(kv, CTX, m) for m in (1, 2, 3)]))
        kv = kv.reshape(part, 2 * KEY_VALUE_HEADS * D).T
        k = lax.dynamic_slice_in_dim(kv, low * D, 2 * D, 0)
        v = lax.dynamic_slice_in_dim(kv, (KEY_VALUE_HEADS + low) * D, 2 * D, 0)
        own = jnp.concatenate([got[: heads * D], k, v, got[heads * D :]], axis=0)
        full = spread_dp(own)
        return call(
            functools.partial(pad_kernel, heads),
            [scalars[0], full],
            [((2 * (heads + 1) * LANES, width), BF)],
            smem=1,
        )[0]

    def ffn_weights(l):
        raw = jnp.concatenate([w_gate[l], w_up[l], w_down[l]], axis=0).T
        got = ctx_exchange(raw.reshape(4, quarter, 3 * share), True)
        own = jnp.transpose(got.reshape(4, quarter, 3, share), (2, 1, 0, 3)).reshape(
            3, quarter, part
        )
        slots = [spread_dp(s) for s in tp_gather(own)]
        return jnp.concatenate(slots, axis=1)

    if dps == 2:
        cfg = (layers, seqs, block, width, heads, units, share)
        small = jnp.pad(
            shards.astype(F32).reshape(2 * layers, share), ((0, 8 - 2 * layers), (0, 256 - share))
        )
        qo = jnp.concatenate([w_query, w_out], axis=2)
        kvw = jnp.concatenate([key_weight, value_weight], axis=2)
        fp = jnp.concatenate([w_gate, w_up, w_down], axis=1)
        fp = jnp.transpose(fp, (0, 2, 1)).reshape(layers, 4, quarter, 3 * share)
        f = forward_pass(cfg, tokens, cotangent, prefix, small, qo, kvw, fp, cos, sin)
        grad, done, fd = backward_pass(cfg, tokens, prefix, cotangent, cos4, sin4, f)
        wide = heads * D
        kd = KEY_VALUE_HEADS * D
        kv = jnp.stack([d.kv_o for d in done])
        sums = lax.dynamic_slice_in_dim(done[0].gs_o, (x * 4 + c) * share, share, 1)
        return (
            f.out_o, grad, jnp.stack([d.wq_o for d in done]), kv[:, :, :kd], kv[:, :, kd:],
            jnp.stack([d.wo_o for d in done]),
            jnp.stack([d.g_o for d in fd]), jnp.stack([d.u_o for d in done]), jnp.stack([d.d_o for d in fd]),
            sums[:layers], sums[layers : 2 * layers],
        )
    watt = [None] * layers
    wffn = [None] * layers
    for l in range(layers):
        watt[l] = attn_weights(l)
        wffn[l] = ffn_weights(l)

    stream = [tokens[s].astype(F32) for s in range(seqs)]
    kept = {}
    for l in range(layers):
        for s in range(seqs):
            u, _ = rms(stream[s])
            pieces = ctx_gather((u * gains[0, l]).astype(BF))
            rows, q, kv = call(
                functools.partial(qkv_kernel, heads),
                [scalars[s], *pieces, watt[l], cos, sin],
                [((4, block, width), BF), ((4, heads, block, LANES), BF), ((4, block, 2 * LANES), BF)],
                smem=1,
                flops=2 * keys * width * (heads + 2) * LANES,
            )
            kvs = tp_gather(kv)
            att, lse, *parts = call(
                functools.partial(attn_kernel, heads),
                [scalars[s], q, *kvs, watt[l]],
                [((4, block, heads * LANES), BF), ((4, 1, heads * block), F32)] + [((block, width), BF)] * 4,
                smem=1,
                scratch=[
                    pltpu.VMEM((4, keys, LANES), BF),
                    pltpu.VMEM((4, LANES, keys), BF),
                    pltpu.VMEM((1, heads * block), F32),
                    pltpu.VMEM((1, heads * block), F32),
                    pltpu.VMEM((LANES, heads * block), F32),
                ],
                flops=2 * 2 * keys * long * heads * 256 * 0.7 + 2 * keys * heads * LANES * width,
                exps=keys * long * heads,
            )
            middle = stream[s] + ctx_reduce(parts)
            u, _ = rms(middle)
            pieces = ctx_gather((u * gains[1, l]).astype(BF))
            frows, gate, up, *parts = call(
                ffn_kernel,
                [*pieces, wffn[l]],
                [((4, block, width), BF)] + [((keys, units), BF)] * 2 + [((block, width), BF)] * 4,
                scratch=[pltpu.VMEM((keys, width), F32)],
                flops=2 * keys * width * units * 3,
            )
            kept[l, s] = (stream[s], rows, q, kvs, att, lse, middle, frows, gate, up)
            stream[s] = middle + ctx_reduce(parts)

    output = jnp.stack(stream).astype(BF)

    def norm_back(grad, local, v, gain):
        u, r = rms(v)
        e = local * gain
        grad = grad + r * (e - u * jnp.mean(e * u, axis=-1, keepdims=True))
        return grad, jnp.sum(local * u, axis=0)

    def weight_grad(lefts, rights):
        n = len(lefts)
        u_count = lefts[0].shape[-1]
        return call(
            functools.partial(weight_grad_kernel, dps if dps == 2 else 1, n),
            [a.reshape(keys, u_count) for a in lefts] + list(rights),
            [((u_count, width // dps), BF)] * 2 if dps == 2 else [((u_count, width), BF)],
            flops=2 * n * keys * u_count * width,
        )

    def collect_dp(halves):
        if dps == 2:
            mine = jnp.where(x == 0, halves[0], halves[1])
            other = jnp.where(x == 0, halves[1], halves[0])
            got = lax.ppermute(other, DP, [(0, 1), (1, 0)])
            return mine.astype(F32) + got.astype(F32)
        return lax.psum_scatter(
            halves[0], DP, scatter_dimension=halves[0].ndim - 1, tiled=True
        ).astype(F32)

    grads = {}

    def ffn_grads(l, lefts_rights):
        sums = [collect_dp(weight_grad(a, b)).reshape(4, quarter, part) for a, b in lefts_rights]
        slots = [jnp.stack([s[i] for s in sums]).astype(BF) for i in range(4)]
        own = tp_reduce(slots).reshape(3 * quarter, part).astype(BF)
        got = ctx_exchange(own.T.reshape(4, share, 3 * quarter), False).astype(F32)
        got = jnp.transpose(got.reshape(4, share, 3, quarter), (2, 1, 0, 3)).reshape(3, share, units)
        grads[l, "g"], grads[l, "u"], grads[l, "d"] = got[0], got[1], got[2]

    def attn_grads(l, dqkv, rows, att, drows):
        a = weight_grad(dqkv, rows)
        b = weight_grad(att, drows)
        halves = [
            call(
                functools.partial(unpad_kernel, heads),
                [scalars[0], i, j],
                [((2 * heads * D + 2 * LANES, i.shape[1]), BF)],
                smem=1,
            )[0]
            for i, j in zip(a, b)
        ]
        own = collect_dp(halves).astype(BF).T.reshape(4, share, 2 * heads * D + 2 * LANES)
        got = ctx_exchange(own, False)
        lo, hi = heads * D, heads * D + 2 * LANES
        qo = jnp.concatenate([got[:, :, :lo], got[:, :, hi:]], axis=-1)
        qo = [lax.dynamic_index_in_dim(qo, t ^ i, 0, keepdims=False) for i in range(4)]
        qo = tp_reduce(qo)
        grads[l, "q"], grads[l, "o"] = qo[:, :lo], qo[:, lo:]
        kv = got[:, :, lo:hi].astype(F32)
        both = []
        for first in (0, LANES):
            total = jnp.zeros((share, KEY_VALUE_HEADS * D), F32)
            for i in range(4):
                h = i * heads // GROUP
                term = kv[i, :, first : first + LANES]
                total = total + jnp.pad(term, ((0, 0), (h * D, (KEY_VALUE_HEADS - 2 - h) * D)))
            both.append(total)
        both = jnp.concatenate(both, axis=1)
        sent = both.astype(BF)
        for m in (1, 2, 3):
            both = both + flip(sent, TP, m).astype(F32)
        grads[l, "k"], grads[l, "v"] = (
            both[:, : KEY_VALUE_HEADS * D],
            both[:, KEY_VALUE_HEADS * D :],
        )

    grad = [cotangent[s].astype(F32) for s in range(seqs)]
    gain_sums = {}
    for l in reversed(range(layers)):
        hidden, dgate, dup, dy = [], [], [], []
        gain_sums[1, l] = 0.0
        gain_sums[0, l] = 0.0
        for s in range(seqs):
            _, _, _, _, _, _, middle, frows, gate, up = kept[l, s]
            drows, dg, du, hid, *parts = call(
                ffn_back_kernel,
                [*ctx_gather(grad[s].astype(BF)), wffn[l], gate, up],
                [((4, block, width), BF)] + [((keys, units), BF)] * 3 + [((block, width), BF)] * 4,
                scratch=[pltpu.VMEM((keys, width), F32)],
                flops=2 * keys * width * units * 3,
            )
            hidden.append(hid), dgate.append(dg), dup.append(du), dy.append(drows)
            grad[s], extra = norm_back(grad[s], ctx_reduce(parts), middle, gains[1, l])
            gain_sums[1, l] += extra
        ffn_grads(
            l,
            [
                (dgate, [kept[l, s][7] for s in range(seqs)]),
                (dup, [kept[l, s][7] for s in range(seqs)]),
                (hidden, dy),
            ],
        )
        dqkvs, dys = [], []
        for s in range(seqs):
            start, rows, q, kvs, att, lse, *_ = kept[l, s]
            drows, dq, *dkv = call(
                functools.partial(attn_back_kernel, heads),
                [scalars[s], *ctx_gather(grad[s].astype(BF)), watt[l], q, *kvs, att, lse, cos4, sin4],
                [((4, block, width), BF), ((4, block, heads * LANES), BF)] + [((4, block, 2 * LANES), BF)] * 4,
                smem=1,
                scratch=[
                    pltpu.VMEM((4, heads * block, LANES), BF),
                    pltpu.VMEM((4, 1, heads * block), F32),
                    pltpu.VMEM((4, LANES, heads * block), F32),
                    pltpu.VMEM((keys, LANES), F32),
                    pltpu.VMEM((keys, LANES), F32),
                ],
                flops=2 * 5 * keys * long * heads * 256 * 0.7 + 2 * keys * heads * LANES * width,
                exps=keys * long * heads,
            )
            one = flip(dkv[1], TP, 1)
            handed = lax.ppermute(dkv[3], TP, [(0, 1), (3, 2)])
            mid = lax.ppermute(dkv[3], TP, [(1, 2), (2, 1)])
            two = flip((dkv[2].astype(F32) + handed.astype(F32)).astype(BF), TP, 2)
            dqkv, *parts = call(
                functools.partial(proj_back_kernel, heads),
                [dkv[0], one, two, mid, dq, watt[l], cos4, sin4],
                [((4, block, (heads + 2) * LANES), BF)] + [((block, width), BF)] * 4,
                flops=2 * keys * (heads + 2) * LANES * width,
            )
            dqkvs.append(dqkv), dys.append(drows)
            grad[s], extra = norm_back(grad[s], ctx_reduce(parts), start, gains[0, l])
            gain_sums[0, l] += extra
        attn_grads(
            l,
            dqkvs,
            [kept[l, s][1] for s in range(seqs)],
            [kept[l, s][4] for s in range(seqs)],
            dys,
        )

    sums = jnp.stack([gain_sums[k, l] for k in range(2) for l in range(layers)])
    sums = lax.psum(sums, (DP, CTX, TP))
    sums = lax.dynamic_slice_in_dim(sums, (x * 4 + c) * share, share, 1).reshape(2, layers, share)

    def stacked(name):
        return jnp.stack([grads[l, name] for l in range(layers)])

    return (
        output,
        jnp.stack(grad),
        stacked("q"),
        stacked("k"),
        stacked("v"),
        stacked("o"),
        stacked("g"),
        stacked("u"),
        stacked("d"),
        sums[0],
        sums[1],
    )


def solution(mesh):
    rows = P(DP, (CTX, TP), None)
    sharded = P(None, (DP, CTX), TP)
    heads = P(None, (DP, CTX), None)
    gains = P(None, (DP, CTX))
    in_specs = (rows, P(DP), sharded, heads, heads, sharded, sharded, sharded, sharded, gains, gains, rows)
    out_specs = (rows, rows, sharded, heads, heads, sharded, sharded, sharded, sharded, gains, gains)
    return jax.shard_map(
        per_device, mesh=mesh, in_specs=in_specs, out_specs=out_specs, check_vma=False
    )
```
